32 devices in a mesh: dp: 8 (over y, x, core), tensor: 4 (over z).
Axes of the slice: x: 2, y: 2, z: 4, core: 2. Of those that a mesh axis runs over, the one named last changes fastest.
Arguments:
- tokens: bfloat16 [36928, 1024], P(('dp', 'tensor')), may hold values from -6 to 6
- cotangent: bfloat16 [36928, 1024], P(('dp', 'tensor')), may hold values from -14 to 14
- attn_master: float32 [1024, 4, 1024], P('dp', None, 'tensor'), may hold values from -2 to 2
- attn_first: float32 [1024, 4, 1024], P('dp', None, 'tensor'), may hold values from -0.00036621094 to 0.00036621094
- attn_second: float32 [1024, 4, 1024], P('dp', None, 'tensor'), may hold values from 2.9701488e-09 to 1.1768514e-08
- attn_ema: float32 [1024, 4, 1024], P('dp', None, 'tensor'), may hold values from -0.1875 to 0.1875
- mlp_master: float32 [1024, 2, 4096], P('dp', None, 'tensor'), may hold values from -0.1875 to 0.1875
- mlp_first: float32 [1024, 2, 4096], P('dp', None, 'tensor'), may hold values from -0.00036621094 to 0.00036621094
- mlp_second: float32 [1024, 2, 4096], P('dp', None, 'tensor'), may hold values from 2.9701488e-09 to 1.1768514e-08
- mlp_ema: float32 [1024, 2, 4096], P('dp', None, 'tensor'), may hold values from -0.1875 to 0.1875
- msg_master: float32 [1024, 5, 1024], P('dp'), may hold values from -0.1875 to 0.1875
- msg_first: float32 [1024, 5, 1024], P('dp'), may hold values from -4.5776367e-05 to 4.5776367e-05
- msg_second: float32 [1024, 5, 1024], P('dp'), may hold values from 4.1180573e-11 to 1.631683e-10
- msg_ema: float32 [1024, 5, 1024], P('dp'), may hold values from -0.1875 to 0.1875
- vec_master: float32 [1024, 18], P('dp'), may hold values from -3 to 3
- vec_first: float32 [1024, 18], P('dp'), may hold values from -0.0014648438 to 0.0014648438
- vec_second: float32 [1024, 18], P('dp'), may hold values from 4.7074057e-08 to 1.9053785e-07
- vec_ema: float32 [1024, 18], P('dp'), may hold values from 0.5 to 1.5
Outputs:
- block_output: float32 [36928, 1024], P(('dp', 'tensor'))
- input_grad: float32 [36928, 1024], P(('dp', 'tensor'))
- grad_norm: float32 [], replicated
- attn_grad: float32 [1024, 4, 1024], P('dp', None, 'tensor')
- attn_first_new: float32 [1024, 4, 1024], P('dp', None, 'tensor')
- attn_second_new: float32 [1024, 4, 1024], P('dp', None, 'tensor')
- attn_weight: float32 [1024, 4, 1024], P('dp', None, 'tensor')
- attn_average: float32 [1024, 4, 1024], P('dp', None, 'tensor')
- mlp_grad: float32 [1024, 2, 4096], P('dp', None, 'tensor')
- mlp_first_new: float32 [1024, 2, 4096], P('dp', None, 'tensor')
- mlp_second_new: float32 [1024, 2, 4096], P('dp', None, 'tensor')
- mlp_weight: float32 [1024, 2, 4096], P('dp', None, 'tensor')
- mlp_average: float32 [1024, 2, 4096], P('dp', None, 'tensor')
- msg_grad: float32 [1024, 5, 1024], P('dp')
- msg_first_new: float32 [1024, 5, 1024], P('dp')
- msg_second_new: float32 [1024, 5, 1024], P('dp')
- msg_weight: float32 [1024, 5, 1024], P('dp')
- msg_average: float32 [1024, 5, 1024], P('dp')
- vec_grad: float32 [1024, 18], P('dp')
- vec_first_new: float32 [1024, 18], P('dp')
- vec_second_new: float32 [1024, 18], P('dp')
- vec_weight: float32 [1024, 18], P('dp')
- vec_average: float32 [1024, 18], P('dp')
The draws below stay inside these ranges and needn't reach their ends.
All inputs are finite; a program needn't handle non-finite values.
Results may differ from the reference program's by a relative error of at most 0.025.
The reference program's roundings to bfloat16 on the way count: a program that leaves them out, or rounds other values in their place, can miss the bound.
Values may be sent and summed in bfloat16 or wider, within the bound.
No kernel may reach another device: no remote copies, remote signals or barrier semaphores. Data moves between devices by JAX's collectives and lax.ppermute only.
A program may use at most 320 MiB of HBM per device.

```python
import math
import jax
import jax.numpy as jnp
from jax import lax

D = 1024
HEADS = 16
HEAD = 64
FF = 4096
PATCHES = 577
FRAMES = 8
VID_DEV = 1
STEP = 10
NV = 18
VIDEOS = 8
TOKENS = 36928
PARAMS = 17844224


def draw_attn_master(key, part):
    key = jax.random.fold_in(key, 11)
    raw_draw = jnp.clip(jax.random.normal(key, (D, 4, D), jnp.float32), -4.0, 4.0)
    slot_scale = jnp.where(jnp.arange(4) == 3, 2.5, 1.0).astype(jnp.float32)
    return raw_draw * slot_scale[None, :, None] * D ** (-0.5)


def draw_cotangent(key, part):
    key = jax.random.fold_in(key, 12)
    group_rows = VID_DEV * FRAMES * PATCHES
    row_place = (jnp.arange(TOKENS) % group_rows).astype(jnp.float32) / group_rows
    col_place = jnp.arange(D).astype(jnp.float32) / D
    scale_map = (0.6 + 1.2 * row_place)[:, None] * (0.6 + 1.2 * col_place)[None, :]
    raw_draw = jnp.clip(jax.random.normal(key, (TOKENS, D), jnp.float32), -4.0, 4.0)
    return (raw_draw * scale_map).astype(jnp.bfloat16)


def draw_vec_master(key, part):
    key = jax.random.fold_in(key, 13)
    ramp_place = jnp.arange(D).astype(jnp.float32) / D
    ramp_line = 0.6 + 1.2 * ramp_place
    noise_part = jnp.clip(jax.random.normal(key, (D, NV), jnp.float32), -4.0, 4.0) * 0.2
    wobble = jax.random.uniform(jax.random.fold_in(key, 1), (D, NV), jnp.float32, -0.15, 0.15)
    columns = jnp.arange(NV)
    gain_cols = (columns == 0) | (columns == 2) | (columns == 4)
    return jnp.where(gain_cols[None, :], ramp_line[:, None] * (1.0 + wobble), noise_part)


def block_scale(own_key, dims, split, smallest, high):
    def one(dim, blocks):
        steps = jax.random.uniform(jax.random.fold_in(jax.random.fold_in(own_key, 6), dim), (blocks,), jnp.float32, smallest / len(split), high / len(split))
        return jnp.repeat(jnp.exp(steps), dims[dim] // blocks).reshape((-1,) + (1,) * (len(dims) - dim - 1))

    loudness = one(*split[0])
    for cut in split[1:]:
        loudness = loudness * one(*cut)
    return loudness


def noise(stream_key, extent, scale, limit, shards=(), dtype=jnp.bfloat16):
    factor_of = block_scale(stream_key, extent, shards, -0.22, 0.18) if shards else 1.0
    values = jax.random.normal(stream_key, extent, jnp.float32) * scale * factor_of
    return jnp.minimum(jnp.maximum(values, -limit), limit).astype(dtype)


def setup_inputs(seed: int = 0) -> dict:
    arg_keys = jax.random.split(jax.random.key(seed), 19)
    tokens = noise(arg_keys[0], (TOKENS, D), 1.0, 6.0, ((0, 32),))
    cotangent = draw_cotangent(jax.random.fold_in(arg_keys[18], 71), 0)
    attn_master = draw_attn_master(jax.random.fold_in(arg_keys[18], 71), 0)
    attn_first = noise(arg_keys[3], (D, 4, D), (0.11 * PARAMS ** -0.5), 0.00036621094, ((0, 8), (2, 4)), jnp.float32)
    attn_second = jnp.clip(jnp.exp(math.log(1.1768514163179589e-08) - 1.37681562 * jax.random.uniform(arg_keys[4], (D, 4, D), jnp.float32) ** block_scale(arg_keys[4], (D, 4, D), ((0, 8), (2, 4)), -0.2, 0.2)), 2.9701487935795967e-09, 1.1768514163179589e-08)
    attn_ema = noise(arg_keys[5], (D, 4, D), D ** -0.5, 0.1875, ((0, 8), (2, 4)), jnp.float32)
    mlp_master = noise(arg_keys[6], (D, 2, FF), D ** -0.5, 0.1875, ((0, 8), (2, 4)), jnp.float32)
    mlp_first = noise(arg_keys[7], (D, 2, FF), (0.11 * PARAMS ** -0.5), 0.00036621094, ((0, 8), (2, 4)), jnp.float32)
    mlp_second = jnp.clip(jnp.exp(math.log(1.1768514163179589e-08) - 1.37681562 * jax.random.uniform(arg_keys[8], (D, 2, FF), jnp.float32) ** block_scale(arg_keys[8], (D, 2, FF), ((0, 8), (2, 4)), -0.2, 0.2)), 2.9701487935795967e-09, 1.1768514163179589e-08)
    mlp_ema = noise(arg_keys[9], (D, 2, FF), D ** -0.5, 0.1875, ((0, 8), (2, 4)), jnp.float32)
    msg_master = noise(arg_keys[10], (D, 5, D), D ** -0.5, 0.1875, ((0, 8),), jnp.float32)
    msg_first = noise(arg_keys[11], (D, 5, D), (0.11 * (FRAMES / PATCHES) ** 0.5 * PARAMS ** -0.5), 4.57763671875e-05, ((0, 8),), jnp.float32)
    msg_second = jnp.clip(jnp.exp(math.log(1.631682983171956e-10) - 1.3768156 * jax.random.uniform(arg_keys[12], (D, 5, D), jnp.float32) ** block_scale(arg_keys[12], (D, 5, D), ((0, 8),), -0.2, 0.2)), 4.118057284063781e-11, 1.631682983171956e-10)
    msg_ema = noise(arg_keys[13], (D, 5, D), D ** -0.5, 0.1875, ((0, 8),), jnp.float32)
    vec_master = draw_vec_master(jax.random.fold_in(arg_keys[18], 71), 0)
    vec_first = noise(arg_keys[15], (D, NV), (0.44 * PARAMS ** -0.5), 0.0014648438, ((0, 8),), jnp.float32)
    vec_second = jnp.clip(jnp.exp(math.log(1.9053784683364938e-07) - 1.39812881 * jax.random.uniform(arg_keys[16], (D, NV), jnp.float32) ** block_scale(arg_keys[16], (D, NV), ((0, 8),), -0.2, 0.2)), 4.7074056652718355e-08, 1.9053784683364938e-07)
    vec_ema = jnp.clip(1.0 + 0.1 * jax.random.normal(arg_keys[17], (D, NV), jnp.float32), 0.5, 1.5)
    return dict(tokens=tokens, cotangent=cotangent, attn_master=attn_master, attn_first=attn_first, attn_second=attn_second, attn_ema=attn_ema, mlp_master=mlp_master, mlp_first=mlp_first, mlp_second=mlp_second, mlp_ema=mlp_ema, msg_master=msg_master, msg_first=msg_first, msg_second=msg_second, msg_ema=msg_ema, vec_master=vec_master, vec_first=vec_first, vec_second=vec_second, vec_ema=vec_ema)


@jax.custom_vjp
def low(v):
    return lax.optimization_barrier(v.astype(jnp.bfloat16)).astype(jnp.float32)

@jax.custom_vjp
def low_back(v):
    return v

def low_keep(v):
    return (low(v), None)

def low_pass(kept, grad):
    return (grad,)

def back_keep(v):
    return (v, None)

def back_low(kept, grad):
    return (low(grad),)
low.defvjp(low_keep, low_pass)
low_back.defvjp(back_keep, back_low)
norm_eps = 1e-05
beta_one = 0.9
beta_two = 0.95
adam_eps = 1e-08
decay_mat = 0.05
ema_keep = 0.7
clip_limit = 1.0
rate_mat = 0.02
rate_vec = 0.4
highest = lax.Precision.HIGHEST

def both_ways(values):
    return low_back(low(values))

def matmul(left_side, right_side):
    return jnp.dot(left_side, right_side, precision=highest)

def layer_norm(values, gain_row, shift_row):
    centre = values - lax.optimization_barrier(jnp.mean(values, -1, keepdims=True))
    spread = lax.optimization_barrier(jnp.mean(centre * centre, -1, keepdims=True))
    return centre * lax.rsqrt(spread + norm_eps) * gain_row + shift_row

def split_heads(values):
    shaped = values.reshape(values.shape[:-1] + (HEADS, HEAD))
    return jnp.moveaxis(shaped, -2, -3)

def merge_heads(values):
    moved_axes = jnp.moveaxis(values, -3, -2)
    return moved_axes.reshape(moved_axes.shape[:-2] + (HEADS * HEAD,))

def attend(queries, key_rows, value_rows):
    scores = low_back(jnp.einsum('...qe,...ke->...qk', queries, key_rows, precision=highest) * HEAD ** (-0.5))
    shifted = jnp.exp(scores - lax.optimization_barrier(jnp.max(scores, -1, keepdims=True)))
    probability = shifted / lax.optimization_barrier(jnp.sum(shifted, -1, keepdims=True))
    return jnp.einsum('...qk,...ke->...qe', low(probability), value_rows, precision=highest)

def frame_attention(inputs):
    queries, key_rows, value_rows = inputs
    return merge_heads(attend(split_heads(queries), split_heads(key_rows), split_heads(value_rows)))

def video_block(video_rows, attn_w, mlp_w, msg_w, vectors):
    ff_bias = vectors[:, 14:].T.reshape(FF)
    tokens_cls = video_rows[:, 0, :]
    first_msg = low_back(matmul(tokens_cls, msg_w[:, 0]) + vectors[:, 6])
    normed_msg = low(layer_norm(first_msg, vectors[:, 4], vectors[:, 5]))
    msg_query = both_ways(matmul(normed_msg, msg_w[:, 1]) + vectors[:, 7])
    msg_keys = both_ways(matmul(normed_msg, msg_w[:, 2]))
    msg_values = both_ways(matmul(normed_msg, msg_w[:, 3]) + vectors[:, 8])
    msg_mixed = both_ways(frame_attention((msg_query, msg_keys, msg_values)))
    message = low_back(first_msg + matmul(msg_mixed, msg_w[:, 4]) + vectors[:, 9])
    normed = low(layer_norm(video_rows, vectors[:, 0], vectors[:, 1]))
    normed_tok = low(layer_norm(message, vectors[:, 0], vectors[:, 1]))
    queries = both_ways(matmul(normed, attn_w[:, 0]) + vectors[:, 10])
    key_rows = both_ways(jnp.concatenate([matmul(normed, attn_w[:, 1]), matmul(normed_tok, attn_w[:, 1])[:, None]], axis=1))
    value_rows = both_ways(jnp.concatenate([matmul(normed, attn_w[:, 2]), matmul(normed_tok, attn_w[:, 2])[:, None]], axis=1) + vectors[:, 11])
    attended = both_ways(lax.map(jax.checkpoint(frame_attention), (queries, key_rows, value_rows)))
    middle = low_back(video_rows + jnp.einsum('fpi,oi->fpo', attended, attn_w[:, 3], precision=highest) + vectors[:, 12])
    normed_mid = low(layer_norm(low(middle), vectors[:, 2], vectors[:, 3]))
    hidden_pre = low_back(matmul(normed_mid, mlp_w[:, 0]) + ff_bias)
    hidden_act = low(hidden_pre * jax.nn.sigmoid(1.702 * hidden_pre))
    return middle + jnp.einsum('fph,oh->fpo', hidden_act, mlp_w[:, 1], precision=highest) + vectors[:, 13]

def adam_step(weight, first_moment, second_moment, gradient, factor, step_rate, decay_rate):
    clipped = gradient * factor
    first_new = beta_one * first_moment + (1.0 - beta_one) * clipped
    second_new = beta_two * second_moment + (1.0 - beta_two) * clipped * clipped
    update = first_new / (1.0 - beta_one ** STEP) / (jnp.sqrt(second_new / (1.0 - beta_two ** STEP)) + adam_eps)
    weight_new = weight - step_rate * (update + decay_rate * weight)
    return (first_new, second_new, weight_new)

def reference(tokens, cotangent, attn_master, attn_first, attn_second, attn_ema, mlp_master, mlp_first, mlp_second, mlp_ema, msg_master, msg_first, msg_second, msg_ema, vec_master, vec_first, vec_second, vec_ema):
    videos_in = tokens.astype(jnp.float32).reshape(VIDEOS, FRAMES, PATCHES, D)

    def forward(video_set, attn_w, mlp_w, msg_w, vectors):
        attn_w = low(attn_w)
        mlp_w = low(mlp_w)
        msg_w = low(msg_w)
        vectors = low(vectors)

        def one_video(video_rows):
            return video_block(video_rows, attn_w, mlp_w, msg_w, vectors)
        return lax.map(jax.checkpoint(one_video), video_set)
    block_out, pull_back = jax.vjp(forward, videos_in, attn_master, mlp_master, msg_master, vec_master)
    gradients = pull_back(cotangent.astype(jnp.float32).reshape(block_out.shape))
    input_grad = gradients[0].reshape(TOKENS, D)
    attn_grad, mlp_grad, msg_grad, vec_grad = (gradients[1], gradients[2], gradients[3], gradients[4])
    squares = jnp.sum(attn_grad * attn_grad) + jnp.sum(mlp_grad * mlp_grad) + jnp.sum(msg_grad * msg_grad) + jnp.sum(vec_grad * vec_grad)
    grad_norm = jnp.sqrt(squares)
    factor = clip_limit / jnp.maximum(grad_norm, clip_limit)
    attn_m, attn_s, attn_w = adam_step(attn_master, attn_first, attn_second, attn_grad, factor, rate_mat, decay_mat)
    mlp_m, mlp_s, mlp_w = adam_step(mlp_master, mlp_first, mlp_second, mlp_grad, factor, rate_mat, decay_mat)
    msg_m, msg_s, msg_w = adam_step(msg_master, msg_first, msg_second, msg_grad, factor, rate_mat, decay_mat)
    vec_m, vec_s, vec_w = adam_step(vec_master, vec_first, vec_second, vec_grad, factor, rate_vec, 0.0)
    attn_avg = ema_keep * attn_ema + (1.0 - ema_keep) * attn_w
    mlp_avg = ema_keep * mlp_ema + (1.0 - ema_keep) * mlp_w
    msg_avg = ema_keep * msg_ema + (1.0 - ema_keep) * msg_w
    vec_avg = ema_keep * vec_ema + (1.0 - ema_keep) * vec_w
    return (block_out.reshape(TOKENS, D), input_grad, grad_norm, attn_grad, attn_m, attn_s, attn_w, attn_avg, mlp_grad, mlp_m, mlp_s, mlp_w, mlp_avg, msg_grad, msg_m, msg_s, msg_w, msg_avg, vec_grad, vec_m, vec_s, vec_w, vec_avg)
```

```python
import functools

import jax
import jax.numpy as jnp
from jax import lax
from jax.experimental import pallas as pl
from jax.experimental.pallas import tpu as pltpu
from jax.sharding import PartitionSpec as P

D = 1024
HEADS = 16
HEAD = 64
FF = 4096
PATCHES = 577
FRAMES = 8
STEP = 10
ROWS = 592


norm_eps = 1e-05
beta_one = 0.9
beta_two = 0.95
adam_eps = 1e-08
decay_mat = 0.05
ema_keep = 0.7
clip_limit = 1.0
rate_mat = 0.02
rate_vec = 0.4
far_below = -1e30
bf16 = jnp.bfloat16
f32 = jnp.float32
NN = (((1,), (0,)), ((), ()))
NT = (((1,), (1,)), ((), ()))
TN = (((0,), (0,)), ((), ()))


def dot(left_side, right_side, dims=NN):
    return lax.dot_general(left_side, right_side, dims, preferred_element_type=f32)


def norm_rows(values, gain_row, shift_row):
    centre = values - jnp.mean(values, -1, keepdims=True)
    spread = jnp.mean(centre * centre, -1, keepdims=True)
    inverse = lax.rsqrt(spread + norm_eps)
    scaled = centre * inverse
    return (scaled * gain_row + shift_row, scaled, inverse)


def norm_back(gradient, scaled, inverse, gain_row):
    inner = gradient * gain_row
    return inverse * (
        inner
        - jnp.mean(inner, -1, keepdims=True)
        - scaled * jnp.mean(inner * scaled, -1, keepdims=True)
    )


def pad_rows(values, count):
    if values.shape[0] == count:
        return values
    extra = jnp.zeros((count - values.shape[0],) + values.shape[1:], values.dtype)
    return jnp.concatenate([values, extra], 0)


def head_pair(queries, key_rows, head):
    lane = lax.broadcasted_iota(jnp.int32, queries.shape, 1)
    key_lane = lax.broadcasted_iota(jnp.int32, key_rows.shape, 1)
    key_row = lax.broadcasted_iota(jnp.int32, key_rows.shape, 0)
    spare = HEAD * (1 - head)
    mask = jnp.where(
        (key_lane == spare) & (key_row > PATCHES), jnp.asarray(far_below, bf16), jnp.asarray(0, bf16)
    )
    keys_one = jnp.where((key_lane // HEAD) == head, key_rows, mask)
    queries_one = jnp.where(lane == spare, jnp.asarray(1, bf16), queries)
    return queries_one, keys_one


def attend_forward_kernel(q_ref, k_ref, v_ref, out_ref, total_ref):
    rows = q_ref.shape[1]
    key_count = -(-rows // 128) * 128
    queries = q_ref[0] * jnp.asarray(HEAD**-0.5, bf16)
    key_rows = pad_rows(k_ref[0], key_count)
    value_rows = pad_rows(v_ref[0], key_count)
    lane = lax.broadcasted_iota(jnp.int32, (rows, 128), 1)
    outs, totals = [], []
    for head in range(2):
        queries_one, keys_one = head_pair(queries, key_rows, head)
        scores = dot(queries_one, keys_one, NT)
        highest = jnp.max(scores, 1, keepdims=True)
        shifted = jnp.exp(scores - highest)
        total = jnp.sum(shifted, 1, keepdims=True)
        probability = (shifted * (1.0 / total)).astype(bf16)
        outs.append(dot(probability, value_rows))
        totals.append(highest + jnp.log(total))
    out_ref[0] = jnp.where(lane < HEAD, outs[0], outs[1]).astype(bf16)
    both = jnp.where(lane < HEAD, totals[0], totals[1]).T
    total_ref[0, 0] = jnp.concatenate([both[0:1], both[HEAD : HEAD + 1]], 0)


def attend_backward_kernel(q_ref, k_ref, v_ref, total_ref, grad_ref, dq_ref, dk_ref, dv_ref):
    rows = q_ref.shape[1]
    query_count = -(-rows // 128) * 128
    queries = pad_rows(q_ref[0], query_count) * jnp.asarray(HEAD**-0.5, bf16)
    grads = pad_rows(grad_ref[0], query_count)
    key_rows = k_ref[0]
    value_rows = v_ref[0]
    keys_t = pad_rows(key_rows, query_count).astype(f32).T.astype(bf16)
    lane = lax.broadcasted_iota(jnp.int32, (rows, 128), 1)
    grad_q, grad_k, grad_v = [], [], []
    for head in range(2):
        queries_one, keys_one = head_pair(queries, key_rows, head)
        total = total_ref[0, 0, head : head + 1, :]
        if query_count > rows:
            total = jnp.concatenate([total, jnp.zeros((1, query_count - rows), f32)], 1)
        probability = jnp.exp(dot(keys_one, queries_one, NT) - total)
        values_one = jnp.where((lane // HEAD) == head, value_rows, jnp.asarray(0, bf16))
        grad_prob = dot(values_one, grads, NT)
        inner = jnp.sum(grad_prob * probability, 0, keepdims=True)
        grad_scores = (probability * (grad_prob - inner)).astype(bf16)
        grad_v.append(dot(probability.astype(bf16), grads))
        grad_k.append(dot(grad_scores, queries))
        grad_q.append(dot(keys_t[HEAD * head : HEAD * (head + 1)], pad_rows(grad_scores, query_count)))
    grad_q = jnp.concatenate(grad_q, 0) * HEAD**-0.5
    dq_ref[0] = grad_q.T[:rows].astype(bf16)
    dk_ref[0] = jnp.where(lane < HEAD, grad_k[0], grad_k[1]).astype(bf16)
    dv_ref[0] = jnp.where(lane < HEAD, grad_v[0], grad_v[1]).astype(bf16)


def attend_cost(frames, rows, width, matmuls):
    return pl.CostEstimate(
        flops=2 * matmuls * frames * rows * rows * width,
        bytes_accessed=2 * matmuls * frames * rows * width * 2,
        transcendentals=frames * rows * rows * width // HEAD,
    )


def attend_forward(queries, key_rows, value_rows):
    frames, rows, width = queries.shape
    spec = pl.BlockSpec((1, rows, 128), lambda f, h: (f, 0, h))
    return pl.pallas_call(
        attend_forward_kernel,
        grid=(frames, width // 128),
        in_specs=[spec] * 3,
        out_specs=[spec, pl.BlockSpec((1, 1, 2, rows), lambda f, h: (f, h, 0, 0))],
        out_shape=[
            jax.ShapeDtypeStruct((frames, rows, width), bf16),
            jax.ShapeDtypeStruct((frames, width // 128, 2, rows), f32),
        ],
        compiler_params=pltpu.CompilerParams(vmem_limit_bytes=48 << 20),
        cost_estimate=attend_cost(frames, rows, width, 4),
        name="attend_forward",
    )(queries, key_rows, value_rows)


def attend_backward(queries, key_rows, value_rows, totals, grads):
    frames, rows, width = queries.shape
    spec = pl.BlockSpec((1, rows, 128), lambda f, h: (f, 0, h))
    return pl.pallas_call(
        attend_backward_kernel,
        grid=(frames, width // 128),
        in_specs=[spec] * 3 + [pl.BlockSpec((1, 1, 2, rows), lambda f, h: (f, h, 0, 0)), spec],
        out_specs=[spec] * 3,
        out_shape=[jax.ShapeDtypeStruct((frames, rows, width), bf16)] * 3,
        compiler_params=pltpu.CompilerParams(vmem_limit_bytes=48 << 20),
        cost_estimate=attend_cost(frames, rows, width, 8),
        name="attend_backward",
    )(queries, key_rows, value_rows, totals, grads)


def feed_kernel(
    n2_ref,
    n2t_ref,
    g_ref,
    gt_ref,
    bias_ref,
    up_own_ref,
    up_other_ref,
    down_own_ref,
    down_other_ref,
    out_ref,
    dn2_ref,
    dup_own_ref,
    dup_other_ref,
    ddown_own_ref,
    ddown_other_ref,
    db_ref,
    act_ref,
    dpre_ref,
):
    frames, rows = n2_ref.shape[:2]
    blocks, _, part, chunk = up_own_ref.shape
    half = blocks * part

    @pl.when(pl.program_id(0) == 0)
    def _():
        out_ref[...] = jnp.zeros_like(out_ref)
        dn2_ref[...] = jnp.zeros_like(dn2_ref)
        act_ref[...] = jnp.zeros_like(act_ref)
        dpre_ref[...] = jnp.zeros_like(dpre_ref)

    def whole(own_ref, other_ref):
        return jnp.concatenate(
            [own_ref[:, 0].reshape(half, chunk), other_ref[:, 0].reshape(half, chunk)], 0
        )

    first = whole(up_own_ref, up_other_ref)
    second = whole(down_own_ref, down_other_ref)
    bias_sum = jnp.zeros((1, chunk), f32)
    for frame in range(frames):
        place = pl.ds(frame * rows, rows)
        pre = dot(n2_ref[frame], first) + bias_ref[0]
        sigma = 1.0 / (1.0 + jnp.exp(-1.702 * pre))
        act = (pre * sigma).astype(bf16)
        act_ref[place] = act
        out_ref[frame] += dot(act, second, NT)
        grad_act = dot(g_ref[frame], second)
        grad_pre = grad_act * (sigma + 1.702 * pre * sigma * (1.0 - sigma))
        grad_low = grad_pre.astype(bf16)
        dpre_ref[place] = grad_low
        bias_sum += jnp.sum(grad_low.astype(f32), 0, keepdims=True)
        dn2_ref[frame] += dot(grad_low, first, NT)
    db_ref[0] = bias_sum

    def place_grad(left_ref, right_ref, own_ref, other_ref):
        for at, ref in ((0, own_ref), (half, other_ref)):
            grad = dot(left_ref[at : at + half], right_ref[...]).astype(bf16)
            ref[:, 0] = grad.reshape(blocks, part, chunk)

    place_grad(n2t_ref, dpre_ref, dup_own_ref, dup_other_ref)
    place_grad(gt_ref, act_ref, ddown_own_ref, ddown_other_ref)


def feed_forward(n2, n2t, grads, grads_t, bias, weights):
    frames, rows, _ = n2.shape
    blocks, ff_blocks, part, local = weights[0].shape
    chunk = min(512, local)
    per = local // chunk
    steps = ff_blocks * per
    deep = n2t.shape[1]
    whole3 = lambda n: (0, 0, 0)
    whole2 = lambda n: (0, 0)
    once = pl.Buffered(1)
    w_spec = pl.BlockSpec((blocks, 1, part, chunk), lambda n: (0, n // per, 0, n % per))
    return pl.pallas_call(
        feed_kernel,
        grid=(steps,),
        in_specs=[
            pl.BlockSpec((frames, rows, D), whole3, pipeline_mode=once),
            pl.BlockSpec((D, deep), whole2, pipeline_mode=once),
            pl.BlockSpec((frames, rows, D), whole3, pipeline_mode=once),
            pl.BlockSpec((D, deep), whole2, pipeline_mode=once),
            pl.BlockSpec((1, 1, chunk), lambda n: (n, 0, 0)),
        ]
        + [w_spec] * 4,
        out_specs=[pl.BlockSpec((frames, rows, D), whole3)] * 2
        + [w_spec] * 4
        + [pl.BlockSpec((1, 1, chunk), lambda n: (n, 0, 0))],
        out_shape=[jax.ShapeDtypeStruct((frames, rows, D), f32)] * 2
        + [jax.ShapeDtypeStruct(weights[0].shape, bf16)] * 4
        + [jax.ShapeDtypeStruct((steps, 1, chunk), f32)],
        scratch_shapes=[pltpu.VMEM((deep, chunk), bf16), pltpu.VMEM((deep, chunk), bf16)],
        compiler_params=pltpu.CompilerParams(vmem_limit_bytes=60 << 20),
        cost_estimate=pl.CostEstimate(
            flops=12 * frames * rows * D * ff_blocks * local,
            bytes_accessed=8 * D * ff_blocks * local + 16 * frames * rows * D,
            transcendentals=frames * rows * ff_blocks * local,
        ),
        name="feed_forward",
    )(n2, n2t, grads, grads_t, bias.reshape(steps, 1, chunk), *weights)


def swap(values, axis, bit):
    pairs = [(i, i ^ bit) for i in range(lax.axis_size(axis))]
    return lax.ppermute(values, axis, pairs)


def bits_of(axis):
    size = lax.axis_size(axis)
    return [1 << i for i in range(size.bit_length() - 1)]


def chip_orders():
    bits = bits_of("dp")[1:]
    middle = len(bits) // 2
    return bits[::-1], (bits, bits[middle:] + bits[:middle])


def gather_chips(values, which):
    high_first, orders = chip_orders()
    done = []
    for bit in orders[which]:
        at = sum(b > bit for b in done)
        values = jnp.stack([values, swap(values, "dp", bit)], at)
        done.append(bit)
    return values.reshape((-1,) + values.shape[len(done) :])


def gather_small(values):
    chips = gather_chips(values, 0)
    return jnp.concatenate([chips, swap(chips, "dp", 1)], 0)


def add_low(left_side, right_side):
    return (left_side.astype(f32) + right_side.astype(f32)).astype(bf16)


def scatter_chips(kept, sent, which):
    high_first, orders = chip_orders()
    left = list(high_first)
    shape = (2,) * len(left) + kept.shape[1:]
    kept, received = kept.reshape(shape), swap(sent, "dp", 1).reshape(shape)
    for bit in orders[which][::-1]:
        at = left.index(bit)
        left.remove(bit)
        take = lambda v, i: lax.index_in_dim(v, i, at, keepdims=False)
        going = add_low(take(kept, 1), take(received, 1))
        kept = add_low(take(kept, 0), take(received, 0))
        received = swap(going, "dp", bit)
    return add_low(kept, received)


def scatter_videos(values, earlier):
    if earlier:
        values, _ = lax.optimization_barrier((values, earlier[-1]))
    return lax.psum_scatter(values, "tensor", scatter_dimension=0, tiled=False)


def sum_everywhere(values):
    for axis in ("dp", "tensor"):
        for bit in bits_of(axis):
            values = values + swap(values, axis, bit)
    return values


def gather_videos(values):
    values = values[None]
    for bit in bits_of("tensor"):
        values = jnp.concatenate([values, swap(values, "tensor", bit)], 0)
    order = lax.iota(jnp.int32, values.shape[0]) ^ lax.axis_index("tensor")
    return jnp.take(values, order, axis=0, mode="clip").reshape(-1, values.shape[-1])


def relative_places():
    count = lax.axis_size("dp")
    return [
        lax.axis_index("dp") ^ (2 * (r % (count // 2)) + r // (count // 2)) for r in range(count)
    ]


def absolute_places():
    differs = lax.iota(jnp.int32, lax.axis_size("dp")) ^ lax.axis_index("dp")
    return (differs & 1) * (lax.axis_size("dp") // 2) + (differs >> 1)


def to_relative(values):
    part = D // lax.axis_size("dp")
    return jnp.concatenate(
        [
            lax.dynamic_slice_in_dim(values, place * part, part, values.ndim - 1)
            for place in relative_places()
        ],
        -1,
    )


def to_absolute(values):
    part = D // lax.axis_size("dp")
    places = absolute_places()
    return jnp.concatenate(
        [
            lax.dynamic_slice_in_dim(values, places[i] * part, part, values.ndim - 1)
            for i in range(lax.axis_size("dp"))
        ],
        -1,
    )


def to_heads(rows_in):
    return jnp.moveaxis(rows_in.reshape(rows_in.shape[0], HEADS, HEAD), 1, 0)


def from_heads(values):
    return jnp.moveaxis(values, 0, 1).reshape(values.shape[1], D)


def message_attend(queries, key_rows, value_rows):
    scores = jnp.einsum("hqe,hke->hqk", queries, key_rows, preferred_element_type=f32) * HEAD**-0.5
    highest = jnp.max(scores, -1, keepdims=True)
    shifted = jnp.exp(scores - highest)
    probability = shifted / jnp.sum(shifted, -1, keepdims=True)
    out = jnp.einsum(
        "hqk,hke->hqe", probability.astype(bf16), value_rows, preferred_element_type=f32
    )
    return out, probability


def message_attend_back(queries, key_rows, value_rows, probability, grads):
    grad_prob = jnp.einsum("hqe,hke->hqk", grads, value_rows, preferred_element_type=f32)
    grad_scores = (
        probability * (grad_prob - jnp.sum(grad_prob * probability, -1, keepdims=True))
    ).astype(bf16)
    scale = HEAD**-0.5
    grad_q = jnp.einsum("hqk,hke->hqe", grad_scores, key_rows, preferred_element_type=f32) * scale
    grad_k = jnp.einsum("hqk,hqe->hke", grad_scores, queries, preferred_element_type=f32) * scale
    grad_v = jnp.einsum("hqk,hqe->hke", probability.astype(bf16), grads, preferred_element_type=f32)
    return grad_q, grad_k, grad_v


def adam_step(weight, first_moment, second_moment, gradient, factor, step_rate, decay_rate):
    clipped = gradient * factor
    first_new = beta_one * first_moment + (1.0 - beta_one) * clipped
    second_new = beta_two * second_moment + (1.0 - beta_two) * clipped * clipped
    update = (
        first_new
        / (1.0 - beta_one**STEP)
        / (jnp.sqrt(second_new / (1.0 - beta_two**STEP)) + adam_eps)
    )
    weight_new = weight - step_rate * (update + decay_rate * weight)
    return (first_new, second_new, weight_new)


def on_device(
    tokens,
    cotangent,
    attn_master,
    attn_first,
    attn_second,
    attn_ema,
    mlp_master,
    mlp_first,
    mlp_second,
    mlp_ema,
    msg_master,
    msg_first,
    msg_second,
    msg_ema,
    vec_master,
    vec_first,
    vec_second,
    vec_ema,
):
    z_index = lax.axis_index("tensor")
    z_count = lax.axis_size("tensor")
    dp_index = lax.axis_index("dp")
    dp_count = lax.axis_size("dp")
    part = attn_master.shape[0]
    local_width = attn_master.shape[2]
    local_ff = mlp_master.shape[2]
    frames = tokens.shape[0] // PATCHES
    half_ff = local_ff // 2

    attn_z = lax.all_gather(jnp.swapaxes(attn_master, 0, 1).astype(bf16), "tensor", axis=0)
    mlp_z = lax.all_gather(jnp.swapaxes(mlp_master, 0, 1).astype(bf16), "tensor", axis=0)
    vec_all = gather_small(vec_master.astype(bf16).T)
    class_own = tokens.reshape(frames, PATCHES, D)[:, 0]
    class_rows = gather_videos(class_own)

    def both_cores(values):
        return [values, swap(values, "dp", 1)]

    msg_low = jnp.swapaxes(msg_master, 0, 1).astype(bf16)
    msg_half = [
        both_cores(gather_chips(msg_low[..., i * D // 2 : (i + 1) * D // 2], i)) for i in range(2)
    ]
    attn_half = [both_cores(gather_chips(attn_z[:, 2 * i : 2 * i + 2], i)) for i in range(2)]
    mlp_parts = [
        [
            side
            for i in range(2)
            for side in both_cores(gather_chips(mlp_z[:, i, :, j * half_ff : (j + 1) * half_ff], i))
        ]
        for j in range(2)
    ]
    vec_rel = jnp.moveaxis(vec_all, 0, 1).reshape(-1, D).astype(f32)
    vectors = to_absolute(vec_rel)
    ff_bias = vectors[14:].reshape(z_count, 2, half_ff)
    msg_w = [
        jnp.concatenate(
            [
                jnp.concatenate([side[:, i].reshape(D // 2, D // 2) for side in sides], 0)
                for sides in msg_half
            ],
            1,
        )
        for i in range(5)
    ]
    attn_w = [
        jnp.concatenate(
            [
                jnp.swapaxes(side[:, :, i % 2], 1, 2).reshape(D // 2, z_count * local_width)
                for side in attn_half[i // 2]
            ],
            0,
        )
        for i in range(4)
    ]

    first_msg = dot(to_relative(class_rows), msg_w[0]) + vectors[6]
    normed_msg, scaled_msg, inverse_msg = norm_rows(first_msg, vectors[4], vectors[5])
    normed_msg = normed_msg.astype(bf16)
    normed_rel = to_relative(normed_msg)
    msg_q = to_heads((dot(normed_rel, msg_w[1]) + vectors[7]).astype(bf16))
    msg_k = to_heads(dot(normed_rel, msg_w[2]).astype(bf16))
    msg_v = to_heads((dot(normed_rel, msg_w[3]) + vectors[8]).astype(bf16))
    msg_out, msg_prob = message_attend(msg_q, msg_k, msg_v)
    msg_mixed = from_heads(msg_out).astype(bf16)
    message = first_msg + dot(to_relative(msg_mixed), msg_w[4]) + vectors[9]
    own_message = to_relative(lax.dynamic_slice_in_dim(message, z_index * frames, frames, 0))

    token_rows = to_relative(tokens).reshape(frames, PATCHES, D)
    zero_rows = jnp.zeros((frames, ROWS - PATCHES - 1, D), f32)
    full_rows = jnp.concatenate(
        [token_rows.astype(f32), own_message[:, None], zero_rows], axis=1
    )
    normed, scaled, inverse = norm_rows(full_rows, vec_rel[0], vec_rel[1])
    normed = normed.astype(bf16).reshape(frames * ROWS, D)
    queries = (dot(normed, attn_w[0]) + vectors[10]).astype(bf16).reshape(frames, ROWS, D)
    key_rows = dot(normed, attn_w[1]).astype(bf16).reshape(frames, ROWS, D)
    value_rows = (dot(normed, attn_w[2]) + vectors[11]).astype(bf16).reshape(frames, ROWS, D)
    attended, totals = attend_forward(queries, key_rows, value_rows)
    attended_flat = attended.reshape(frames * ROWS, D)
    middle = (
        full_rows + dot(attended_flat, attn_w[3], NT).reshape(frames, ROWS, D) + vec_rel[12]
    )

    scaled_gain, scaled_mid, inverse_mid = norm_rows(
        middle.astype(bf16).astype(f32), vec_rel[2], vec_rel[3]
    )
    normed_mid = scaled_gain.astype(bf16)
    grads = jnp.concatenate(
        [
            to_relative(cotangent).reshape(frames, PATCHES, D),
            jnp.zeros((frames, ROWS - PATCHES, D), bf16),
        ],
        1,
    )
    deep = -(-frames * ROWS // 128) * 128
    normed_mid_t = pad_rows(normed_mid.reshape(frames * ROWS, D), deep).T
    grads_t = pad_rows(grads.reshape(frames * ROWS, D), deep).T
    mlp_out, grad_mid_in, mlp_grads, bias_grads = 0.0, 0.0, [], []
    for j in range(2):
        out_j, dn2_j, *dw_j, db_j = feed_forward(
            normed_mid, normed_mid_t, grads, grads_t, ff_bias[:, j], mlp_parts[j]
        )
        mlp_out += out_j
        grad_mid_in += dn2_j
        sums = [scatter_chips(dw_j[2 * i], dw_j[2 * i + 1], i) for i in range(2)]
        mlp_grads.append(scatter_videos(jnp.stack(sums, 1), mlp_grads))
        bias_grads.append(db_j.reshape(z_count, half_ff))
    block_output = to_absolute(
        (middle + mlp_out + vec_rel[13])[:, :PATCHES].reshape(-1, D)
    )
    ff_bias_grad = jnp.stack(bias_grads, 1).reshape(FF // D, D)

    back_mid = norm_back(grad_mid_in, scaled_mid, inverse_mid, vec_rel[2])
    middle_grad = (grads.astype(f32) + back_mid).astype(bf16)
    middle_flat = middle_grad.reshape(frames * ROWS, D)
    grad_attended = dot(middle_flat, attn_w[3]).astype(bf16).reshape(frames, ROWS, D)
    grad_out_w = dot(middle_flat, attended_flat, TN).astype(bf16)
    grad_q, grad_k, grad_v = attend_backward(queries, key_rows, value_rows, totals, grad_attended)
    flat = [g.reshape(frames * ROWS, D) for g in (grad_q, grad_k, grad_v)]
    attn_full = [dot(normed, g, TN).astype(bf16) for g in flat] + [grad_out_w]
    attn_sums = []
    for i in range(2):
        sides = []
        for side in range(2):
            rows = [
                g[side * D // 2 : (side + 1) * D // 2].reshape(-1, part, z_count, local_width)
                for g in attn_full[2 * i : 2 * i + 2]
            ]
            sides.append(jnp.stack([jnp.swapaxes(g, 1, 2) for g in rows], 2))
        attn_sums.append(scatter_chips(sides[0], sides[1], i))
    attn_grad = scatter_videos(jnp.concatenate(attn_sums, 1), mlp_grads)
    attn_grad = jnp.swapaxes(attn_grad, 0, 1).astype(f32)
    grad_normed = (
        dot(flat[0], attn_w[0], NT) + dot(flat[1], attn_w[1], NT) + dot(flat[2], attn_w[2], NT)
    ).reshape(frames, ROWS, D)
    back_rows = norm_back(grad_normed, scaled, inverse, vec_rel[0])
    input_grad = middle_grad.astype(f32) + back_rows

    msg_grad_own = to_absolute(back_rows[:, PATCHES].astype(bf16))
    msg_grad_low = gather_videos(msg_grad_own)
    grad_mixed = to_absolute(dot(msg_grad_low, msg_w[4], NT).astype(bf16))
    msg_dq, msg_dk, msg_dv = message_attend_back(
        msg_q, msg_k, msg_v, msg_prob, to_heads(grad_mixed)
    )
    msg_dq, msg_dk, msg_dv = (from_heads(g).astype(bf16) for g in (msg_dq, msg_dk, msg_dv))
    grad_normed_msg = to_absolute(
        dot(msg_dq, msg_w[1], NT) + dot(msg_dk, msg_w[2], NT) + dot(msg_dv, msg_w[3], NT)
    )
    back_first = norm_back(grad_normed_msg, scaled_msg, inverse_msg, vectors[4])
    grad_first = (msg_grad_low.astype(f32) + back_first).astype(bf16)
    grad_class = dot(grad_first, msg_w[0], NT)
    own_class = lax.dynamic_slice_in_dim(grad_class, z_index * frames, frames, 0)
    class_mark = (lax.iota(jnp.int32, PATCHES) == 0)[None, :, None]
    input_grad = to_absolute(
        (input_grad[:, :PATCHES] + jnp.where(class_mark, own_class[:, None], 0.0)).reshape(-1, D)
    )
    sent = jnp.stack(
        [class_rows, normed_msg, msg_mixed, grad_first, msg_dq, msg_dk, msg_dv, msg_grad_low], 0
    )
    everyone = jnp.moveaxis(gather_small(sent), 0, 1).reshape(8, -1, D)
    mine = lax.dynamic_slice_in_dim(everyone[:3], dp_index * part, part, 2)
    msg_grad = jnp.stack(
        [
            dot(mine[0], everyone[3], TN),
            dot(mine[1], everyone[4], TN),
            dot(mine[1], everyone[5], TN),
            dot(mine[1], everyone[6], TN),
            dot(mine[2], everyone[7], TN),
        ],
        1,
    )

    def over_rows(values):
        return jnp.sum(values.astype(f32), (0, 1))

    def over_messages(values):
        return jnp.where(z_index == 0, jnp.sum(values.astype(f32), 0), 0.0)

    relative = to_absolute(
        jnp.stack(
            [
                over_rows(grad_normed * scaled),
                over_rows(grad_normed),
                over_rows(grad_mid_in * scaled_mid),
                over_rows(grad_mid_in),
                over_rows(middle_grad),
                over_rows(grads),
            ]
        )
    )
    straight = jnp.stack(
        [
            over_messages(grad_normed_msg * scaled_msg),
            over_messages(grad_normed_msg),
            over_messages(grad_first),
            over_messages(msg_dq),
            over_messages(msg_dv),
            over_messages(msg_grad_low),
            over_rows(grad_q),
            over_rows(grad_v),
        ]
    )
    table = sum_everywhere(
        jnp.concatenate([relative[:4], straight, relative[4:], ff_bias_grad], 0)
    )
    vec_grad = lax.dynamic_slice_in_dim(table, dp_index * part, part, 1).T

    mlp_grad = jnp.swapaxes(jnp.concatenate(mlp_grads, 2), 0, 1).astype(f32)

    keep_share = (z_index == 0).astype(f32)
    squares = (
        jnp.sum(attn_grad * attn_grad)
        + jnp.sum(mlp_grad * mlp_grad)
        + keep_share * (jnp.sum(msg_grad * msg_grad) + jnp.sum(vec_grad * vec_grad))
    )
    squares = sum_everywhere(jnp.broadcast_to(squares, (8, 128)))[0, 0]
    grad_norm = jnp.sqrt(squares)
    factor = clip_limit / jnp.maximum(grad_norm, clip_limit)

    def update(master, first, second, ema, grad, rate, decay):
        first_new, second_new, weight = adam_step(master, first, second, grad, factor, rate, decay)
        return grad, first_new, second_new, weight, ema_keep * ema + (1.0 - ema_keep) * weight

    return (
        block_output,
        input_grad,
        grad_norm,
        *update(attn_master, attn_first, attn_second, attn_ema, attn_grad, rate_mat, decay_mat),
        *update(mlp_master, mlp_first, mlp_second, mlp_ema, mlp_grad, rate_mat, decay_mat),
        *update(msg_master, msg_first, msg_second, msg_ema, msg_grad, rate_mat, decay_mat),
        *update(vec_master, vec_first, vec_second, vec_ema, vec_grad, rate_vec, 0.0),
    )


def solution(mesh):
    rows = P(("dp", "tensor"), None)
    split = P("dp", None, "tensor")
    copied = P("dp", None, None)
    table = P("dp", None)
    in_specs = (rows,) * 2 + (split,) * 8 + (copied,) * 4 + (table,) * 4
    out_specs = (rows,) * 2 + (P(),) + (split,) * 10 + (copied,) * 5 + (table,) * 5
    return jax.shard_map(
        on_device, mesh=mesh, in_specs=in_specs, out_specs=out_specs, check_vma=False
    )
```

```python
import jax
import jax.numpy as jnp
from jax import lax
from jax.experimental import pallas as pl
from jax.experimental.pallas import tpu as pltpu
from jax.sharding import PartitionSpec as P

D = 1024
HEADS = 16
HEAD = 64
FF = 4096
PATCHES = 577
FRAMES = 8
STEP = 10
ROWS = 592


norm_eps = 1e-05
beta_one = 0.9
beta_two = 0.95
adam_eps = 1e-08
decay_mat = 0.05
ema_keep = 0.7
clip_limit = 1.0
rate_mat = 0.02
rate_vec = 0.4
far_below = -1e30
bf16 = jnp.bfloat16
f32 = jnp.float32
NN = (((1,), (0,)), ((), ()))
NT = (((1,), (1,)), ((), ()))
TN = (((0,), (0,)), ((), ()))


def dot(left_side, right_side, dims=NN):
    return lax.dot_general(left_side, right_side, dims, preferred_element_type=f32)


def norm_rows(values, gain_row, shift_row):
    centre = values - jnp.mean(values, -1, keepdims=True)
    spread = jnp.mean(centre * centre, -1, keepdims=True)
    inverse = lax.rsqrt(spread + norm_eps)
    scaled = centre * inverse
    return (scaled * gain_row + shift_row, scaled, inverse)


def norm_back(gradient, scaled, inverse, gain_row):
    inner = gradient * gain_row
    return inverse * (
        inner
        - jnp.mean(inner, -1, keepdims=True)
        - scaled * jnp.mean(inner * scaled, -1, keepdims=True)
    )


def pad_rows(values, count):
    if values.shape[0] == count:
        return values
    extra = jnp.zeros((count - values.shape[0],) + values.shape[1:], values.dtype)
    return jnp.concatenate([values, extra], 0)


def head_pair(queries, key_rows, head):
    lane = lax.broadcasted_iota(jnp.int32, queries.shape, 1)
    key_lane = lax.broadcasted_iota(jnp.int32, key_rows.shape, 1)
    key_row = lax.broadcasted_iota(jnp.int32, key_rows.shape, 0)
    spare = HEAD * (1 - head)
    mask = jnp.where(
        (key_lane == spare) & (key_row > PATCHES), jnp.asarray(far_below, bf16), jnp.asarray(0, bf16)
    )
    keys_one = jnp.where((key_lane // HEAD) == head, key_rows, mask)
    queries_one = jnp.where(lane == spare, jnp.asarray(1, bf16), queries)
    return queries_one, keys_one


def attend_forward_kernel(q_ref, k_ref, v_ref, out_ref, total_ref):
    rows = q_ref.shape[1]
    key_count = -(-rows // 128) * 128
    queries = q_ref[0] * jnp.asarray(HEAD**-0.5, bf16)
    key_rows = pad_rows(k_ref[0], key_count)
    value_rows = pad_rows(v_ref[0], key_count)
    lane = lax.broadcasted_iota(jnp.int32, (rows, 128), 1)
    outs, totals = [], []
    for head in range(2):
        queries_one, keys_one = head_pair(queries, key_rows, head)
        scores = dot(queries_one, keys_one, NT)
        highest = jnp.max(scores, 1, keepdims=True)
        shifted = jnp.exp(scores - highest)
        total = jnp.sum(shifted, 1, keepdims=True)
        probability = (shifted * (1.0 / total)).astype(bf16)
        outs.append(dot(probability, value_rows))
        totals.append(highest + jnp.log(total))
    out_ref[0] = jnp.where(lane < HEAD, outs[0], outs[1]).astype(bf16)
    both = jnp.where(lane < HEAD, totals[0], totals[1]).T
    total_ref[0, 0] = jnp.concatenate([both[0:1], both[HEAD : HEAD + 1]], 0)


def attend_backward_kernel(q_ref, k_ref, v_ref, total_ref, grad_ref, *rest):
    dq_ref, dk_ref, dv_ref = rest[-3:]
    rows = q_ref.shape[1]
    query_count = -(-rows // 128) * 128
    queries = pad_rows(q_ref[0], query_count) * jnp.asarray(HEAD**-0.5, bf16)
    grads = pad_rows(grad_ref[0], query_count)
    key_rows = k_ref[0]
    value_rows = v_ref[0]
    keys_t = pad_rows(key_rows, query_count).astype(f32).T.astype(bf16)
    lane = lax.broadcasted_iota(jnp.int32, (rows, 128), 1)
    grad_q, grad_k, grad_v = [], [], []
    for head in range(2):
        queries_one, keys_one = head_pair(queries, key_rows, head)
        total = total_ref[0, 0, head : head + 1, :]
        if query_count > rows:
            total = jnp.concatenate([total, jnp.zeros((1, query_count - rows), f32)], 1)
        probability = jnp.exp(dot(keys_one, queries_one, NT) - total)
        values_one = jnp.where((lane // HEAD) == head, value_rows, jnp.asarray(0, bf16))
        grad_prob = dot(values_one, grads, NT)
        inner = jnp.sum(grad_prob * probability, 0, keepdims=True)
        grad_scores = (probability * (grad_prob - inner)).astype(bf16)
        grad_v.append(dot(probability.astype(bf16), grads))
        grad_k.append(dot(grad_scores, queries))
        grad_q.append(dot(keys_t[HEAD * head : HEAD * (head + 1)], pad_rows(grad_scores, query_count)))
    grad_q = jnp.concatenate(grad_q, 0) * HEAD**-0.5
    dq_ref[0] = grad_q.T[:rows].astype(bf16)
    dk_ref[0] = jnp.where(lane < HEAD, grad_k[0], grad_k[1]).astype(bf16)
    dv_ref[0] = jnp.where(lane < HEAD, grad_v[0], grad_v[1]).astype(bf16)


def attend_cost(frames, rows, width, matmuls):
    return pl.CostEstimate(
        flops=2 * matmuls * frames * rows * rows * width,
        bytes_accessed=2 * matmuls * frames * rows * width * 2,
        transcendentals=frames * rows * rows * width // HEAD,
    )


def attend_forward(queries, key_rows, value_rows):
    frames, rows, width = queries.shape
    spec = pl.BlockSpec((1, rows, 128), lambda f, h: (f, 0, h))
    return pl.pallas_call(
        attend_forward_kernel,
        grid=(frames, width // 128),
        in_specs=[spec] * 3,
        out_specs=[spec, pl.BlockSpec((1, 1, 2, rows), lambda f, h: (f, h, 0, 0))],
        out_shape=[
            jax.ShapeDtypeStruct((frames, rows, width), bf16),
            jax.ShapeDtypeStruct((frames, width // 128, 2, rows), f32),
        ],
        compiler_params=pltpu.CompilerParams(vmem_limit_bytes=48 << 20),
        cost_estimate=attend_cost(frames, rows, width, 4),
        name="attend_forward",
    )(queries, key_rows, value_rows)


def attend_backward(queries, key_rows, value_rows, totals, grads, begin, count, earlier=()):
    frames, rows, width = queries.shape
    spec = pl.BlockSpec((1, rows, 128), lambda f, h: (f, 0, h + begin))
    total_spec = pl.BlockSpec((1, 1, 2, rows), lambda f, h: (f, h + begin, 0, 0))
    return pl.pallas_call(
        attend_backward_kernel,
        grid=(frames, count),
        in_specs=[spec] * 3 + [total_spec, spec] + [pl.BlockSpec(memory_space=pl.ANY)] * len(earlier),
        out_specs=[spec] * 3,
        out_shape=[jax.ShapeDtypeStruct((frames, rows, width), bf16)] * 3,
        input_output_aliases={5 + i: i for i in range(len(earlier))},
        compiler_params=pltpu.CompilerParams(vmem_limit_bytes=48 << 20),
        cost_estimate=attend_cost(frames, rows, count * 128, 8),
        name="attend_backward",
    )(queries, key_rows, value_rows, totals, grads, *earlier)


def feed_kernel(
    n2_ref,
    n2t_ref,
    g_ref,
    gt_ref,
    bias_ref,
    up_own_ref,
    up_other_ref,
    down_own_ref,
    down_other_ref,
    out_ref,
    dn2_ref,
    dup_own_ref,
    dup_other_ref,
    ddown_own_ref,
    ddown_other_ref,
    db_ref,
    act_ref,
    dpre_ref,
):
    frames, rows = n2_ref.shape[:2]
    blocks, _, part, chunk = up_own_ref.shape
    half = blocks * part

    @pl.when(pl.program_id(0) == 0)
    def _():
        out_ref[...] = jnp.zeros_like(out_ref)
        dn2_ref[...] = jnp.zeros_like(dn2_ref)
        act_ref[...] = jnp.zeros_like(act_ref)
        dpre_ref[...] = jnp.zeros_like(dpre_ref)

    def whole(own_ref, other_ref):
        return jnp.concatenate(
            [own_ref[:, 0].reshape(half, chunk), other_ref[:, 0].reshape(half, chunk)], 0
        )

    first = whole(up_own_ref, up_other_ref)
    second = whole(down_own_ref, down_other_ref)
    bias_sum = jnp.zeros((1, chunk), f32)
    for frame in range(frames):
        place = pl.ds(frame * rows, rows)
        pre = dot(n2_ref[frame], first) + bias_ref[0]
        sigma = 1.0 / (1.0 + jnp.exp(-1.702 * pre))
        act = (pre * sigma).astype(bf16)
        act_ref[place] = act
        out_ref[frame] += dot(act, second, NT)
        grad_act = dot(g_ref[frame], second)
        grad_pre = grad_act * (sigma + 1.702 * pre * sigma * (1.0 - sigma))
        grad_low = grad_pre.astype(bf16)
        dpre_ref[place] = grad_low
        bias_sum += jnp.sum(grad_low.astype(f32), 0, keepdims=True)
        dn2_ref[frame] += dot(grad_low, first, NT)
    db_ref[0] = bias_sum

    def place_grad(left_ref, right_ref, own_ref, other_ref):
        for at, ref in ((0, own_ref), (half, other_ref)):
            grad = dot(left_ref[at : at + half], right_ref[...]).astype(bf16)
            ref[:, 0] = grad.reshape(blocks, part, chunk)

    place_grad(n2t_ref, dpre_ref, dup_own_ref, dup_other_ref)
    place_grad(gt_ref, act_ref, ddown_own_ref, ddown_other_ref)


def feed_forward(n2, n2t, grads, grads_t, bias, weights):
    frames, rows, _ = n2.shape
    blocks, ff_blocks, part, local = weights[0].shape
    chunk = min(512, local)
    per = local // chunk
    steps = ff_blocks * per
    deep = n2t.shape[1]
    whole3 = lambda n: (0, 0, 0)
    whole2 = lambda n: (0, 0)
    single = pl.Buffered(1)
    w_spec = pl.BlockSpec((blocks, 1, part, chunk), lambda n: (0, n // per, 0, n % per))
    return pl.pallas_call(
        feed_kernel,
        grid=(steps,),
        in_specs=[
            pl.BlockSpec((frames, rows, D), whole3, pipeline_mode=single),
            pl.BlockSpec((D, deep), whole2, pipeline_mode=single),
            pl.BlockSpec((frames, rows, D), whole3, pipeline_mode=single),
            pl.BlockSpec((D, deep), whole2, pipeline_mode=single),
            pl.BlockSpec((1, 1, chunk), lambda n: (n, 0, 0)),
        ]
        + [w_spec] * 4,
        out_specs=[pl.BlockSpec((frames, rows, D), whole3)] * 2
        + [w_spec] * 4
        + [pl.BlockSpec((1, 1, chunk), lambda n: (n, 0, 0))],
        out_shape=[jax.ShapeDtypeStruct((frames, rows, D), f32)] * 2
        + [jax.ShapeDtypeStruct(weights[0].shape, bf16)] * 4
        + [jax.ShapeDtypeStruct((steps, 1, chunk), f32)],
        scratch_shapes=[pltpu.VMEM((deep, chunk), bf16), pltpu.VMEM((deep, chunk), bf16)],
        compiler_params=pltpu.CompilerParams(vmem_limit_bytes=60 << 20),
        cost_estimate=pl.CostEstimate(
            flops=12 * frames * rows * D * ff_blocks * local,
            bytes_accessed=8 * D * ff_blocks * local + 16 * frames * rows * D,
            transcendentals=frames * rows * ff_blocks * local,
        ),
        name="feed_forward",
    )(n2, n2t, grads, grads_t, bias.reshape(steps, 1, chunk), *weights)


BLOCK = 128
BLOCKS = D // BLOCK


def permuted(ref, info_ref, first):
    return jnp.concatenate(
        [
            ref[:, pl.ds(pl.multiple_of(info_ref[first + i] * BLOCK, BLOCK), BLOCK)]
            for i in range(BLOCKS)
        ],
        1,
    )


def call(kernel, info, args, grid, in_specs, out_specs, out_shape, name, scratch=(), flops=0, vmem=56):
    moved = sum(a.size * a.dtype.itemsize for a in args)
    moved += sum(o.size * o.dtype.itemsize for o in out_shape)
    return pl.pallas_call(
        kernel,
        grid_spec=pltpu.PrefetchScalarGridSpec(
            num_scalar_prefetch=1,
            grid=grid,
            in_specs=in_specs,
            out_specs=out_specs,
            scratch_shapes=list(scratch),
        ),
        out_shape=out_shape,
        compiler_params=pltpu.CompilerParams(vmem_limit_bytes=vmem << 20),
        cost_estimate=pl.CostEstimate(flops=flops, bytes_accessed=moved, transcendentals=0),
        name=name,
    )(info, *args)


def shaped(dtype, *shape):
    return jax.ShapeDtypeStruct(shape, dtype)


def once(*block, at=None):
    index = at or (0,) * len(block)
    return pl.BlockSpec(block, lambda *_: index, pipeline_mode=pl.Buffered(1))


def kept(*block):
    index = (0,) * len(block)
    return pl.BlockSpec(block, lambda *_: index)


def row_count(frames):
    return -(-frames * ROWS // 128) * 128


def prepare_kernel(info_ref, tokens_ref, cot_ref, x_ref, g_ref, gt_ref, gsum_ref, hold_ref):
    frames = x_ref.shape[0]
    count = tokens_ref.shape[0]
    inside = lax.broadcasted_iota(jnp.int32, (ROWS, BLOCK), 0) < PATCHES
    hold_ref[...] = jnp.zeros_like(hold_ref)

    def padded(ref):
        hold_ref[0:count] = ref[...].astype(f32)
        return [
            jnp.where(inside, hold_ref[pl.ds(f * PATCHES, ROWS)], 0.0) for f in range(frames)
        ]

    for f, rows in enumerate(padded(tokens_ref)):
        x_ref[f] = rows.astype(bf16)
    grads = padded(cot_ref)
    for f, rows in enumerate(grads):
        g_ref[f] = rows.astype(bf16)
    full = pad_rows(jnp.concatenate(grads, 0), gt_ref.shape[1])
    gt_ref[...] = full.T.astype(bf16)
    gsum_ref[...] = jnp.sum(full, 0, keepdims=True)


def prepare(info, tokens, cotangent):
    count = tokens.shape[0]
    frames = count // PATCHES
    deep = row_count(frames)
    taken = pl.BlockSpec((count, BLOCK), lambda r, info_ref: (0, info_ref[r]))
    placed = pl.BlockSpec((frames, ROWS, BLOCK), lambda r, info_ref: (0, 0, r))
    return call(
        prepare_kernel,
        info,
        (tokens, cotangent),
        (BLOCKS,),
        [taken] * 2,
        [
            placed,
            placed,
            pl.BlockSpec((BLOCK, deep), lambda r, info_ref: (r, 0)),
            pl.BlockSpec((1, BLOCK), lambda r, info_ref: (0, r)),
        ],
        [
            shaped(bf16, frames, ROWS, D),
            shaped(bf16, frames, ROWS, D),
            shaped(bf16, D, deep),
            shaped(f32, 1, D),
        ],
        "prepare",
        [pltpu.VMEM((-(-((frames - 1) * PATCHES + ROWS) // 8) * 8, BLOCK), f32)],
    )


def plain_order_kernel(info_ref, in_ref, out_ref):
    out_ref[...] = permuted(in_ref, info_ref, BLOCKS)


def plain_order(info, values):
    return call(
        plain_order_kernel,
        info,
        (values,),
        (1,),
        [kept(*values.shape)],
        [kept(*values.shape)],
        [shaped(f32, *values.shape)],
        "plain_order",
    )[0]


def finish_kernel(info_ref, *refs):
    *in_refs, row_ref, out_ref = refs
    frames = in_refs[0].shape[0]
    for f in range(frames):
        rows = in_refs[0][f]
        for ref in in_refs[1:]:
            rows = rows + ref[f]
        if row_ref.shape[0] == 1:
            rows = rows + row_ref[...]
        else:
            class_row = row_ref[pl.ds(info_ref[2 * BLOCKS] * frames + f, 1)]
            first = lax.broadcasted_iota(jnp.int32, (ROWS, BLOCK), 0) == 0
            rows = rows + jnp.where(first, class_row, 0.0)
        out_ref[pl.ds(f * PATCHES, PATCHES)] = rows[:PATCHES]


def finish(info, parts, row, name):
    frames = parts[0].shape[0]
    taken = pl.BlockSpec((frames, ROWS, BLOCK), lambda d, info_ref: (0, 0, info_ref[BLOCKS + d]))
    row_spec = pl.BlockSpec((row.shape[0], BLOCK), lambda d, info_ref: (0, info_ref[BLOCKS + d]))
    return call(
        finish_kernel,
        info,
        (*parts, row),
        (BLOCKS,),
        [taken] * len(parts) + [row_spec],
        [pl.BlockSpec((frames * PATCHES, BLOCK), lambda d, info_ref: (0, d))],
        [shaped(f32, frames * PATCHES, D)],
        name,
    )[0]


def with_message(x_ref, msg_ref, info_ref, f):
    frames = x_ref.shape[0]
    message = msg_ref[pl.ds(info_ref[2 * BLOCKS] * frames + f, 1)]
    place = lax.broadcasted_iota(jnp.int32, (ROWS, D), 0) == PATCHES
    return jnp.where(place, message, x_ref[f].astype(f32))


def put_transposed(ref, rows):
    for c in range(BLOCKS):
        block = pad_rows(rows[:, c * BLOCK : (c + 1) * BLOCK].astype(f32), ref.shape[1])
        ref[c * BLOCK : (c + 1) * BLOCK] = block.T.astype(bf16)


def halves(own_ref, other_ref, *at):
    return [ref[(slice(None), *at)].reshape(D // 2, ref.shape[-1]) for ref in (own_ref, other_ref)]


def project_kernel(
    info_ref, x_ref, msg_ref, gain_ref, shift_ref, bq_ref, bv_ref, ao_ref, ap_ref, bo_ref, bp_ref,
    q_ref, k_ref, v_ref, ht_ref, h_ref,
):
    frames = x_ref.shape[0]

    @pl.when(pl.program_id(0) == 0)
    def _():
        for f in range(frames):
            rows = with_message(x_ref, msg_ref, info_ref, f)
            normed = norm_rows(rows, gain_ref[...], shift_ref[...])[0]
            h_ref[pl.ds(f * ROWS, ROWS)] = normed.astype(bf16)
        put_transposed(ht_ref, h_ref[...])

    sides = (slice(0, D // 2), slice(D // 2, D))
    for out_ref, weights, bias in (
        (q_ref, halves(ao_ref, ap_ref, 0, 0), bq_ref[...]),
        (k_ref, halves(ao_ref, ap_ref, 0, 1), 0.0),
        (v_ref, halves(bo_ref, bp_ref, 0, 0), bv_ref[...]),
    ):
        for f in range(frames):
            place = pl.ds(f * ROWS, ROWS)
            rows = dot(h_ref[place, sides[0]], weights[0]) + dot(h_ref[place, sides[1]], weights[1])
            out_ref[f] = (rows + bias).astype(bf16)


def project(info, x, message, vec_rel, vectors, attn):
    frames = x.shape[0]
    n, z, _, part, width = attn[0].shape
    deep = row_count(frames)
    bias = pl.BlockSpec((1, width), lambda j, info_ref: (0, j))
    a_spec = pl.BlockSpec((n, 1, 2, part, width), lambda j, info_ref: (0, j, 0, 0, 0))
    b_spec = pl.BlockSpec((n, 1, 1, part, width), lambda j, info_ref: (0, j, 0, 0, 0))
    out = pl.BlockSpec((frames, ROWS, width), lambda j, info_ref: (0, 0, j))
    return call(
        project_kernel,
        info,
        (x, message, vec_rel[0:1], vec_rel[1:2], vectors[10:11], vectors[11:12], *attn),
        (z,),
        [once(frames, ROWS, D), once(FRAMES, D), once(1, D), once(1, D), bias, bias]
        + [a_spec] * 2
        + [b_spec] * 2,
        [out] * 3 + [kept(D, deep)],
        [shaped(bf16, frames, ROWS, D)] * 3 + [shaped(bf16, D, deep)],
        "project",
        [pltpu.VMEM((frames * ROWS, D), bf16)],
        6 * frames * ROWS * D * D,
    )


def combine_kernel(
    info_ref, x_ref, a_ref, bias_ref, gain_ref, shift_ref, bo_ref, bp_ref, mid_ref, n2_ref, n2t_ref, hold_ref
):
    frames = x_ref.shape[0]
    z, width = bo_ref.shape[1], bo_ref.shape[-1]
    for f in range(frames):
        for side, ref in enumerate((bo_ref, bp_ref)):
            half = slice(side * D // 2, (side + 1) * D // 2)
            total = x_ref[f, :, half].astype(f32) + bias_ref[:, half]
            for j in range(z):
                weight = ref[:, j, 0].reshape(D // 2, width)
                total += dot(a_ref[f, :, j * width : (j + 1) * width], weight, NT)
            mid_ref[f, :, half] = total
        low = mid_ref[f].astype(bf16).astype(f32)
        normed = norm_rows(low, gain_ref[...], shift_ref[...])[0].astype(bf16)
        n2_ref[f] = normed
        hold_ref[pl.ds(f * ROWS, ROWS)] = normed
    put_transposed(n2t_ref, hold_ref[...])


def combine(info, x, attended, vec_rel, attn):
    frames = x.shape[0]
    n, z, _, part, width = attn[2].shape
    deep = row_count(frames)
    weight = once(n, z, 1, part, width, at=(0, 0, 1, 0, 0))
    return call(
        combine_kernel,
        info,
        (x, attended, vec_rel[12:13], vec_rel[2:3], vec_rel[3:4], attn[2], attn[3]),
        (1,),
        [once(frames, ROWS, D)] * 2 + [once(1, D)] * 3 + [weight] * 2,
        [once(frames, ROWS, D), once(frames, ROWS, D), once(D, deep)],
        [shaped(f32, frames, ROWS, D), shaped(bf16, frames, ROWS, D), shaped(bf16, D, deep)],
        "combine",
        [pltpu.VMEM((frames * ROWS, D), bf16)],
        2 * frames * ROWS * D * D,
    )


def between_kernel(
    info_ref, ea_ref, eb_ref, mid_ref, g_ref, a_ref, gain_ref, bo_ref, bp_ref,
    dmid_ref, da_ref, keep_ref, send_ref, sums_ref, total_ref, dmt_ref,
):
    f = pl.program_id(0)
    z, width = bo_ref.shape[1], bo_ref.shape[-1]
    n, part = bo_ref.shape[0], bo_ref.shape[3]
    grad = ea_ref[0] + eb_ref[0]
    low = mid_ref[0].astype(bf16).astype(f32)
    _, scaled, inverse = norm_rows(low, 1.0, 0.0)
    back = norm_back(grad, scaled, inverse, gain_ref[...])
    dmid = (g_ref[0].astype(f32) + back).astype(bf16)
    dmid_ref[0] = dmid
    sums = jnp.concatenate(
        [
            jnp.sum(grad * scaled, 0, keepdims=True),
            jnp.sum(grad, 0, keepdims=True),
            jnp.sum(dmid.astype(f32), 0, keepdims=True),
        ],
        0,
    )

    @pl.when(f == 0)
    def _():
        sums_ref[...] = jnp.zeros_like(sums_ref)
        total_ref[...] = jnp.zeros_like(total_ref)

    sums_ref[...] += sums
    for j in range(z):
        weights = halves(bo_ref, bp_ref, j, 0)
        rows = dot(dmid[:, : D // 2], weights[0]) + dot(dmid[:, D // 2 :], weights[1])
        da_ref[0, :, j * width : (j + 1) * width] = rows.astype(bf16)
    put_transposed(dmt_ref, dmid)
    attended = pad_rows(a_ref[0], dmt_ref.shape[1])
    for j in range(z):
        lanes = slice(j * width, (j + 1) * width)
        total_ref[:, lanes] += dot(dmt_ref[...], attended[:, lanes])

    @pl.when(f == pl.num_programs(0) - 1)
    def _():
        for j in range(z):
            lanes = slice(j * width, (j + 1) * width)
            for at, ref in ((0, keep_ref), (D // 2, send_ref)):
                ref[:, j] = total_ref[at : at + D // 2, lanes].astype(bf16).reshape(n, part, width)


def between(info, ea, eb, middle, grads, attended, vec_rel, attn):
    frames = ea.shape[0]
    n, z, _, part, width = attn[2].shape
    frame = pl.BlockSpec((1, ROWS, D), lambda f, info_ref: (f, 0, 0))
    weight = once(n, z, 1, part, width, at=(0, 0, 1, 0, 0))
    return call(
        between_kernel,
        info,
        (ea, eb, middle, grads, attended, vec_rel[2:3], attn[2], attn[3]),
        (frames,),
        [frame] * 5 + [once(1, D)] + [weight] * 2,
        [frame, frame, kept(n, z, part, width), kept(n, z, part, width), kept(3, D)],
        [shaped(bf16, frames, ROWS, D)] * 2
        + [shaped(bf16, n, z, part, width)] * 2
        + [shaped(f32, 3, D)],
        "between",
        [pltpu.VMEM((D, D), f32), pltpu.VMEM((D, row_count(1)), bf16)],
        4 * frames * ROWS * D * D,
    )


def project_grads_kernel(
    info_ref, ht_ref, dq_ref, dk_ref, dv_ref, ak_ref, as_ref, bk_ref, bs_ref, sq_ref, sv_ref
):
    frames = dq_ref.shape[0]
    deep = ht_ref.shape[1]
    n, part, width = bk_ref.shape[0], bk_ref.shape[2], bk_ref.shape[3]
    for w, ref in enumerate((dq_ref, dk_ref, dv_ref)):
        rows = pad_rows(jnp.concatenate([ref[f] for f in range(frames)], 0), deep)
        for at, a_ref, b_ref in ((0, ak_ref, bk_ref), (D // 2, as_ref, bs_ref)):
            grad = dot(ht_ref[at : at + D // 2], rows).astype(bf16).reshape(n, part, width)
            if w < 2:
                a_ref[:, 0, w] = grad
            else:
                b_ref[:, 0] = grad
        if w != 1:
            (sq_ref if w == 0 else sv_ref)[...] = jnp.sum(rows.astype(f32), 0, keepdims=True)


def project_grads(info, normed_t, grads, attn):
    frames = grads[0].shape[0]
    n, z, _, part, width = attn[0].shape
    block = pl.BlockSpec((frames, ROWS, width), lambda j, info_ref: (0, 0, j))
    a_spec = pl.BlockSpec((n, 1, 2, part, width), lambda j, info_ref: (0, j, 0, 0, 0))
    b_spec = pl.BlockSpec((n, 1, part, width), lambda j, info_ref: (0, j, 0, 0))
    row = pl.BlockSpec((1, width), lambda j, info_ref: (0, j))
    return call(
        project_grads_kernel,
        info,
        (normed_t, *grads),
        (z,),
        [once(*normed_t.shape)] + [block] * 3,
        [a_spec] * 2 + [b_spec] * 2 + [row] * 2,
        [shaped(bf16, n, z, 2, part, width)] * 2
        + [shaped(bf16, n, z, part, width)] * 2
        + [shaped(f32, 1, D)] * 2,
        "project_grads",
        (),
        6 * frames * ROWS * D * D,
    )


def project_back_kernel(
    info_ref, x_ref, msg_ref, dmid_ref, gain_ref, dq_ref, dk_ref, dv_ref, ao_ref, ap_ref, bo_ref, bp_ref,
    ing_ref, dmsg_ref, sums_ref, total_ref,
):
    frames = x_ref.shape[0]
    j = pl.program_id(0)

    @pl.when(j == 0)
    def _():
        total_ref[...] = jnp.zeros_like(total_ref)

    for side, (a_ref, b_ref) in enumerate(((ao_ref, bo_ref), (ap_ref, bp_ref))):
        half = slice(side * D // 2, (side + 1) * D // 2)
        width = a_ref.shape[-1]
        weights = [a_ref[:, 0, 0], a_ref[:, 0, 1], b_ref[:, 0, 0]]
        for f in range(frames):
            rows = jnp.zeros((ROWS, D // 2), f32)
            for ref, weight in zip((dq_ref, dk_ref, dv_ref), weights):
                rows += dot(ref[f], weight.reshape(D // 2, width), NT)
            total_ref[f, :, half] += rows

    @pl.when(j == pl.num_programs(0) - 1)
    def _():
        gain_sum, shift_sum = jnp.zeros((1, D), f32), jnp.zeros((1, D), f32)
        for f in range(frames):
            rows = with_message(x_ref, msg_ref, info_ref, f)
            _, scaled, inverse = norm_rows(rows, 1.0, 0.0)
            grad = total_ref[f]
            gain_sum += jnp.sum(grad * scaled, 0, keepdims=True)
            shift_sum += jnp.sum(grad, 0, keepdims=True)
            back = norm_back(grad, scaled, inverse, gain_ref[...])
            ing_ref[f] = dmid_ref[f].astype(f32) + back
            dmsg_ref[f] = back[PATCHES : PATCHES + 1]
        sums_ref[...] = jnp.concatenate([gain_sum, shift_sum], 0)


def project_back(info, x, message, dmid, vec_rel, grads, attn):
    frames = x.shape[0]
    n, z, _, part, width = attn[0].shape
    block = pl.BlockSpec((frames, ROWS, width), lambda j, info_ref: (0, 0, j))
    a_spec = pl.BlockSpec((n, 1, 2, part, width), lambda j, info_ref: (0, j, 0, 0, 0))
    b_spec = pl.BlockSpec((n, 1, 1, part, width), lambda j, info_ref: (0, j, 0, 0, 0))
    return call(
        project_back_kernel,
        info,
        (x, message, dmid, vec_rel[0:1], *grads, *attn),
        (z,),
        [once(frames, ROWS, D), once(FRAMES, D), once(frames, ROWS, D), once(1, D)]
        + [block] * 3
        + [a_spec] * 2
        + [b_spec] * 2,
        [once(frames, ROWS, D), kept(frames, 1, D), kept(2, D)],
        [shaped(f32, frames, ROWS, D), shaped(f32, frames, 1, D), shaped(f32, 2, D)],
        "project_back",
        [pltpu.VMEM((frames, ROWS, D), f32)],
        6 * frames * ROWS * D * D,
    )


def message_times(rows, refs, i):
    own, other = rows[:, : D // 2], rows[:, D // 2 :]
    cols = []
    for own_ref, other_ref in (refs[:2], refs[2:]):
        weights = halves(own_ref, other_ref, i)
        cols.append(dot(own, weights[0]) + dot(other, weights[1]))
    return jnp.concatenate(cols, 1)


def message_times_t(rows, refs, i):
    left, right = rows[:, : D // 2], rows[:, D // 2 :]
    first, second = halves(refs[0], refs[1], i), halves(refs[2], refs[3], i)
    return jnp.concatenate(
        [dot(left, first[s], NT) + dot(right, second[s], NT) for s in range(2)], 1
    )


def by_head(rows):
    full = jnp.concatenate([rows.astype(f32)] * HEADS, 0)
    return jnp.where(head_mask(), full, 0.0).astype(bf16)


def head_mask():
    shape = (HEADS * FRAMES, D)
    head = lax.broadcasted_iota(jnp.int32, shape, 0) // FRAMES
    return head == lax.broadcasted_iota(jnp.int32, shape, 1) // HEAD


def over_heads(rows):
    rows = jnp.where(head_mask(), rows, 0.0)
    return jnp.sum(rows.reshape(HEADS, FRAMES, D), 0)


def message_probability(queries, keys):
    scores = dot(by_head(queries), keys, NT) * HEAD**-0.5
    shifted = jnp.exp(scores - jnp.max(scores, 1, keepdims=True))
    return shifted * (1.0 / jnp.sum(shifted, 1, keepdims=True))


def message_forward_kernel(info_ref, cls_ref, vec_ref, *refs):
    weights, (msg_ref, first_ref, pack_ref, hold_ref) = refs[:4], refs[4:]

    def relative(rows):
        hold_ref[...] = rows
        return permuted(hold_ref, info_ref, 0)

    first = message_times(relative(cls_ref[...]).astype(bf16), weights, 0) + vec_ref[6:7]
    normed = norm_rows(first, vec_ref[4:5], vec_ref[5:6])[0].astype(bf16).astype(f32)
    normed_rel = relative(normed).astype(bf16)
    queries = (message_times(normed_rel, weights, 1) + vec_ref[7:8]).astype(bf16)
    keys = message_times(normed_rel, weights, 2).astype(bf16)
    values = (message_times(normed_rel, weights, 3) + vec_ref[8:9]).astype(bf16)
    probability = message_probability(queries, keys).astype(bf16)
    mixed = over_heads(dot(probability, values)).astype(bf16).astype(f32)
    message = first + message_times(relative(mixed).astype(bf16), weights, 4) + vec_ref[9:10]
    msg_ref[...] = relative(message)
    first_ref[...] = first
    for i, rows in enumerate((normed, mixed, queries, keys, values)):
        pack_ref[i] = rows.astype(f32)


def message_forward(info, class_rows, vectors, weights):
    one = kept(FRAMES, D)
    return call(
        message_forward_kernel,
        info,
        (class_rows, vectors, *weights),
        (1,),
        [one, kept(*vectors.shape)] + [once(*weights[0].shape)] * 4,
        [one, one, kept(5, FRAMES, D)],
        [shaped(f32, FRAMES, D), shaped(f32, FRAMES, D), shaped(f32, 5, FRAMES, D)],
        "message_forward",
        [pltpu.VMEM((FRAMES, D), f32)],
        10 * FRAMES * D * D,
    )


def message_backward_kernel(info_ref, dmsg_ref, first_ref, pack_ref, vec_ref, *refs):
    weights, (class_ref, sent_ref, sums_ref, hold_ref) = refs[:4], refs[4:]
    frames = dmsg_ref.shape[1]
    for i in range(dmsg_ref.shape[0]):
        place = lax.bitwise_xor(info_ref[2 * BLOCKS], i)
        for f in range(frames):
            hold_ref[i * frames + f : i * frames + f + 1] = dmsg_ref[place, f : f + 1]
    dmsg = permuted(hold_ref, info_ref, BLOCKS)

    def plain(rows):
        hold_ref[...] = rows
        return permuted(hold_ref, info_ref, BLOCKS)

    queries, keys, values = (pack_ref[i].astype(bf16) for i in (2, 3, 4))
    grad_mixed = plain(message_times_t(dmsg.astype(bf16), weights, 4)).astype(bf16)
    probability = message_probability(queries, keys)
    grads_big = by_head(grad_mixed)
    grad_prob = dot(grads_big, values, NT)
    inner = jnp.sum(grad_prob * probability, 1, keepdims=True)
    grad_scores = (probability * (grad_prob - inner)).astype(bf16)
    dq = (over_heads(dot(grad_scores, keys)) * HEAD**-0.5).astype(bf16)
    dk = (dot(grad_scores, by_head(queries), TN) * HEAD**-0.5).astype(bf16)
    dv = dot(probability.astype(bf16), grads_big, TN).astype(bf16)
    grad = plain(
        message_times_t(dq, weights, 1)
        + message_times_t(dk, weights, 2)
        + message_times_t(dv, weights, 3)
    )
    _, scaled, inverse = norm_rows(first_ref[...], 1.0, 0.0)
    back = norm_back(grad, scaled, inverse, vec_ref[4:5])
    dfirst = (dmsg + back).astype(bf16)
    class_ref[...] = message_times_t(dfirst, weights, 0)
    sent = [rows.astype(f32) for rows in (dfirst, dq, dk, dv, dmsg)]
    for i, rows in enumerate(sent):
        sent_ref[i] = rows
    sums = [grad * scaled, grad, sent[0], sent[1], sent[3], dmsg]
    sums_ref[...] = jnp.concatenate([jnp.sum(rows, 0, keepdims=True) for rows in sums], 0)


def message_backward(info, dmsg, first, pack, vectors, weights):
    one = kept(FRAMES, D)
    return call(
        message_backward_kernel,
        info,
        (dmsg, first, pack, vectors, *weights),
        (1,),
        [kept(*dmsg.shape), one, kept(*pack.shape), kept(*vectors.shape)]
        + [once(*weights[0].shape)] * 4,
        [one, kept(5, FRAMES, D), kept(6, D)],
        [shaped(f32, FRAMES, D), shaped(f32, 5, FRAMES, D), shaped(f32, 6, D)],
        "message_backward",
        [pltpu.VMEM((FRAMES, D), f32)],
        10 * FRAMES * D * D,
    )


def relative_order():
    return lax.axis_size("dp") * BLOCK == D


def make_info():
    place = lax.iota(jnp.int32, BLOCKS)
    if relative_order():
        mine = lax.axis_index("dp")
        differs = place ^ mine
        places = mine ^ (2 * (place % 4) + place // 4)
        blocks = (differs % 2) * 4 + differs // 2
    else:
        places = blocks = place
    return jnp.concatenate([places, blocks, lax.axis_index("tensor")[None]]).astype(jnp.int32)


def swap(values, axis, bit):
    pairs = [(i, i ^ bit) for i in range(lax.axis_size(axis))]
    return lax.ppermute(values, axis, pairs)


def bits_of(axis):
    size = lax.axis_size(axis)
    return [1 << i for i in range(size.bit_length() - 1)]


def after(values, *earlier):
    return lax.optimization_barrier((values, earlier))[0]


def gather_chips(values, which):
    if not which:
        values = jnp.stack([values, swap(values, "dp", 2)])
        values = jnp.stack([values, swap(values, "dp", 4)])
    else:
        values = jnp.stack([values, swap(values, "dp", 4)])
        values = jnp.stack([values, swap(values, "dp", 2)], 1)
    return values.reshape((4,) + values.shape[2:])


def gather_sides(values, which):
    if relative_order():
        own = gather_chips(values, which)
        return own, swap(own, "dp", 1)
    everything = lax.all_gather(values, "dp", axis=0)
    count = everything.shape[0] // 2
    return everything[:count], everything[count:]


def gather_small(values):
    if relative_order():
        own = gather_chips(values, 0)
        return jnp.concatenate([own, swap(own, "dp", 1)], 0)
    return lax.all_gather(values, "dp", axis=0)


def add_low(left_side, right_side):
    return (left_side.astype(f32) + right_side.astype(f32)).astype(bf16)


class Scatter:
    def __init__(self, keep, send, which):
        self.which, self.place = which, 0
        self.held = keep
        if relative_order():
            self.held = keep.reshape((2, 2) + keep.shape[1:])
            self.arrived = swap(send, "dp", 1).reshape(self.held.shape)
        else:
            self.total = lax.psum_scatter(
                jnp.concatenate([keep, send], 0), "dp", scatter_dimension=0, tiled=False
            )

    def step(self):
        if not relative_order():
            return self.total
        axis, bit = ((0, 4), (0, 2))[self.place] if not self.which else ((1, 2), (0, 4))[self.place]
        take = lambda v, i: lax.index_in_dim(v, i, axis, keepdims=False)
        going = add_low(take(self.held, 1), take(self.arrived, 1))
        self.held = add_low(take(self.held, 0), take(self.arrived, 0))
        self.arrived = swap(going, "dp", bit)
        self.place += 1
        return going

    def result(self):
        if not relative_order():
            return self.total
        return add_low(self.held, self.arrived)


def scatter_videos(values, earlier=None):
    if earlier is not None:
        values = after(values, earlier)
    return lax.psum_scatter(values, "tensor", scatter_dimension=0, tiled=False)


def scatter_videos_swaps(values):
    count = values.shape[0]
    if count != 4:
        return scatter_videos(values)
    mine = lax.axis_index("tensor")
    low, high = mine % 2, mine // 2
    pairs = values.reshape((2, 2) + values.shape[1:])
    take = lambda v, i, axis: lax.dynamic_index_in_dim(v, i, axis, keepdims=False)
    going, held = take(pairs, 1 - low, 1), take(pairs, low, 1)
    held = add_low(held, swap(going, "tensor", 1))
    going, held = take(held, 1 - high, 0), take(held, high, 0)
    return add_low(held, swap(going, "tensor", 2))


def sum_everywhere(values):
    for axis in ("dp", "tensor"):
        for bit in bits_of(axis):
            values = values + swap(values, axis, bit)
    return values


def gather_videos(values):
    values = values[None]
    for bit in bits_of("tensor"):
        values = jnp.concatenate([values, swap(values, "tensor", bit)], 0)
    return values


def adam_step(weight, first_moment, second_moment, gradient, factor, step_rate, decay_rate):
    clipped = gradient * factor
    first_new = beta_one * first_moment + (1.0 - beta_one) * clipped
    second_new = beta_two * second_moment + (1.0 - beta_two) * clipped * clipped
    update = (
        first_new
        / (1.0 - beta_one**STEP)
        / (jnp.sqrt(second_new / (1.0 - beta_two**STEP)) + adam_eps)
    )
    weight_new = weight - step_rate * (update + decay_rate * weight)
    return (first_new, second_new, weight_new)


def on_device(
    tokens,
    cotangent,
    attn_master,
    attn_first,
    attn_second,
    attn_ema,
    mlp_master,
    mlp_first,
    mlp_second,
    mlp_ema,
    msg_master,
    msg_first,
    msg_second,
    msg_ema,
    vec_master,
    vec_first,
    vec_second,
    vec_ema,
):
    z_index = lax.axis_index("tensor")
    z_count = lax.axis_size("tensor")
    dp_index = lax.axis_index("dp")
    part = attn_master.shape[0]
    local_width = attn_master.shape[2]
    local_ff = mlp_master.shape[2]
    frames = tokens.shape[0] // PATCHES
    half_ff = local_ff // 2
    info = make_info()

    attn_z = lax.all_gather(jnp.swapaxes(attn_master, 0, 1).astype(bf16), "tensor", axis=0)
    mlp_z = lax.all_gather(jnp.swapaxes(mlp_master, 0, 1).astype(bf16), "tensor", axis=0)
    class_own = tokens.reshape(frames, PATCHES, D)[:, 0]
    class_rows = gather_videos(class_own)
    order = lax.iota(jnp.int32, z_count) ^ z_index
    class_rows = jnp.take(class_rows, order, axis=0, mode="clip").reshape(FRAMES, D)
    msg_low = jnp.swapaxes(msg_master, 0, 1).astype(bf16)
    msg_w = [
        side
        for i in range(2)
        for side in gather_sides(msg_low[..., i * D // 2 : (i + 1) * D // 2], i)
    ]
    vec_rel = jnp.moveaxis(gather_small(vec_master.astype(bf16).T), 0, 1)
    vec_rel = vec_rel.reshape(-1, D).astype(f32)
    vectors = plain_order(info, vec_rel)
    ff_bias = vectors[14:].reshape(z_count, 2, half_ff)
    attn_w = [side for i in range(2) for side in gather_sides(attn_z[:, 2 * i : 2 * i + 2], i)]
    mlp_w = [
        [
            side
            for i in range(2)
            for side in gather_sides(mlp_z[:, i, :, j * half_ff : (j + 1) * half_ff], i)
        ]
        for j in range(2)
    ]

    x, grads, grads_t, grad_sum = prepare(info, tokens, cotangent)
    message, first_msg, msg_pack = message_forward(
        info, class_rows.astype(f32), vectors, msg_w
    )
    queries, key_rows, value_rows, normed_t = project(info, x, message, vec_rel, vectors, attn_w)
    attended, totals = attend_forward(queries, key_rows, value_rows)
    middle, n2, n2_t = combine(info, x, attended, vec_rel, attn_w)

    def feed(j):
        return feed_forward(n2, n2_t, grads, grads_t, ff_bias[:, j], mlp_w[j])

    def two(grads_of):
        return [Scatter(grads_of[2 * i], grads_of[2 * i + 1], i) for i in range(2)]

    out_0, dn2_0, *dw_0, db_0 = feed(0)
    sums_0 = two(dw_0)
    out_1, dn2_1, *dw_1, db_1 = feed(1)
    sums_1 = two(dw_1)
    going = [s.step() for s in sums_0]
    dmid, grad_attended, *grad_out_w, sums_two = between(
        info, after(dn2_0, *going), dn2_1, middle, grads, attended, vec_rel, attn_w
    )
    going = [s.step() for s in sums_1]
    pairs = HEADS // 2
    back = (queries, key_rows, value_rows, totals)
    grad_qkv = attend_backward(*back, after(grad_attended, *going), 0, pairs // 2)
    going = [s.step() for s in sums_0]
    grad_qkv = attend_backward(
        *back, after(grad_attended, *going), pairs // 2, pairs - pairs // 2, grad_qkv
    )
    mlp_0 = scatter_videos(jnp.stack([s.result() for s in sums_0], 1))
    going = [s.step() for s in sums_1]
    dqk_keep, dqk_send, dv_keep, dv_send, sum_q, sum_v = project_grads(
        info, after(normed_t, *going), grad_qkv, attn_w
    )
    sums_attn = [
        Scatter(dqk_keep, dqk_send, 0),
        Scatter(
            jnp.stack([dv_keep, grad_out_w[0]], 2), jnp.stack([dv_send, grad_out_w[1]], 2), 1
        ),
    ]
    mlp_1 = jnp.stack([s.result() for s in sums_1], 1)
    mlp_1 = scatter_videos(mlp_1, mlp_0)
    going = [s.step() for s in sums_attn]
    ing, dmsg, sums_one = project_back(
        info, after(x, *going), message, dmid, vec_rel, grad_qkv, attn_w
    )
    dmsg = gather_videos(dmsg[:, 0].astype(bf16)).astype(f32)
    going = [s.step() for s in sums_attn]
    grad_class, sent, sums_msg = message_backward(
        info, after(dmsg, *going), first_msg, msg_pack, vectors, msg_w
    )
    input_grad = finish(info, [ing], grad_class, "input_grad")
    block_output = finish(info, [middle, out_0, out_1], vec_rel[13:14], "block_output")
    attn_sum = jnp.concatenate([s.result() for s in sums_attn], 1)
    attn_grad = scatter_videos_swaps(attn_sum)

    sent = jnp.concatenate([class_rows[None], msg_pack[:2].astype(bf16), sent.astype(bf16)], 0)
    everyone = jnp.moveaxis(gather_small(sent), 0, 1).reshape(8, -1, D)
    mine = lax.dynamic_slice_in_dim(everyone[:3], dp_index * part, part, 2)
    msg_grad = jnp.stack(
        [
            dot(mine[0], everyone[3], TN),
            dot(mine[1], everyone[4], TN),
            dot(mine[1], everyone[5], TN),
            dot(mine[1], everyone[6], TN),
            dot(mine[2], everyone[7], TN),
        ],
        1,
    )

    relative = plain_order(info, jnp.concatenate([sums_one, sums_two, grad_sum], 0))
    ff_bias_grad = jnp.stack(
        [db.reshape(z_count, half_ff) for db in (db_0, db_1)], 1
    ).reshape(FF // D, D)
    sums_msg = jnp.where(z_index == 0, sums_msg, 0.0)
    table = sum_everywhere(
        jnp.concatenate([relative[:4], sums_msg, sum_q, sum_v, relative[4:], ff_bias_grad], 0)
    )
    vec_grad = lax.dynamic_slice_in_dim(table, dp_index * part, part, 1).T

    attn_grad = jnp.swapaxes(attn_grad, 0, 1).astype(f32)
    mlp_grad = jnp.swapaxes(jnp.concatenate([mlp_0, mlp_1], 2), 0, 1).astype(f32)

    keep_share = (z_index == 0).astype(f32)
    squares = (
        jnp.sum(attn_grad * attn_grad)
        + jnp.sum(mlp_grad * mlp_grad)
        + keep_share * (jnp.sum(msg_grad * msg_grad) + jnp.sum(vec_grad * vec_grad))
    )
    squares = sum_everywhere(jnp.broadcast_to(squares, (8, 128)))[0, 0]
    grad_norm = jnp.sqrt(squares)
    factor = clip_limit / jnp.maximum(grad_norm, clip_limit)

    def update(master, first, second, ema, grad, rate, decay):
        first_new, second_new, weight = adam_step(master, first, second, grad, factor, rate, decay)
        return grad, first_new, second_new, weight, ema_keep * ema + (1.0 - ema_keep) * weight

    return (
        block_output,
        input_grad,
        grad_norm,
        *update(attn_master, attn_first, attn_second, attn_ema, attn_grad, rate_mat, decay_mat),
        *update(mlp_master, mlp_first, mlp_second, mlp_ema, mlp_grad, rate_mat, decay_mat),
        *update(msg_master, msg_first, msg_second, msg_ema, msg_grad, rate_mat, decay_mat),
        *update(vec_master, vec_first, vec_second, vec_ema, vec_grad, rate_vec, 0.0),
    )


def solution(mesh):
    rows = P(("dp", "tensor"), None)
    split = P("dp", None, "tensor")
    copied = P("dp", None, None)
    table = P("dp", None)
    in_specs = (rows,) * 2 + (split,) * 8 + (copied,) * 4 + (table,) * 4
    out_specs = (rows,) * 2 + (P(),) + (split,) * 10 + (copied,) * 5 + (table,) * 5
    return jax.shard_map(
        on_device, mesh=mesh, in_specs=in_specs, out_specs=out_specs, check_vma=False
    )
```

```python
import jax
import jax.numpy as jnp
from jax import lax
from jax.experimental import pallas as pl
from jax.experimental.pallas import tpu as pltpu
from jax.sharding import PartitionSpec as P

D = 1024
HEADS = 16
HEAD = 64
FF = 4096
PATCHES = 577
FRAMES = 8
STEP = 10
ROWS = 592


norm_eps = 1e-05
beta_one = 0.9
beta_two = 0.95
adam_eps = 1e-08
decay_mat = 0.05
ema_keep = 0.7
clip_limit = 1.0
rate_mat = 0.02
rate_vec = 0.4
far_below = -1e30
COST_PART = 16
bf16 = jnp.bfloat16
f32 = jnp.float32
NN = (((1,), (0,)), ((), ()))
NT = (((1,), (1,)), ((), ()))
TN = (((0,), (0,)), ((), ()))


def dot(left_side, right_side, dims=NN):
    return lax.dot_general(left_side, right_side, dims, preferred_element_type=f32)


def norm_rows(values, gain_row, shift_row):
    centre = values - jnp.mean(values, -1, keepdims=True)
    spread = jnp.mean(centre * centre, -1, keepdims=True)
    inverse = lax.rsqrt(spread + norm_eps)
    scaled = centre * inverse
    return (scaled * gain_row + shift_row, scaled, inverse)


def norm_back(gradient, scaled, inverse, gain_row):
    inner = gradient * gain_row
    return inverse * (
        inner
        - jnp.mean(inner, -1, keepdims=True)
        - scaled * jnp.mean(inner * scaled, -1, keepdims=True)
    )


def pad_rows(values, count):
    if values.shape[0] == count:
        return values
    extra = jnp.zeros((count - values.shape[0],) + values.shape[1:], values.dtype)
    return jnp.concatenate([values, extra], 0)


def head_pair(queries, key_rows, head):
    lane = lax.broadcasted_iota(jnp.int32, queries.shape, 1)
    key_lane = lax.broadcasted_iota(jnp.int32, key_rows.shape, 1)
    key_row = lax.broadcasted_iota(jnp.int32, key_rows.shape, 0)
    spare = HEAD * (1 - head)
    mask = jnp.where(
        (key_lane == spare) & (key_row > PATCHES), jnp.asarray(far_below, bf16), jnp.asarray(0, bf16)
    )
    keys_one = jnp.where((key_lane // HEAD) == head, key_rows, mask)
    queries_one = jnp.where(lane == spare, jnp.asarray(1, bf16), queries)
    return queries_one, keys_one


def attend_forward_kernel(q_ref, k_ref, v_ref, out_ref, total_ref):
    rows = q_ref.shape[1]
    key_count = -(-rows // 128) * 128
    queries = q_ref[0] * jnp.asarray(HEAD**-0.5, bf16)
    key_rows = pad_rows(k_ref[0], key_count)
    value_rows = pad_rows(v_ref[0], key_count)
    lane = lax.broadcasted_iota(jnp.int32, (rows, 128), 1)
    outs, totals = [], []
    for head in range(2):
        queries_one, keys_one = head_pair(queries, key_rows, head)
        scores = dot(queries_one, keys_one, NT)
        highest = jnp.max(scores, 1, keepdims=True)
        shifted = jnp.exp(scores - highest)
        total = jnp.sum(shifted, 1, keepdims=True)
        probability = (shifted * (1.0 / total)).astype(bf16)
        outs.append(dot(probability, value_rows))
        totals.append(highest + jnp.log(total))
    out_ref[0] = jnp.where(lane < HEAD, outs[0], outs[1]).astype(bf16)
    both = jnp.where(lane < HEAD, totals[0], totals[1]).T
    total_ref[0, 0] = jnp.concatenate([both[0:1], both[HEAD : HEAD + 1]], 0)


def attend_backward_kernel(q_ref, k_ref, v_ref, total_ref, grad_ref, *rest):
    dq_ref, dk_ref, dv_ref = rest[-3:]
    rows = q_ref.shape[1]
    query_count = -(-rows // 128) * 128
    queries = pad_rows(q_ref[0], query_count) * jnp.asarray(HEAD**-0.5, bf16)
    grads = pad_rows(grad_ref[0], query_count)
    key_rows = k_ref[0]
    value_rows = v_ref[0]
    keys_t = pad_rows(key_rows, query_count).astype(f32).T.astype(bf16)
    lane = lax.broadcasted_iota(jnp.int32, (rows, 128), 1)
    grad_q, grad_k, grad_v = [], [], []
    for head in range(2):
        queries_one, keys_one = head_pair(queries, key_rows, head)
        total = total_ref[0, 0, head : head + 1, :]
        if query_count > rows:
            total = jnp.concatenate([total, jnp.zeros((1, query_count - rows), f32)], 1)
        probability = jnp.exp(dot(keys_one, queries_one, NT) - total)
        values_one = jnp.where((lane // HEAD) == head, value_rows, jnp.asarray(0, bf16))
        grad_prob = dot(values_one, grads, NT)
        inner = jnp.sum(grad_prob * probability, 0, keepdims=True)
        grad_scores = (probability * (grad_prob - inner)).astype(bf16)
        grad_v.append(dot(probability.astype(bf16), grads))
        grad_k.append(dot(grad_scores, queries))
        grad_q.append(dot(keys_t[HEAD * head : HEAD * (head + 1)], pad_rows(grad_scores, query_count)))
    grad_q = jnp.concatenate(grad_q, 0) * HEAD**-0.5
    dq_ref[0] = grad_q.T[:rows].astype(bf16)
    dk_ref[0] = jnp.where(lane < HEAD, grad_k[0], grad_k[1]).astype(bf16)
    dv_ref[0] = jnp.where(lane < HEAD, grad_v[0], grad_v[1]).astype(bf16)


def cost(flops, moved):
    return pl.CostEstimate(
        flops=flops // COST_PART, bytes_accessed=moved // COST_PART, transcendentals=0
    )


def attend_cost(frames, rows, width, matmuls):
    return cost(2 * matmuls * frames * rows * rows * width, 4 * matmuls * frames * rows * width)


def attend_forward(queries, key_rows, value_rows):
    frames, rows, width = queries.shape
    spec = pl.BlockSpec((1, rows, 128), lambda f, h: (f, 0, h))
    return pl.pallas_call(
        attend_forward_kernel,
        grid=(frames, width // 128),
        in_specs=[spec] * 3,
        out_specs=[spec, pl.BlockSpec((1, 1, 2, rows), lambda f, h: (f, h, 0, 0))],
        out_shape=[
            jax.ShapeDtypeStruct((frames, rows, width), bf16),
            jax.ShapeDtypeStruct((frames, width // 128, 2, rows), f32),
        ],
        compiler_params=pltpu.CompilerParams(vmem_limit_bytes=48 << 20),
        cost_estimate=attend_cost(frames, rows, width, 4),
        name="attend_forward",
    )(queries, key_rows, value_rows)


def attend_backward(queries, key_rows, value_rows, totals, grads, begin, count, earlier=()):
    frames, rows, width = queries.shape
    spec = pl.BlockSpec((1, rows, 128), lambda f, h: (f, 0, h + begin))
    total_spec = pl.BlockSpec((1, 1, 2, rows), lambda f, h: (f, h + begin, 0, 0))
    return pl.pallas_call(
        attend_backward_kernel,
        grid=(frames, count),
        in_specs=[spec] * 3 + [total_spec, spec] + [pl.BlockSpec(memory_space=pl.ANY)] * len(earlier),
        out_specs=[spec] * 3,
        out_shape=[jax.ShapeDtypeStruct((frames, rows, width), bf16)] * 3,
        input_output_aliases={5 + i: i for i in range(len(earlier))},
        compiler_params=pltpu.CompilerParams(vmem_limit_bytes=48 << 20),
        cost_estimate=attend_cost(frames, rows, count * 128, 8),
        name="attend_backward",
    )(queries, key_rows, value_rows, totals, grads, *earlier)


def feed_kernel(
    n2_ref,
    n2t_ref,
    g_ref,
    gt_ref,
    bias_ref,
    up_own_ref,
    up_other_ref,
    down_own_ref,
    down_other_ref,
    out_ref,
    dn2_ref,
    dup_own_ref,
    dup_other_ref,
    ddown_own_ref,
    ddown_other_ref,
    db_ref,
    act_ref,
    dpre_ref,
):
    frames, rows = n2_ref.shape[:2]
    blocks, _, part, chunk = up_own_ref.shape
    half = blocks * part

    @pl.when(pl.program_id(0) == 0)
    def _():
        out_ref[...] = jnp.zeros_like(out_ref)
        dn2_ref[...] = jnp.zeros_like(dn2_ref)
        act_ref[...] = jnp.zeros_like(act_ref)
        dpre_ref[...] = jnp.zeros_like(dpre_ref)

    def whole(own_ref, other_ref):
        return jnp.concatenate(
            [own_ref[:, 0].reshape(half, chunk), other_ref[:, 0].reshape(half, chunk)], 0
        )

    first = whole(up_own_ref, up_other_ref)
    second = whole(down_own_ref, down_other_ref)
    bias_sum = jnp.zeros((1, chunk), f32)
    for frame in range(frames):
        place = pl.ds(frame * rows, rows)
        pre = dot(n2_ref[frame], first) + bias_ref[0]
        sigma = 1.0 / (1.0 + jnp.exp(-1.702 * pre))
        act = (pre * sigma).astype(bf16)
        act_ref[place] = act
        out_ref[frame] += dot(act, second, NT)
        grad_act = dot(g_ref[frame], second)
        grad_pre = grad_act * (sigma + 1.702 * pre * sigma * (1.0 - sigma))
        grad_low = grad_pre.astype(bf16)
        dpre_ref[place] = grad_low
        bias_sum += jnp.sum(grad_low.astype(f32), 0, keepdims=True)
        dn2_ref[frame] += dot(grad_low, first, NT)
    db_ref[0] = bias_sum

    def place_grad(left_ref, right_ref, own_ref, other_ref):
        for at, ref in ((0, own_ref), (half, other_ref)):
            grad = dot(left_ref[at : at + half], right_ref[...]).astype(bf16)
            ref[:, 0] = grad.reshape(blocks, part, chunk)

    place_grad(n2t_ref, dpre_ref, dup_own_ref, dup_other_ref)
    place_grad(gt_ref, act_ref, ddown_own_ref, ddown_other_ref)


def feed_forward(n2, n2t, grads, grads_t, bias, weights):
    frames, rows, _ = n2.shape
    blocks, ff_blocks, part, local = weights[0].shape
    chunk = min(512, local)
    per = local // chunk
    steps = ff_blocks * per
    deep = n2t.shape[1]
    whole3 = lambda n: (0, 0, 0)
    whole2 = lambda n: (0, 0)
    single = pl.Buffered(1)
    w_spec = pl.BlockSpec((blocks, 1, part, chunk), lambda n: (0, n // per, 0, n % per))
    return pl.pallas_call(
        feed_kernel,
        grid=(steps,),
        in_specs=[
            pl.BlockSpec((frames, rows, D), whole3, pipeline_mode=single),
            pl.BlockSpec((D, deep), whole2, pipeline_mode=single),
            pl.BlockSpec((frames, rows, D), whole3, pipeline_mode=single),
            pl.BlockSpec((D, deep), whole2, pipeline_mode=single),
            pl.BlockSpec((1, 1, chunk), lambda n: (n, 0, 0)),
        ]
        + [w_spec] * 4,
        out_specs=[pl.BlockSpec((frames, rows, D), whole3)] * 2
        + [w_spec] * 4
        + [pl.BlockSpec((1, 1, chunk), lambda n: (n, 0, 0))],
        out_shape=[jax.ShapeDtypeStruct((frames, rows, D), f32)] * 2
        + [jax.ShapeDtypeStruct(weights[0].shape, bf16)] * 4
        + [jax.ShapeDtypeStruct((steps, 1, chunk), f32)],
        scratch_shapes=[pltpu.VMEM((deep, chunk), bf16), pltpu.VMEM((deep, chunk), bf16)],
        compiler_params=pltpu.CompilerParams(vmem_limit_bytes=60 << 20),
        cost_estimate=cost(
            12 * frames * rows * D * ff_blocks * local,
            8 * D * ff_blocks * local + 16 * frames * rows * D,
        ),
        name="feed_forward",
    )(n2, n2t, grads, grads_t, bias.reshape(steps, 1, chunk), *weights)


BLOCK = 128
BLOCKS = D // BLOCK


def permuted(ref, info_ref, first):
    return jnp.concatenate(
        [
            ref[:, pl.ds(pl.multiple_of(info_ref[first + i] * BLOCK, BLOCK), BLOCK)]
            for i in range(BLOCKS)
        ],
        1,
    )


def call(kernel, info, args, grid, in_specs, out_specs, out_shape, name, scratch=(), flops=0, vmem=56):
    moved = sum(a.size * a.dtype.itemsize for a in args)
    moved += sum(o.size * o.dtype.itemsize for o in out_shape)
    return pl.pallas_call(
        kernel,
        grid_spec=pltpu.PrefetchScalarGridSpec(
            num_scalar_prefetch=1,
            grid=grid,
            in_specs=in_specs,
            out_specs=out_specs,
            scratch_shapes=list(scratch),
        ),
        out_shape=out_shape,
        compiler_params=pltpu.CompilerParams(vmem_limit_bytes=vmem << 20),
        cost_estimate=cost(flops, moved),
        name=name,
    )(info, *args)


def shaped(dtype, *shape):
    return jax.ShapeDtypeStruct(shape, dtype)


def once(*block, at=None):
    index = at or (0,) * len(block)
    return pl.BlockSpec(block, lambda *_: index, pipeline_mode=pl.Buffered(1))


def kept(*block):
    index = (0,) * len(block)
    return pl.BlockSpec(block, lambda *_: index)


def row_count(frames):
    return -(-frames * ROWS // 128) * 128


def prepare_kernel(info_ref, tokens_ref, cot_ref, x_ref, g_ref, gt_ref, gsum_ref, hold_ref):
    frames = x_ref.shape[0]
    count = tokens_ref.shape[0]
    inside = lax.broadcasted_iota(jnp.int32, (ROWS, BLOCK), 0) < PATCHES
    hold_ref[...] = jnp.zeros_like(hold_ref)

    def padded(ref):
        hold_ref[0:count] = ref[...].astype(f32)
        return [
            jnp.where(inside, hold_ref[pl.ds(f * PATCHES, ROWS)], 0.0) for f in range(frames)
        ]

    for f, rows in enumerate(padded(tokens_ref)):
        x_ref[f] = rows.astype(bf16)
    grads = padded(cot_ref)
    for f, rows in enumerate(grads):
        g_ref[f] = rows.astype(bf16)
    full = pad_rows(jnp.concatenate(grads, 0), gt_ref.shape[1])
    gt_ref[...] = full.T.astype(bf16)
    gsum_ref[...] = jnp.sum(full, 0, keepdims=True)


def prepare(info, tokens, cotangent):
    count = tokens.shape[0]
    frames = count // PATCHES
    deep = row_count(frames)
    taken = pl.BlockSpec((count, BLOCK), lambda r, info_ref: (0, info_ref[r]))
    placed = pl.BlockSpec((frames, ROWS, BLOCK), lambda r, info_ref: (0, 0, r))
    return call(
        prepare_kernel,
        info,
        (tokens, cotangent),
        (BLOCKS,),
        [taken] * 2,
        [
            placed,
            placed,
            pl.BlockSpec((BLOCK, deep), lambda r, info_ref: (r, 0)),
            pl.BlockSpec((1, BLOCK), lambda r, info_ref: (0, r)),
        ],
        [
            shaped(bf16, frames, ROWS, D),
            shaped(bf16, frames, ROWS, D),
            shaped(bf16, D, deep),
            shaped(f32, 1, D),
        ],
        "prepare",
        [pltpu.VMEM((-(-((frames - 1) * PATCHES + ROWS) // 8) * 8, BLOCK), f32)],
    )


def plain_order_kernel(info_ref, in_ref, out_ref):
    out_ref[...] = permuted(in_ref, info_ref, BLOCKS)


def plain_order(info, values):
    return call(
        plain_order_kernel,
        info,
        (values,),
        (1,),
        [kept(*values.shape)],
        [kept(*values.shape)],
        [shaped(f32, *values.shape)],
        "plain_order",
    )[0]


def finish_kernel(info_ref, *refs):
    *in_refs, row_ref, out_ref = refs
    frames = in_refs[0].shape[0]
    for f in range(frames):
        rows = in_refs[0][f]
        for ref in in_refs[1:]:
            rows = rows + ref[f]
        if row_ref.shape[0] == 1:
            rows = rows + row_ref[...]
        else:
            class_row = row_ref[pl.ds(info_ref[2 * BLOCKS] * frames + f, 1)]
            first = lax.broadcasted_iota(jnp.int32, (ROWS, BLOCK), 0) == 0
            rows = rows + jnp.where(first, class_row, 0.0)
        out_ref[pl.ds(f * PATCHES, PATCHES)] = rows[:PATCHES]


def finish(info, parts, row, name):
    frames = parts[0].shape[0]
    taken = pl.BlockSpec((frames, ROWS, BLOCK), lambda d, info_ref: (0, 0, info_ref[BLOCKS + d]))
    row_spec = pl.BlockSpec((row.shape[0], BLOCK), lambda d, info_ref: (0, info_ref[BLOCKS + d]))
    return call(
        finish_kernel,
        info,
        (*parts, row),
        (BLOCKS,),
        [taken] * len(parts) + [row_spec],
        [pl.BlockSpec((frames * PATCHES, BLOCK), lambda d, info_ref: (0, d))],
        [shaped(f32, frames * PATCHES, D)],
        name,
    )[0]


def with_message(x_ref, msg_ref, info_ref, f):
    frames = x_ref.shape[0]
    message = msg_ref[pl.ds(info_ref[2 * BLOCKS] * frames + f, 1)]
    place = lax.broadcasted_iota(jnp.int32, (ROWS, D), 0) == PATCHES
    return jnp.where(place, message, x_ref[f].astype(f32))


def put_transposed(ref, rows):
    for c in range(BLOCKS):
        block = pad_rows(rows[:, c * BLOCK : (c + 1) * BLOCK].astype(f32), ref.shape[1])
        ref[c * BLOCK : (c + 1) * BLOCK] = block.T.astype(bf16)


def halves(own_ref, other_ref, *at):
    return [ref[(slice(None), *at)].reshape(D // 2, ref.shape[-1]) for ref in (own_ref, other_ref)]


def project_kernel(
    info_ref, x_ref, msg_ref, gain_ref, shift_ref, bq_ref, bv_ref, ao_ref, ap_ref, bo_ref, bp_ref,
    q_ref, k_ref, v_ref, ht_ref, h_ref,
):
    frames = x_ref.shape[0]

    @pl.when(pl.program_id(0) == 0)
    def _():
        for f in range(frames):
            rows = with_message(x_ref, msg_ref, info_ref, f)
            normed = norm_rows(rows, gain_ref[...], shift_ref[...])[0]
            h_ref[pl.ds(f * ROWS, ROWS)] = normed.astype(bf16)
        put_transposed(ht_ref, h_ref[...])

    sides = (slice(0, D // 2), slice(D // 2, D))
    for out_ref, weights, bias in (
        (q_ref, halves(ao_ref, ap_ref, 0, 0), bq_ref[...]),
        (k_ref, halves(ao_ref, ap_ref, 0, 1), 0.0),
        (v_ref, halves(bo_ref, bp_ref, 0, 0), bv_ref[...]),
    ):
        for f in range(frames):
            place = pl.ds(f * ROWS, ROWS)
            rows = dot(h_ref[place, sides[0]], weights[0]) + dot(h_ref[place, sides[1]], weights[1])
            out_ref[f] = (rows + bias).astype(bf16)


def project(info, x, message, vec_rel, vectors, attn):
    frames = x.shape[0]
    n, z, _, part, width = attn[0].shape
    deep = row_count(frames)
    bias = pl.BlockSpec((1, width), lambda j, info_ref: (0, j))
    a_spec = pl.BlockSpec((n, 1, 2, part, width), lambda j, info_ref: (0, j, 0, 0, 0))
    b_spec = pl.BlockSpec((n, 1, 1, part, width), lambda j, info_ref: (0, j, 0, 0, 0))
    out = pl.BlockSpec((frames, ROWS, width), lambda j, info_ref: (0, 0, j))
    return call(
        project_kernel,
        info,
        (x, message, vec_rel[0:1], vec_rel[1:2], vectors[10:11], vectors[11:12], *attn),
        (z,),
        [once(frames, ROWS, D), once(FRAMES, D), once(1, D), once(1, D), bias, bias]
        + [a_spec] * 2
        + [b_spec] * 2,
        [out] * 3 + [kept(D, deep)],
        [shaped(bf16, frames, ROWS, D)] * 3 + [shaped(bf16, D, deep)],
        "project",
        [pltpu.VMEM((frames * ROWS, D), bf16)],
        6 * frames * ROWS * D * D,
    )


def combine_kernel(
    info_ref, x_ref, a_ref, bias_ref, gain_ref, shift_ref, bo_ref, bp_ref, mid_ref, n2_ref, n2t_ref, hold_ref
):
    frames = x_ref.shape[0]
    z, width = bo_ref.shape[1], bo_ref.shape[-1]
    for f in range(frames):
        for side, ref in enumerate((bo_ref, bp_ref)):
            half = slice(side * D // 2, (side + 1) * D // 2)
            total = x_ref[f, :, half].astype(f32) + bias_ref[:, half]
            for j in range(z):
                weight = ref[:, j, 0].reshape(D // 2, width)
                total += dot(a_ref[f, :, j * width : (j + 1) * width], weight, NT)
            mid_ref[f, :, half] = total
        low = mid_ref[f].astype(bf16).astype(f32)
        normed = norm_rows(low, gain_ref[...], shift_ref[...])[0].astype(bf16)
        n2_ref[f] = normed
        hold_ref[pl.ds(f * ROWS, ROWS)] = normed
    put_transposed(n2t_ref, hold_ref[...])


def combine(info, x, attended, vec_rel, attn):
    frames = x.shape[0]
    n, z, _, part, width = attn[2].shape
    deep = row_count(frames)
    weight = once(n, z, 1, part, width, at=(0, 0, 1, 0, 0))
    return call(
        combine_kernel,
        info,
        (x, attended, vec_rel[12:13], vec_rel[2:3], vec_rel[3:4], attn[2], attn[3]),
        (1,),
        [once(frames, ROWS, D)] * 2 + [once(1, D)] * 3 + [weight] * 2,
        [once(frames, ROWS, D), once(frames, ROWS, D), once(D, deep)],
        [shaped(f32, frames, ROWS, D), shaped(bf16, frames, ROWS, D), shaped(bf16, D, deep)],
        "combine",
        [pltpu.VMEM((frames * ROWS, D), bf16)],
        2 * frames * ROWS * D * D,
    )


def between_kernel(
    info_ref, ea_ref, eb_ref, mid_ref, g_ref, a_ref, gain_ref, bo_ref, bp_ref,
    dmid_ref, da_ref, keep_ref, send_ref, sums_ref, total_ref, dmt_ref,
):
    f = pl.program_id(0)
    z, width = bo_ref.shape[1], bo_ref.shape[-1]
    n, part = bo_ref.shape[0], bo_ref.shape[3]
    grad = ea_ref[0] + eb_ref[0]
    low = mid_ref[0].astype(bf16).astype(f32)
    _, scaled, inverse = norm_rows(low, 1.0, 0.0)
    back = norm_back(grad, scaled, inverse, gain_ref[...])
    dmid = (g_ref[0].astype(f32) + back).astype(bf16)
    dmid_ref[0] = dmid
    sums = jnp.concatenate(
        [
            jnp.sum(grad * scaled, 0, keepdims=True),
            jnp.sum(grad, 0, keepdims=True),
            jnp.sum(dmid.astype(f32), 0, keepdims=True),
        ],
        0,
    )

    @pl.when(f == 0)
    def _():
        sums_ref[...] = jnp.zeros_like(sums_ref)
        total_ref[...] = jnp.zeros_like(total_ref)

    sums_ref[...] += sums
    for j in range(z):
        weights = halves(bo_ref, bp_ref, j, 0)
        rows = dot(dmid[:, : D // 2], weights[0]) + dot(dmid[:, D // 2 :], weights[1])
        da_ref[0, :, j * width : (j + 1) * width] = rows.astype(bf16)
    put_transposed(dmt_ref, dmid)
    attended = pad_rows(a_ref[0], dmt_ref.shape[1])
    for j in range(z):
        lanes = slice(j * width, (j + 1) * width)
        total_ref[:, lanes] += dot(dmt_ref[...], attended[:, lanes])

    @pl.when(f == pl.num_programs(0) - 1)
    def _():
        for j in range(z):
            lanes = slice(j * width, (j + 1) * width)
            for at, ref in ((0, keep_ref), (D // 2, send_ref)):
                ref[:, j] = total_ref[at : at + D // 2, lanes].astype(bf16).reshape(n, part, width)


def between(info, ea, eb, middle, grads, attended, vec_rel, attn):
    frames = ea.shape[0]
    n, z, _, part, width = attn[2].shape
    frame = pl.BlockSpec((1, ROWS, D), lambda f, info_ref: (f, 0, 0))
    weight = once(n, z, 1, part, width, at=(0, 0, 1, 0, 0))
    return call(
        between_kernel,
        info,
        (ea, eb, middle, grads, attended, vec_rel[2:3], attn[2], attn[3]),
        (frames,),
        [frame] * 5 + [once(1, D)] + [weight] * 2,
        [frame, frame, kept(n, z, part, width), kept(n, z, part, width), kept(3, D)],
        [shaped(bf16, frames, ROWS, D)] * 2
        + [shaped(bf16, n, z, part, width)] * 2
        + [shaped(f32, 3, D)],
        "between",
        [pltpu.VMEM((D, D), f32), pltpu.VMEM((D, row_count(1)), bf16)],
        4 * frames * ROWS * D * D,
    )


def project_grads_kernel(
    info_ref, ht_ref, dq_ref, dk_ref, dv_ref, ak_ref, as_ref, bk_ref, bs_ref, sq_ref, sv_ref
):
    frames = dq_ref.shape[0]
    deep = ht_ref.shape[1]
    n, part, width = bk_ref.shape[0], bk_ref.shape[2], bk_ref.shape[3]
    for w, ref in enumerate((dq_ref, dk_ref, dv_ref)):
        rows = pad_rows(jnp.concatenate([ref[f] for f in range(frames)], 0), deep)
        for at, a_ref, b_ref in ((0, ak_ref, bk_ref), (D // 2, as_ref, bs_ref)):
            grad = dot(ht_ref[at : at + D // 2], rows).astype(bf16).reshape(n, part, width)
            if w < 2:
                a_ref[:, 0, w] = grad
            else:
                b_ref[:, 0] = grad
        if w != 1:
            (sq_ref if w == 0 else sv_ref)[...] = jnp.sum(rows.astype(f32), 0, keepdims=True)


def project_grads(info, normed_t, grads, attn):
    frames = grads[0].shape[0]
    n, z, _, part, width = attn[0].shape
    block = pl.BlockSpec((frames, ROWS, width), lambda j, info_ref: (0, 0, j))
    a_spec = pl.BlockSpec((n, 1, 2, part, width), lambda j, info_ref: (0, j, 0, 0, 0))
    b_spec = pl.BlockSpec((n, 1, part, width), lambda j, info_ref: (0, j, 0, 0))
    row = pl.BlockSpec((1, width), lambda j, info_ref: (0, j))
    return call(
        project_grads_kernel,
        info,
        (normed_t, *grads),
        (z,),
        [once(*normed_t.shape)] + [block] * 3,
        [a_spec] * 2 + [b_spec] * 2 + [row] * 2,
        [shaped(bf16, n, z, 2, part, width)] * 2
        + [shaped(bf16, n, z, part, width)] * 2
        + [shaped(f32, 1, D)] * 2,
        "project_grads",
        (),
        6 * frames * ROWS * D * D,
    )


def project_back_kernel(
    info_ref, x_ref, msg_ref, dmid_ref, gain_ref, dq_ref, dk_ref, dv_ref, ao_ref, ap_ref, bo_ref, bp_ref,
    ing_ref, dmsg_ref, sums_ref, total_ref,
):
    frames = x_ref.shape[0]
    j = pl.program_id(0)

    @pl.when(j == 0)
    def _():
        total_ref[...] = jnp.zeros_like(total_ref)

    for side, (a_ref, b_ref) in enumerate(((ao_ref, bo_ref), (ap_ref, bp_ref))):
        half = slice(side * D // 2, (side + 1) * D // 2)
        width = a_ref.shape[-1]
        weights = [a_ref[:, 0, 0], a_ref[:, 0, 1], b_ref[:, 0, 0]]
        for f in range(frames):
            rows = jnp.zeros((ROWS, D // 2), f32)
            for ref, weight in zip((dq_ref, dk_ref, dv_ref), weights):
                rows += dot(ref[f], weight.reshape(D // 2, width), NT)
            total_ref[f, :, half] += rows

    @pl.when(j == pl.num_programs(0) - 1)
    def _():
        gain_sum, shift_sum = jnp.zeros((1, D), f32), jnp.zeros((1, D), f32)
        for f in range(frames):
            rows = with_message(x_ref, msg_ref, info_ref, f)
            _, scaled, inverse = norm_rows(rows, 1.0, 0.0)
            grad = total_ref[f]
            gain_sum += jnp.sum(grad * scaled, 0, keepdims=True)
            shift_sum += jnp.sum(grad, 0, keepdims=True)
            back = norm_back(grad, scaled, inverse, gain_ref[...])
            ing_ref[f] = dmid_ref[f].astype(f32) + back
            dmsg_ref[f] = back[PATCHES : PATCHES + 1]
        sums_ref[...] = jnp.concatenate([gain_sum, shift_sum], 0)


def project_back(info, x, message, dmid, vec_rel, grads, attn):
    frames = x.shape[0]
    n, z, _, part, width = attn[0].shape
    block = pl.BlockSpec((frames, ROWS, width), lambda j, info_ref: (0, 0, j))
    a_spec = pl.BlockSpec((n, 1, 2, part, width), lambda j, info_ref: (0, j, 0, 0, 0))
    b_spec = pl.BlockSpec((n, 1, 1, part, width), lambda j, info_ref: (0, j, 0, 0, 0))
    return call(
        project_back_kernel,
        info,
        (x, message, dmid, vec_rel[0:1], *grads, *attn),
        (z,),
        [once(frames, ROWS, D), once(FRAMES, D), once(frames, ROWS, D), once(1, D)]
        + [block] * 3
        + [a_spec] * 2
        + [b_spec] * 2,
        [once(frames, ROWS, D), kept(frames, 1, D), kept(2, D)],
        [shaped(f32, frames, ROWS, D), shaped(f32, frames, 1, D), shaped(f32, 2, D)],
        "project_back",
        [pltpu.VMEM((frames, ROWS, D), f32)],
        6 * frames * ROWS * D * D,
    )


def message_halves(own_ref, other_ref, i):
    count = own_ref.shape[0]
    part = D // 2 // count
    return [
        ref[:, i * part : (i + 1) * part].reshape(D // 2, ref.shape[-1])
        for ref in (own_ref, other_ref)
    ]


def message_times(rows, refs, i):
    own, other = rows[:, : D // 2], rows[:, D // 2 :]
    cols = []
    for own_ref, other_ref in (refs[:2], refs[2:]):
        weights = message_halves(own_ref, other_ref, i)
        cols.append(dot(own, weights[0]) + dot(other, weights[1]))
    return jnp.concatenate(cols, 1)


def message_times_t(rows, refs, i):
    left, right = rows[:, : D // 2], rows[:, D // 2 :]
    first, second = message_halves(*refs[:2], i), message_halves(*refs[2:], i)
    return jnp.concatenate(
        [dot(left, first[s], NT) + dot(right, second[s], NT) for s in range(2)], 1
    )


def by_head(rows):
    full = jnp.concatenate([rows.astype(f32)] * HEADS, 0)
    return jnp.where(head_mask(), full, 0.0).astype(bf16)


def head_mask():
    shape = (HEADS * FRAMES, D)
    head = lax.broadcasted_iota(jnp.int32, shape, 0) // FRAMES
    return head == lax.broadcasted_iota(jnp.int32, shape, 1) // HEAD


def over_heads(rows):
    rows = jnp.where(head_mask(), rows, 0.0)
    return jnp.sum(rows.reshape(HEADS, FRAMES, D), 0)


def message_probability(queries, keys):
    scores = dot(by_head(queries), keys, NT) * HEAD**-0.5
    shifted = jnp.exp(scores - jnp.max(scores, 1, keepdims=True))
    return shifted * (1.0 / jnp.sum(shifted, 1, keepdims=True))


def message_forward_kernel(info_ref, cls_ref, vec_ref, *refs):
    weights, (msg_ref, first_ref, pack_ref, hold_ref) = refs[:4], refs[4:]

    def relative(rows):
        hold_ref[...] = rows
        return permuted(hold_ref, info_ref, 0)

    first = message_times(relative(cls_ref[...]).astype(bf16), weights, 0) + vec_ref[6:7]
    normed = norm_rows(first, vec_ref[4:5], vec_ref[5:6])[0].astype(bf16).astype(f32)
    normed_rel = relative(normed).astype(bf16)
    queries = (message_times(normed_rel, weights, 1) + vec_ref[7:8]).astype(bf16)
    keys = message_times(normed_rel, weights, 2).astype(bf16)
    values = (message_times(normed_rel, weights, 3) + vec_ref[8:9]).astype(bf16)
    probability = message_probability(queries, keys).astype(bf16)
    mixed = over_heads(dot(probability, values)).astype(bf16).astype(f32)
    message = first + message_times(relative(mixed).astype(bf16), weights, 4) + vec_ref[9:10]
    msg_ref[...] = relative(message)
    first_ref[...] = first
    for i, rows in enumerate((normed, mixed, queries, keys, values)):
        pack_ref[i] = rows.astype(f32)


def message_forward(info, class_rows, vectors, weights):
    one = kept(FRAMES, D)
    return call(
        message_forward_kernel,
        info,
        (class_rows, vectors, *weights),
        (1,),
        [one, kept(*vectors.shape)] + [once(*w.shape) for w in weights],
        [one, one, kept(5, FRAMES, D)],
        [shaped(f32, FRAMES, D), shaped(f32, FRAMES, D), shaped(f32, 5, FRAMES, D)],
        "message_forward",
        [pltpu.VMEM((FRAMES, D), f32)],
        10 * FRAMES * D * D,
    )


def message_backward_kernel(info_ref, dmsg_ref, first_ref, pack_ref, vec_ref, *refs):
    weights, (class_ref, sent_ref, sums_ref, hold_ref) = refs[:4], refs[4:]
    frames = dmsg_ref.shape[1]
    for i in range(dmsg_ref.shape[0]):
        place = lax.bitwise_xor(info_ref[2 * BLOCKS], i)
        for f in range(frames):
            hold_ref[i * frames + f : i * frames + f + 1] = dmsg_ref[place, f : f + 1]
    dmsg = permuted(hold_ref, info_ref, BLOCKS)

    def plain(rows):
        hold_ref[...] = rows
        return permuted(hold_ref, info_ref, BLOCKS)

    queries, keys, values = (pack_ref[i].astype(bf16) for i in (2, 3, 4))
    grad_mixed = plain(message_times_t(dmsg.astype(bf16), weights, 4)).astype(bf16)
    probability = message_probability(queries, keys)
    grads_big = by_head(grad_mixed)
    grad_prob = dot(grads_big, values, NT)
    inner = jnp.sum(grad_prob * probability, 1, keepdims=True)
    grad_scores = (probability * (grad_prob - inner)).astype(bf16)
    dq = (over_heads(dot(grad_scores, keys)) * HEAD**-0.5).astype(bf16)
    dk = (dot(grad_scores, by_head(queries), TN) * HEAD**-0.5).astype(bf16)
    dv = dot(probability.astype(bf16), grads_big, TN).astype(bf16)
    grad = plain(
        message_times_t(dq, weights, 1)
        + message_times_t(dk, weights, 2)
        + message_times_t(dv, weights, 3)
    )
    _, scaled, inverse = norm_rows(first_ref[...], 1.0, 0.0)
    back = norm_back(grad, scaled, inverse, vec_ref[4:5])
    dfirst = (dmsg + back).astype(bf16)
    class_ref[...] = message_times_t(dfirst, weights, 0)
    sent = [rows.astype(f32) for rows in (dfirst, dq, dk, dv, dmsg)]
    for i, rows in enumerate(sent):
        sent_ref[i] = rows
    sums = [grad * scaled, grad, sent[0], sent[1], sent[3], dmsg]
    sums_ref[...] = jnp.concatenate([jnp.sum(rows, 0, keepdims=True) for rows in sums], 0)


def message_backward(info, dmsg, first, pack, vectors, weights):
    one = kept(FRAMES, D)
    return call(
        message_backward_kernel,
        info,
        (dmsg, first, pack, vectors, *weights),
        (1,),
        [kept(*dmsg.shape), one, kept(*pack.shape), kept(*vectors.shape)]
        + [once(*w.shape) for w in weights],
        [one, kept(5, FRAMES, D), kept(6, D)],
        [shaped(f32, FRAMES, D), shaped(f32, 5, FRAMES, D), shaped(f32, 6, D)],
        "message_backward",
        [pltpu.VMEM((FRAMES, D), f32)],
        10 * FRAMES * D * D,
    )


def relative_order():
    return lax.axis_size("dp") * BLOCK == D


def make_info():
    place = lax.iota(jnp.int32, BLOCKS)
    if relative_order():
        mine = lax.axis_index("dp")
        differs = place ^ mine
        places = mine ^ (2 * (place % 4) + place // 4)
        blocks = (differs % 2) * 4 + differs // 2
    else:
        places = blocks = place
    return jnp.concatenate([places, blocks, lax.axis_index("tensor")[None]]).astype(jnp.int32)


def swap(values, axis, bit):
    pairs = [(i, i ^ bit) for i in range(lax.axis_size(axis))]
    return lax.ppermute(values, axis, pairs)


def bits_of(axis):
    size = lax.axis_size(axis)
    return [1 << i for i in range(size.bit_length() - 1)]


def after(values, *earlier):
    return lax.optimization_barrier((values, earlier))[0]


class Gather:
    def __init__(self, values, which):
        self.which, self.place, self.own = which, 0, values
        if relative_order():
            self.arrived = swap(values, "dp", 4 if which else 2)
        else:
            everything = lax.all_gather(values, "dp", axis=0)
            count = everything.shape[0] // 2
            self.own, self.arrived = everything[:count], everything[count:]

    def step(self, *earlier):
        if not relative_order():
            return self.own
        arrived = after(self.arrived, *earlier) if earlier else self.arrived
        self.place += 1
        if self.place == 1:
            self.own = jnp.stack([self.own, arrived])
            self.arrived = swap(self.own, "dp", 2 if self.which else 4)
        else:
            own = jnp.stack([self.own, arrived], 1 if self.which else 0)
            self.own = own.reshape((4,) + own.shape[2:])
            self.arrived = swap(self.own, "dp", 1)
        return self.own

    def result(self):
        return self.own, self.arrived


def gather_small(values):
    if not relative_order():
        return lax.all_gather(values, "dp", axis=0)
    values = values[None]
    for bit in (2, 4, 1):
        values = jnp.concatenate([values, swap(values, "dp", bit)], 0)
    return values


def add_low(left_side, right_side):
    return (left_side.astype(f32) + right_side.astype(f32)).astype(bf16)


class Scatter:
    def __init__(self, keep, send, which):
        self.which, self.place = which, 0
        self.held, self.sent = keep, send
        if relative_order():
            self.held = keep.reshape((2, 2) + keep.shape[1:])
            self.arrived = swap(send, "dp", 1).reshape(self.held.shape)
        else:
            self.total = lax.psum_scatter(
                jnp.concatenate([keep, send], 0), "dp", scatter_dimension=0, tiled=False
            )

    def step(self, *earlier):
        if not relative_order():
            return self.total
        if earlier:
            self.arrived = after(self.arrived, *earlier)
        axis, bit = ((0, 4), (0, 2))[self.place] if not self.which else ((1, 2), (0, 4))[self.place]
        take = lambda v, i: lax.index_in_dim(v, i, axis, keepdims=False)
        going = add_low(take(self.held, 1), take(self.arrived, 1))
        self.held = add_low(take(self.held, 0), take(self.arrived, 0))
        self.arrived = swap(going, "dp", bit)
        self.place += 1
        return going

    def result(self, *earlier):
        if not relative_order():
            return self.total
        if earlier:
            self.arrived = after(self.arrived, *earlier)
        return add_low(self.held, self.arrived)


def scatter_videos(values, earlier=None):
    if earlier is not None:
        values = after(values, earlier)
    return lax.psum_scatter(values, "tensor", scatter_dimension=0, tiled=False)


class ScatterVideos:
    def __init__(self, values):
        self.direct = values.shape[0] != 4
        if self.direct:
            self.going = self.total = scatter_videos(values)
            return
        mine = lax.axis_index("tensor")
        self.low, self.high = mine % 2, mine // 2
        pairs = values.reshape((2, 2) + values.shape[1:])
        self.going, self.held = self.take(pairs, 1 - self.low, 1), self.take(pairs, self.low, 1)
        self.arrived = swap(self.going, "tensor", 1)

    @staticmethod
    def take(values, at, axis):
        return lax.dynamic_index_in_dim(values, at, axis, keepdims=False)

    def step(self, *earlier):
        if self.direct:
            return self.total
        arrived = after(self.arrived, *earlier)
        take = self.take
        going = add_low(take(self.held, 1 - self.high, 0), take(arrived, 1 - self.high, 0))
        self.held = add_low(take(self.held, self.high, 0), take(arrived, self.high, 0))
        self.arrived = swap(going, "tensor", 2)
        return going

    def result(self, *earlier):
        if self.direct:
            return self.total
        return add_low(self.held, after(self.arrived, *earlier) if earlier else self.arrived)


def sum_everywhere(values):
    for axis in ("dp", "tensor"):
        for bit in bits_of(axis):
            values = values + swap(values, axis, bit)
    return values


def gather_and_sum_videos(values, sums):
    values, count = values[None], sums.shape[0]
    for bit in bits_of("tensor"):
        rows = jnp.concatenate([sums, values.reshape(-1, D)], 0)
        arrived = swap(rows, "tensor", bit)
        sums = sums + arrived[:count]
        values = jnp.concatenate([values, arrived[count:].reshape(values.shape)], 0)
    return values, sums


def adam_step(weight, first_moment, second_moment, gradient, factor, step_rate, decay_rate):
    clipped = gradient * factor
    first_new = beta_one * first_moment + (1.0 - beta_one) * clipped
    second_new = beta_two * second_moment + (1.0 - beta_two) * clipped * clipped
    update = (
        first_new
        / (1.0 - beta_one**STEP)
        / (jnp.sqrt(second_new / (1.0 - beta_two**STEP)) + adam_eps)
    )
    weight_new = weight - step_rate * (update + decay_rate * weight)
    return (first_new, second_new, weight_new)


def on_device(
    tokens,
    cotangent,
    attn_master,
    attn_first,
    attn_second,
    attn_ema,
    mlp_master,
    mlp_first,
    mlp_second,
    mlp_ema,
    msg_master,
    msg_first,
    msg_second,
    msg_ema,
    vec_master,
    vec_first,
    vec_second,
    vec_ema,
):
    z_index = lax.axis_index("tensor")
    z_count = lax.axis_size("tensor")
    dp_index = lax.axis_index("dp")
    part = attn_master.shape[0]
    local_width = attn_master.shape[2]
    local_ff = mlp_master.shape[2]
    frames = tokens.shape[0] // PATCHES
    half_ff = local_ff // 2
    info = make_info()

    class_own = tokens.reshape(frames, PATCHES, D)[:, 0].reshape(-1, local_width)
    attn_low = jnp.swapaxes(attn_master, 0, 1).astype(bf16).reshape(4 * part, local_width)
    attn_rows = pad_rows(jnp.concatenate([attn_low, class_own], 0), 4 * part + 16)
    attn_z = lax.all_gather(attn_rows, "tensor", axis=0)
    mlp_z = lax.all_gather(jnp.swapaxes(mlp_master, 0, 1).astype(bf16), "tensor", axis=0)
    class_rows = attn_z[:, 4 * part : 4 * part + class_own.shape[0]].reshape(FRAMES, D)
    attn_z = attn_z[:, : 4 * part].reshape(z_count, 4, part, local_width)

    msg_low = jnp.swapaxes(msg_master, 0, 1).astype(bf16).reshape(5 * part, D)
    vec_count = vec_master.shape[1]
    vec_low = jnp.pad(vec_master.astype(bf16).T, ((0, 32 - vec_count), (0, D // 2 - part)))
    msg_half = [jnp.concatenate([msg_low[:, : D // 2], vec_low], 0), msg_low[:, D // 2 :]]
    msg_go = [Gather(msg_half[i], i) for i in range(2)]
    x, grads, grads_t, grad_sum = prepare(info, tokens, cotangent)
    sent_msg = [g.step(x) for g in msg_go]
    attn_z = after(attn_z, *sent_msg)
    attn_go = [Gather(attn_z[:, 2 * i : 2 * i + 2], i) for i in range(2)]
    sent_attn = [g.step() for g in attn_go]
    sent_msg = [g.step(*sent_attn) for g in msg_go]
    mlp_z = after(mlp_z, *sent_msg)
    mlp_go = [
        [Gather(mlp_z[:, i, :, j * half_ff : (j + 1) * half_ff], i) for i in range(2)]
        for j in range(2)
    ]
    msg_w = [side for g in msg_go for side in g.result()]
    vec_rel = jnp.concatenate(
        [side[:, 5 * part : 5 * part + vec_count, :part] for side in msg_w[:2]], 0
    )
    vec_rel = jnp.moveaxis(vec_rel, 0, 1).reshape(-1, D).astype(f32)
    vectors = plain_order(info, vec_rel)
    ff_bias = vectors[14:].reshape(z_count, 2, half_ff)

    sent_attn = [g.step(*[m.own for m in mlp_go[0]]) for g in attn_go]
    message, first_msg, msg_pack = message_forward(
        info, after(class_rows, *sent_attn).astype(f32), vectors, msg_w
    )
    attn_w = [side for g in attn_go for side in g.result()]
    queries, key_rows, value_rows, normed_t = project(
        info, x, message, vec_rel, vectors, attn_w
    )
    sent_mlp = [g.step(queries) for g in mlp_go[0]]
    attended, totals = attend_forward(after(queries, *sent_mlp), key_rows, value_rows)
    sent_mlp = [g.step(attended) for g in mlp_go[1] + mlp_go[0]]
    middle, n2, n2_t = combine(info, x, after(attended, *sent_mlp), vec_rel, attn_w)
    sent_mlp = [g.step(middle) for g in mlp_go[1]]
    n2 = after(n2, *sent_mlp)

    def feed(j):
        weights = [side for g in mlp_go[j] for side in g.result()]
        return feed_forward(n2, n2_t, grads, grads_t, ff_bias[:, j], weights)

    def two(grads_of):
        return [Scatter(grads_of[2 * i], grads_of[2 * i + 1], i) for i in range(2)]

    out_0, dn2_0, *dw_0, db_0 = feed(0)
    sums_0 = two(dw_0)
    out_1, dn2_1, *dw_1, db_1 = feed(1)
    sums_1 = two(dw_1)
    going = [s.step(db_1) for s in sums_0]
    dmid, grad_attended, *grad_out_w, sums_two = between(
        info, after(dn2_0, *going), dn2_1, middle, grads, attended, vec_rel, attn_w
    )
    going = [s.step(dmid) for s in sums_1]
    pairs = HEADS // 2
    back = (queries, key_rows, value_rows, totals)
    grad_qkv = attend_backward(*back, after(grad_attended, *going), 0, pairs // 2)
    going = [s.step(grad_qkv[0]) for s in sums_0]
    grad_qkv = attend_backward(
        *back, after(grad_attended, *going), pairs // 2, pairs - pairs // 2, grad_qkv
    )
    mlp_0 = ScatterVideos(jnp.stack([s.result(grad_qkv[0]) for s in sums_0], 1))
    going = [s.step(grad_qkv[0]) for s in sums_1]
    dqk_keep, dqk_send, dv_keep, dv_send, sum_q, sum_v = project_grads(
        info, after(normed_t, mlp_0.going, *going), grad_qkv, attn_w
    )
    going = mlp_0.step(sum_q)
    mlp_1 = ScatterVideos(jnp.stack([s.result(sum_q) for s in sums_1], 1))
    dqk_send, dv_send = after((dqk_send, dv_send), going, mlp_1.going)
    sums_attn = [
        Scatter(dqk_keep, dqk_send, 0),
        Scatter(
            jnp.stack([dv_keep, grad_out_w[0]], 2), jnp.stack([dv_send, grad_out_w[1]], 2), 1
        ),
    ]
    block_output = finish(
        info,
        [after(middle, sums_attn[1].sent), out_0, out_1],
        vec_rel[13:14],
        "block_output",
    )
    going = [s.step(block_output) for s in sums_attn]
    going.append(mlp_1.step(block_output))
    mlp_0 = mlp_0.result(block_output)
    ing, dmsg, sums_one = project_back(
        info, after(x, mlp_0, *going), message, dmid, vec_rel, grad_qkv, attn_w
    )
    going = [s.step(ing) for s in sums_attn]
    mlp_1 = mlp_1.result(ing)

    relative = plain_order(info, jnp.concatenate([sums_one, sums_two, grad_sum], 0))
    ff_bias_grad = jnp.stack(
        [db.reshape(z_count, half_ff) for db in (db_0, db_1)], 1
    ).reshape(FF // D, D)
    table = jnp.concatenate([relative[:4], sum_q, sum_v, relative[4:], ff_bias_grad], 0)
    dmsg = dmsg[:, 0].astype(bf16).astype(f32)
    dmsg, table = gather_and_sum_videos(after(dmsg, mlp_1, *going), table)
    grad_class, sent, sums_msg = message_backward(
        info, dmsg, first_msg, msg_pack, vectors, msg_w
    )
    attn_sum = jnp.concatenate([s.result(grad_class) for s in sums_attn], 1)
    attn_go = ScatterVideos(attn_sum)
    input_grad = finish(info, [after(ing, attn_go.going)], grad_class, "input_grad")
    going = attn_go.step(input_grad)

    table = jnp.concatenate([table[:4], sums_msg, table[4:]], 0)
    sent = jnp.concatenate([msg_pack[:2], sent], 0).astype(bf16).reshape(7 * FRAMES, D)
    sent = jnp.concatenate([class_rows, sent, table.astype(bf16)], 0)
    everyone = gather_small(after(sent, going))
    attn_grad = attn_go.result(everyone)
    everyone = after(everyone, attn_grad)
    tables = lax.dynamic_slice_in_dim(everyone[:, 8 * FRAMES :], dp_index * part, part, 2)
    vec_grad = jnp.sum(tables.astype(f32), 0).T
    everyone = everyone[:, : 8 * FRAMES].reshape(-1, 8, FRAMES, D)
    everyone = jnp.moveaxis(everyone, 0, 1).reshape(8, -1, D)
    mine = lax.dynamic_slice_in_dim(everyone[:3], dp_index * part, part, 2)
    msg_grad = jnp.stack(
        [
            dot(mine[0], everyone[3], TN),
            dot(mine[1], everyone[4], TN),
            dot(mine[1], everyone[5], TN),
            dot(mine[1], everyone[6], TN),
            dot(mine[2], everyone[7], TN),
        ],
        1,
    )

    attn_grad = jnp.swapaxes(attn_grad, 0, 1).astype(f32)
    mlp_grad = jnp.swapaxes(jnp.concatenate([mlp_0, mlp_1], 2), 0, 1).astype(f32)

    keep_share = (z_index == 0).astype(f32)
    squares = (
        jnp.sum(attn_grad * attn_grad)
        + jnp.sum(mlp_grad * mlp_grad)
        + keep_share * (jnp.sum(msg_grad * msg_grad) + jnp.sum(vec_grad * vec_grad))
    )
    squares = sum_everywhere(jnp.broadcast_to(squares, (8, 128)))[0, 0]
    grad_norm = jnp.sqrt(squares)
    factor = clip_limit / jnp.maximum(grad_norm, clip_limit)

    def update(master, first, second, ema, grad, rate, decay):
        first_new, second_new, weight = adam_step(master, first, second, grad, factor, rate, decay)
        return grad, first_new, second_new, weight, ema_keep * ema + (1.0 - ema_keep) * weight

    return (
        block_output,
        input_grad,
        grad_norm,
        *update(attn_master, attn_first, attn_second, attn_ema, attn_grad, rate_mat, decay_mat),
        *update(mlp_master, mlp_first, mlp_second, mlp_ema, mlp_grad, rate_mat, decay_mat),
        *update(msg_master, msg_first, msg_second, msg_ema, msg_grad, rate_mat, decay_mat),
        *update(vec_master, vec_first, vec_second, vec_ema, vec_grad, rate_vec, 0.0),
    )


def solution(mesh):
    rows = P(("dp", "tensor"), None)
    split = P("dp", None, "tensor")
    copied = P("dp", None, None)
    table = P("dp", None)
    in_specs = (rows,) * 2 + (split,) * 8 + (copied,) * 4 + (table,) * 4
    out_specs = (rows,) * 2 + (P(),) + (split,) * 10 + (copied,) * 5 + (table,) * 5
    return jax.shard_map(
        on_device, mesh=mesh, in_specs=in_specs, out_specs=out_specs, check_vma=False
    )
```

```python
import functools

import jax
import jax.numpy as jnp
from jax import lax
from jax.experimental import pallas as pl
from jax.experimental.pallas import tpu as pltpu
from jax.sharding import PartitionSpec as P

D = 1024
HEADS = 16
HEAD = 64
FF = 4096
PATCHES = 577
FRAMES = 8
STEP = 10
ROWS = 592


norm_eps = 1e-05
beta_one = 0.9
beta_two = 0.95
adam_eps = 1e-08
decay_mat = 0.05
ema_keep = 0.7
clip_limit = 1.0
rate_mat = 0.02
rate_vec = 0.4
far_below = -1e30
COST_PART = 16
bf16 = jnp.bfloat16
f32 = jnp.float32
NN = (((1,), (0,)), ((), ()))
NT = (((1,), (1,)), ((), ()))
TN = (((0,), (0,)), ((), ()))


def dot(left_side, right_side, dims=NN):
    return lax.dot_general(left_side, right_side, dims, preferred_element_type=f32)


def norm_rows(values, gain_row, shift_row):
    centre = values - jnp.mean(values, -1, keepdims=True)
    spread = jnp.mean(centre * centre, -1, keepdims=True)
    inverse = lax.rsqrt(spread + norm_eps)
    scaled = centre * inverse
    return (scaled * gain_row + shift_row, scaled, inverse)


def norm_back(gradient, scaled, inverse, gain_row):
    inner = gradient * gain_row
    return inverse * (
        inner
        - jnp.mean(inner, -1, keepdims=True)
        - scaled * jnp.mean(inner * scaled, -1, keepdims=True)
    )


def pad_rows(values, count):
    if values.shape[0] == count:
        return values
    extra = jnp.zeros((count - values.shape[0],) + values.shape[1:], values.dtype)
    return jnp.concatenate([values, extra], 0)


def head_pair(queries, key_rows, head):
    lane = lax.broadcasted_iota(jnp.int32, queries.shape, 1)
    key_lane = lax.broadcasted_iota(jnp.int32, key_rows.shape, 1)
    key_row = lax.broadcasted_iota(jnp.int32, key_rows.shape, 0)
    spare = HEAD * (1 - head)
    mask = jnp.where(
        (key_lane == spare) & (key_row > PATCHES), jnp.asarray(far_below, bf16), jnp.asarray(0, bf16)
    )
    keys_one = jnp.where((key_lane // HEAD) == head, key_rows, mask)
    queries_one = jnp.where(lane == spare, jnp.asarray(1, bf16), queries)
    return queries_one, keys_one


def attend_forward_kernel(q_ref, k_ref, v_ref, out_ref, total_ref):
    rows = q_ref.shape[1]
    key_count = -(-rows // 128) * 128
    queries = q_ref[0] * jnp.asarray(HEAD**-0.5, bf16)
    key_rows = pad_rows(k_ref[0], key_count)
    value_rows = pad_rows(v_ref[0], key_count)
    lane = lax.broadcasted_iota(jnp.int32, (rows, 128), 1)
    outs, totals = [], []
    for head in range(2):
        queries_one, keys_one = head_pair(queries, key_rows, head)
        scores = dot(queries_one, keys_one, NT)
        highest = jnp.max(scores, 1, keepdims=True)
        shifted = jnp.exp(scores - highest)
        total = jnp.sum(shifted, 1, keepdims=True)
        probability = (shifted * (1.0 / total)).astype(bf16)
        outs.append(dot(probability, value_rows))
        totals.append(highest + jnp.log(total))
    out_ref[0] = jnp.where(lane < HEAD, outs[0], outs[1]).astype(bf16)
    both = jnp.where(lane < HEAD, totals[0], totals[1]).T
    total_ref[0, 0] = jnp.concatenate([both[0:1], both[HEAD : HEAD + 1]], 0)


def attend_backward_kernel(q_ref, k_ref, v_ref, total_ref, grad_ref, *rest):
    dq_ref, dk_ref, dv_ref = rest[-3:]
    rows = q_ref.shape[1]
    query_count = -(-rows // 128) * 128
    queries = pad_rows(q_ref[0], query_count) * jnp.asarray(HEAD**-0.5, bf16)
    grads = pad_rows(grad_ref[0], query_count)
    key_rows = k_ref[0]
    value_rows = v_ref[0]
    keys_t = pad_rows(key_rows, query_count).astype(f32).T.astype(bf16)
    lane = lax.broadcasted_iota(jnp.int32, (rows, 128), 1)
    grad_q, grad_k, grad_v = [], [], []
    for head in range(2):
        queries_one, keys_one = head_pair(queries, key_rows, head)
        total = total_ref[0, 0, head : head + 1, :]
        if query_count > rows:
            total = jnp.concatenate([total, jnp.zeros((1, query_count - rows), f32)], 1)
        probability = jnp.exp(dot(keys_one, queries_one, NT) - total)
        values_one = jnp.where((lane // HEAD) == head, value_rows, jnp.asarray(0, bf16))
        grad_prob = dot(values_one, grads, NT)
        inner = jnp.sum(grad_prob * probability, 0, keepdims=True)
        grad_scores = (probability * (grad_prob - inner)).astype(bf16)
        grad_v.append(dot(probability.astype(bf16), grads))
        grad_k.append(dot(grad_scores, queries))
        grad_q.append(dot(keys_t[HEAD * head : HEAD * (head + 1)], pad_rows(grad_scores, query_count)))
    grad_q = jnp.concatenate(grad_q, 0) * HEAD**-0.5
    dq_ref[0] = grad_q.T[:rows].astype(bf16)
    dk_ref[0] = jnp.where(lane < HEAD, grad_k[0], grad_k[1]).astype(bf16)
    dv_ref[0] = jnp.where(lane < HEAD, grad_v[0], grad_v[1]).astype(bf16)


def cost(flops, moved):
    return pl.CostEstimate(
        flops=flops // COST_PART, bytes_accessed=moved // COST_PART, transcendentals=0
    )


def attend_cost(frames, rows, width, matmuls):
    return cost(2 * matmuls * frames * rows * rows * width, 4 * matmuls * frames * rows * width)


def attend_forward(queries, key_rows, value_rows):
    frames, rows, width = queries.shape
    spec = pl.BlockSpec((1, rows, 128), lambda f, h: (f, 0, h))
    return pl.pallas_call(
        attend_forward_kernel,
        grid=(frames, width // 128),
        in_specs=[spec] * 3,
        out_specs=[spec, pl.BlockSpec((1, 1, 2, rows), lambda f, h: (f, h, 0, 0))],
        out_shape=[
            jax.ShapeDtypeStruct((frames, rows, width), bf16),
            jax.ShapeDtypeStruct((frames, width // 128, 2, rows), f32),
        ],
        compiler_params=pltpu.CompilerParams(vmem_limit_bytes=48 << 20),
        cost_estimate=attend_cost(frames, rows, width, 4),
        name="attend_forward",
    )(queries, key_rows, value_rows)


def attend_backward(queries, key_rows, value_rows, totals, grads, begin, count, earlier=()):
    frames, rows, width = queries.shape
    spec = pl.BlockSpec((1, rows, 128), lambda f, h: (f, 0, h + begin))
    total_spec = pl.BlockSpec((1, 1, 2, rows), lambda f, h: (f, h + begin, 0, 0))
    return pl.pallas_call(
        attend_backward_kernel,
        grid=(frames, count),
        in_specs=[spec] * 3 + [total_spec, spec] + [pl.BlockSpec(memory_space=pl.ANY)] * len(earlier),
        out_specs=[spec] * 3,
        out_shape=[jax.ShapeDtypeStruct((frames, rows, width), bf16)] * 3,
        input_output_aliases={5 + i: i for i in range(len(earlier))},
        compiler_params=pltpu.CompilerParams(vmem_limit_bytes=48 << 20),
        cost_estimate=attend_cost(frames, rows, count * 128, 8),
        name="attend_backward",
    )(queries, key_rows, value_rows, totals, grads, *earlier)


def feed_kernel(
    n2_ref,
    n2t_ref,
    g_ref,
    gt_ref,
    bias_ref,
    *refs,
):
    up_refs, down_refs = refs[:4], refs[4:8]
    out_ref, dn2_ref, dup_own_ref, dup_other_ref, ddown_own_ref, ddown_other_ref = refs[8:14]
    db_ref, act_ref, dpre_ref = refs[14:]
    frames, rows = n2_ref.shape[:2]
    blocks, _, part, chunk = dup_own_ref.shape
    half = blocks * part

    @pl.when(pl.program_id(0) == 0)
    def _():
        out_ref[...] = jnp.zeros_like(out_ref)
        dn2_ref[...] = jnp.zeros_like(dn2_ref)
        act_ref[...] = jnp.zeros_like(act_ref)
        dpre_ref[...] = jnp.zeros_like(dpre_ref)

    first = jnp.concatenate(halves(up_refs, 0, 0), 0)
    second = jnp.concatenate(halves(down_refs, 1, 0), 0)
    bias_sum = jnp.zeros((1, chunk), f32)
    for frame in range(frames):
        place = pl.ds(frame * rows, rows)
        pre = dot(n2_ref[frame], first) + bias_ref[0]
        sigma = 1.0 / (1.0 + jnp.exp(-1.702 * pre))
        act = (pre * sigma).astype(bf16)
        act_ref[place] = act
        out_ref[frame] += dot(act, second, NT)
        grad_act = dot(g_ref[frame], second)
        grad_pre = grad_act * (sigma + 1.702 * pre * sigma * (1.0 - sigma))
        grad_low = grad_pre.astype(bf16)
        dpre_ref[place] = grad_low
        bias_sum += jnp.sum(grad_low.astype(f32), 0, keepdims=True)
        dn2_ref[frame] += dot(grad_low, first, NT)
    db_ref[0] = bias_sum

    def place_grad(left_ref, right_ref, own_ref, other_ref):
        for at, ref in ((0, own_ref), (half, other_ref)):
            grad = dot(left_ref[at : at + half], right_ref[...]).astype(bf16)
            ref[:, 0] = grad.reshape(blocks, part, chunk)

    place_grad(n2t_ref, dpre_ref, dup_own_ref, dup_other_ref)
    place_grad(gt_ref, act_ref, ddown_own_ref, ddown_other_ref)


def feed_forward(n2, n2t, grads, grads_t, bias, weights):
    frames, rows, _ = n2.shape
    blocks, ff_blocks, part, local = weights[0].shape
    blocks = 2 * blocks
    chunk = min(512, local)
    per = local // chunk
    steps = ff_blocks * per
    deep = n2t.shape[1]
    whole3 = lambda n: (0, 0, 0)
    whole2 = lambda n: (0, 0)
    single = pl.Buffered(1)
    w_spec = pl.BlockSpec((blocks // 2, 1, part, chunk), lambda n: (0, n // per, 0, n % per))
    dw_spec = pl.BlockSpec((blocks, 1, part, chunk), lambda n: (0, n // per, 0, n % per))
    dw_shape = jax.ShapeDtypeStruct((blocks, ff_blocks, part, local), bf16)
    return pl.pallas_call(
        feed_kernel,
        grid=(steps,),
        in_specs=[
            pl.BlockSpec((frames, rows, D), whole3, pipeline_mode=single),
            pl.BlockSpec((D, deep), whole2, pipeline_mode=single),
            pl.BlockSpec((frames, rows, D), whole3, pipeline_mode=single),
            pl.BlockSpec((D, deep), whole2, pipeline_mode=single),
            pl.BlockSpec((1, 1, chunk), lambda n: (n, 0, 0)),
        ]
        + [w_spec] * 8,
        out_specs=[pl.BlockSpec((frames, rows, D), whole3)] * 2
        + [dw_spec] * 4
        + [pl.BlockSpec((1, 1, chunk), lambda n: (n, 0, 0))],
        out_shape=[jax.ShapeDtypeStruct((frames, rows, D), f32)] * 2
        + [dw_shape] * 4
        + [jax.ShapeDtypeStruct((steps, 1, chunk), f32)],
        scratch_shapes=[pltpu.VMEM((deep, chunk), bf16), pltpu.VMEM((deep, chunk), bf16)],
        compiler_params=pltpu.CompilerParams(vmem_limit_bytes=60 << 20),
        cost_estimate=cost(
            12 * frames * rows * D * ff_blocks * local,
            8 * D * ff_blocks * local + 16 * frames * rows * D,
        ),
        name="feed_forward",
    )(n2, n2t, grads, grads_t, bias.reshape(steps, 1, chunk), *weights)


BLOCK = 128
BLOCKS = D // BLOCK


def permuted(ref, info_ref, first):
    return jnp.concatenate(
        [
            ref[:, pl.ds(pl.multiple_of(info_ref[first + i] * BLOCK, BLOCK), BLOCK)]
            for i in range(BLOCKS)
        ],
        1,
    )


def call(
    kernel, info, args, grid, in_specs, out_specs, out_shape, name, scratch=(), flops=0, vmem=56, aliases=None
):
    moved = sum(a.size * a.dtype.itemsize for a in args)
    moved += sum(o.size * o.dtype.itemsize for o in out_shape)
    return pl.pallas_call(
        kernel,
        grid_spec=pltpu.PrefetchScalarGridSpec(
            num_scalar_prefetch=1,
            grid=grid,
            in_specs=in_specs,
            out_specs=out_specs,
            scratch_shapes=list(scratch),
        ),
        out_shape=out_shape,
        input_output_aliases=aliases or {},
        compiler_params=pltpu.CompilerParams(vmem_limit_bytes=vmem << 20),
        cost_estimate=cost(flops, moved),
        name=name,
    )(info, *args)


def shaped(dtype, *shape):
    return jax.ShapeDtypeStruct(shape, dtype)


def once(*block, at=None):
    index = at or (0,) * len(block)
    return pl.BlockSpec(block, lambda *_: index, pipeline_mode=pl.Buffered(1))


def kept(*block):
    index = (0,) * len(block)
    return pl.BlockSpec(block, lambda *_: index)


def row_count(frames):
    return -(-frames * ROWS // 128) * 128


def prepare_kernel(info_ref, tokens_ref, cot_ref, x_ref, g_ref, gt_ref, gsum_ref, hold_ref):
    frames = x_ref.shape[0]
    count = tokens_ref.shape[0]
    inside = lax.broadcasted_iota(jnp.int32, (ROWS, BLOCK), 0) < PATCHES
    hold_ref[...] = jnp.zeros_like(hold_ref)

    def padded(ref):
        hold_ref[0:count] = ref[...].astype(f32)
        return [
            jnp.where(inside, hold_ref[pl.ds(f * PATCHES, ROWS)], 0.0) for f in range(frames)
        ]

    for f, rows in enumerate(padded(tokens_ref)):
        x_ref[f] = rows.astype(bf16)
    grads = padded(cot_ref)
    for f, rows in enumerate(grads):
        g_ref[f] = rows.astype(bf16)
    full = pad_rows(jnp.concatenate(grads, 0), gt_ref.shape[1])
    gt_ref[...] = full.T.astype(bf16)
    gsum_ref[...] = jnp.sum(full, 0, keepdims=True)


def prepare(info, tokens, cotangent):
    count = tokens.shape[0]
    frames = count // PATCHES
    deep = row_count(frames)
    taken = pl.BlockSpec((count, BLOCK), lambda r, info_ref: (0, info_ref[r]))
    placed = pl.BlockSpec((frames, ROWS, BLOCK), lambda r, info_ref: (0, 0, r))
    return call(
        prepare_kernel,
        info,
        (tokens, cotangent),
        (BLOCKS,),
        [taken] * 2,
        [
            placed,
            placed,
            pl.BlockSpec((BLOCK, deep), lambda r, info_ref: (r, 0)),
            pl.BlockSpec((1, BLOCK), lambda r, info_ref: (0, r)),
        ],
        [
            shaped(bf16, frames, ROWS, D),
            shaped(bf16, frames, ROWS, D),
            shaped(bf16, D, deep),
            shaped(f32, 1, D),
        ],
        "prepare",
        [pltpu.VMEM((-(-((frames - 1) * PATCHES + ROWS) // 8) * 8, BLOCK), f32)],
    )


def plain_order_kernel(info_ref, in_ref, out_ref):
    out_ref[...] = permuted(in_ref, info_ref, BLOCKS)


def plain_order(info, values):
    return call(
        plain_order_kernel,
        info,
        (values,),
        (1,),
        [kept(*values.shape)],
        [kept(*values.shape)],
        [shaped(f32, *values.shape)],
        "plain_order",
    )[0]


def finish_kernel(count, info_ref, *refs):
    in_refs, row_ref, out_ref = refs[:count], refs[count], refs[-1]
    frames = in_refs[0].shape[0]
    for f in range(frames):
        rows = in_refs[0][f]
        for ref in in_refs[1:]:
            rows = rows + ref[f]
        if row_ref.shape[0] == 1:
            rows = rows + row_ref[...]
        else:
            class_row = row_ref[pl.ds(info_ref[2 * BLOCKS] * frames + f, 1)]
            first = lax.broadcasted_iota(jnp.int32, (ROWS, BLOCK), 0) == 0
            rows = rows + jnp.where(first, class_row, 0.0)
        out_ref[pl.ds(f * PATCHES, PATCHES)] = rows[:PATCHES]


def finish(info, parts, row, name, begin=0, count=BLOCKS, earlier=()):
    frames = parts[0].shape[0]
    at = lambda d, info_ref: info_ref[BLOCKS + begin + d]
    taken = pl.BlockSpec((frames, ROWS, BLOCK), lambda d, info_ref: (0, 0, at(d, info_ref)))
    row_spec = pl.BlockSpec((row.shape[0], BLOCK), lambda d, info_ref: (0, at(d, info_ref)))
    return call(
        functools.partial(finish_kernel, len(parts)),
        info,
        (*parts, row, *earlier),
        (count,),
        [taken] * len(parts) + [row_spec] + [pl.BlockSpec(memory_space=pl.ANY)] * len(earlier),
        [pl.BlockSpec((frames * PATCHES, BLOCK), lambda d, info_ref: (0, begin + d))],
        [shaped(f32, frames * PATCHES, D)],
        name,
        aliases={len(parts) + 2: 0} if earlier else {},
    )[0]


def with_message(x_ref, msg_ref, info_ref, f):
    frames = x_ref.shape[0]
    message = msg_ref[pl.ds(info_ref[2 * BLOCKS] * frames + f, 1)]
    place = lax.broadcasted_iota(jnp.int32, (ROWS, D), 0) == PATCHES
    return jnp.where(place, message, x_ref[f].astype(f32))


def put_transposed(ref, rows):
    for c in range(BLOCKS):
        block = pad_rows(rows[:, c * BLOCK : (c + 1) * BLOCK].astype(f32), ref.shape[1])
        ref[c * BLOCK : (c + 1) * BLOCK] = block.T.astype(bf16)


def halves(refs, which, *at):
    sides = []
    for pair in (refs[:2], refs[2:]):
        first, second = (ref[(slice(None), *at)] for ref in pair)
        part, width = first.shape[-2:]
        if which and part == BLOCK:
            blocks = [first[0], second[0], first[1], second[1]]
        else:
            blocks = [v.reshape(-1, width) for v in (first, second)]
        sides.append(jnp.concatenate(blocks, 0))
    return sides


def project_kernel(
    info_ref, x_ref, msg_ref, gain_ref, shift_ref, bq_ref, bv_ref, *refs
):
    a_refs, b_refs, (q_ref, k_ref, v_ref, ht_ref, h_ref) = refs[:4], refs[4:8], refs[8:]
    frames = x_ref.shape[0]

    @pl.when(pl.program_id(0) == 0)
    def _():
        for f in range(frames):
            rows = with_message(x_ref, msg_ref, info_ref, f)
            normed = norm_rows(rows, gain_ref[...], shift_ref[...])[0]
            h_ref[pl.ds(f * ROWS, ROWS)] = normed.astype(bf16)
        put_transposed(ht_ref, h_ref[...])

    sides = (slice(0, D // 2), slice(D // 2, D))
    for out_ref, weights, bias in (
        (q_ref, halves(a_refs, 0, 0, 0), bq_ref[...]),
        (k_ref, halves(a_refs, 0, 0, 1), 0.0),
        (v_ref, halves(b_refs, 1, 0, 0), bv_ref[...]),
    ):
        for f in range(frames):
            place = pl.ds(f * ROWS, ROWS)
            rows = dot(h_ref[place, sides[0]], weights[0]) + dot(h_ref[place, sides[1]], weights[1])
            out_ref[f] = (rows + bias).astype(bf16)


def project(info, x, message, vec_rel, vectors, attn):
    frames = x.shape[0]
    n, z, _, part, width = attn[0].shape
    deep = row_count(frames)
    bias = pl.BlockSpec((1, width), lambda j, info_ref: (0, j))
    a_spec = pl.BlockSpec((n, 1, 2, part, width), lambda j, info_ref: (0, j, 0, 0, 0))
    b_spec = pl.BlockSpec((n, 1, 1, part, width), lambda j, info_ref: (0, j, 0, 0, 0))
    out = pl.BlockSpec((frames, ROWS, width), lambda j, info_ref: (0, 0, j))
    return call(
        project_kernel,
        info,
        (x, message, vec_rel[0:1], vec_rel[1:2], vectors[10:11], vectors[11:12], *attn),
        (z,),
        [once(frames, ROWS, D), once(FRAMES, D), once(1, D), once(1, D), bias, bias]
        + [a_spec] * 4
        + [b_spec] * 4,
        [out] * 3 + [kept(D, deep)],
        [shaped(bf16, frames, ROWS, D)] * 3 + [shaped(bf16, D, deep)],
        "project",
        [pltpu.VMEM((frames * ROWS, D), bf16)],
        6 * frames * ROWS * D * D,
    )


def combine_kernel(
    info_ref, x_ref, a_ref, bias_ref, gain_ref, shift_ref, *refs
):
    b_refs, (mid_ref, n2_ref, n2t_ref, hold_ref) = refs[:4], refs[4:]
    frames = x_ref.shape[0]
    z, width = b_refs[0].shape[1], b_refs[0].shape[-1]
    weights = [halves(b_refs, 1, j, 0) for j in range(z)]
    for f in range(frames):
        for side in range(2):
            half = slice(side * D // 2, (side + 1) * D // 2)
            total = x_ref[f, :, half].astype(f32) + bias_ref[:, half]
            for j in range(z):
                total += dot(a_ref[f, :, j * width : (j + 1) * width], weights[j][side], NT)
            mid_ref[f, :, half] = total
        low = mid_ref[f].astype(bf16).astype(f32)
        normed = norm_rows(low, gain_ref[...], shift_ref[...])[0].astype(bf16)
        n2_ref[f] = normed
        hold_ref[pl.ds(f * ROWS, ROWS)] = normed
    put_transposed(n2t_ref, hold_ref[...])


def combine(info, x, attended, vec_rel, attn):
    frames = x.shape[0]
    n, z, _, part, width = attn[4].shape
    deep = row_count(frames)
    weight = once(n, z, 1, part, width, at=(0, 0, 1, 0, 0))
    return call(
        combine_kernel,
        info,
        (x, attended, vec_rel[12:13], vec_rel[2:3], vec_rel[3:4], *attn[4:]),
        (1,),
        [once(frames, ROWS, D)] * 2 + [once(1, D)] * 3 + [weight] * 4,
        [once(frames, ROWS, D), once(frames, ROWS, D), once(D, deep)],
        [shaped(f32, frames, ROWS, D), shaped(bf16, frames, ROWS, D), shaped(bf16, D, deep)],
        "combine",
        [pltpu.VMEM((frames * ROWS, D), bf16)],
        2 * frames * ROWS * D * D,
    )


def between_kernel(
    info_ref, ea_ref, eb_ref, mid_ref, g_ref, a_ref, gain_ref, *refs
):
    b_refs, (dmid_ref, da_ref, keep_ref, send_ref, sums_ref, total_ref, dmt_ref) = refs[:4], refs[4:]
    f = pl.program_id(0)
    n, z, part, width = keep_ref.shape
    grad = ea_ref[0] + eb_ref[0]
    low = mid_ref[0].astype(bf16).astype(f32)
    _, scaled, inverse = norm_rows(low, 1.0, 0.0)
    back = norm_back(grad, scaled, inverse, gain_ref[...])
    dmid = (g_ref[0].astype(f32) + back).astype(bf16)
    dmid_ref[0] = dmid
    sums = jnp.concatenate(
        [
            jnp.sum(grad * scaled, 0, keepdims=True),
            jnp.sum(grad, 0, keepdims=True),
            jnp.sum(dmid.astype(f32), 0, keepdims=True),
        ],
        0,
    )

    @pl.when(f == 0)
    def _():
        sums_ref[...] = jnp.zeros_like(sums_ref)
        total_ref[...] = jnp.zeros_like(total_ref)

    sums_ref[...] += sums
    for j in range(z):
        weights = halves(b_refs, 1, j, 0)
        rows = dot(dmid[:, : D // 2], weights[0]) + dot(dmid[:, D // 2 :], weights[1])
        da_ref[0, :, j * width : (j + 1) * width] = rows.astype(bf16)
    put_transposed(dmt_ref, dmid)
    attended = pad_rows(a_ref[0], dmt_ref.shape[1])
    for j in range(z):
        lanes = slice(j * width, (j + 1) * width)
        total_ref[:, lanes] += dot(dmt_ref[...], attended[:, lanes])

    @pl.when(f == pl.num_programs(0) - 1)
    def _():
        for j in range(z):
            lanes = slice(j * width, (j + 1) * width)
            for at, ref in ((0, keep_ref), (D // 2, send_ref)):
                ref[:, j] = total_ref[at : at + D // 2, lanes].astype(bf16).reshape(n, part, width)


def between(info, ea, eb, middle, grads, attended, vec_rel, attn):
    frames = ea.shape[0]
    n, z, _, part, width = attn[4].shape
    frame = pl.BlockSpec((1, ROWS, D), lambda f, info_ref: (f, 0, 0))
    weight = once(n, z, 1, part, width, at=(0, 0, 1, 0, 0))
    return call(
        between_kernel,
        info,
        (ea, eb, middle, grads, attended, vec_rel[2:3], *attn[4:]),
        (frames,),
        [frame] * 5 + [once(1, D)] + [weight] * 4,
        [frame, frame, kept(2 * n, z, part, width), kept(2 * n, z, part, width), kept(3, D)],
        [shaped(bf16, frames, ROWS, D)] * 2
        + [shaped(bf16, 2 * n, z, part, width)] * 2
        + [shaped(f32, 3, D)],
        "between",
        [pltpu.VMEM((D, D), f32), pltpu.VMEM((D, row_count(1)), bf16)],
        4 * frames * ROWS * D * D,
    )


def project_grads_kernel(
    info_ref, ht_ref, dq_ref, dk_ref, dv_ref, ok_ref, os_ref, ak_ref, as_ref, bk_ref, bs_ref, sq_ref, sv_ref
):
    frames = dq_ref.shape[0]
    deep = ht_ref.shape[1]
    n, _, _, part, width = bk_ref.shape
    bk_ref[:, 0, 1] = ok_ref[:, 0]
    bs_ref[:, 0, 1] = os_ref[:, 0]
    for w, ref in enumerate((dq_ref, dk_ref, dv_ref)):
        rows = pad_rows(jnp.concatenate([ref[f] for f in range(frames)], 0), deep)
        for at, a_ref, b_ref in ((0, ak_ref, bk_ref), (D // 2, as_ref, bs_ref)):
            grad = dot(ht_ref[at : at + D // 2], rows).astype(bf16).reshape(n, part, width)
            if w < 2:
                a_ref[:, 0, w] = grad
            else:
                b_ref[:, 0, 0] = grad
        if w != 1:
            (sq_ref if w == 0 else sv_ref)[...] = jnp.sum(rows.astype(f32), 0, keepdims=True)


def project_grads(info, normed_t, grads, out_grads, attn):
    frames = grads[0].shape[0]
    n, z, _, part, width = attn[0].shape
    n = 2 * n
    block = pl.BlockSpec((frames, ROWS, width), lambda j, info_ref: (0, 0, j))
    spec = pl.BlockSpec((n, 1, 2, part, width), lambda j, info_ref: (0, j, 0, 0, 0))
    o_spec = pl.BlockSpec((n, 1, part, width), lambda j, info_ref: (0, j, 0, 0))
    row = pl.BlockSpec((1, width), lambda j, info_ref: (0, j))
    return call(
        project_grads_kernel,
        info,
        (normed_t, *grads, *out_grads),
        (z,),
        [once(*normed_t.shape)] + [block] * 3 + [o_spec] * 2,
        [spec] * 4 + [row] * 2,
        [shaped(bf16, n, z, 2, part, width)] * 4 + [shaped(f32, 1, D)] * 2,
        "project_grads",
        (),
        6 * frames * ROWS * D * D,
    )


def project_back_kernel(
    info_ref, x_ref, msg_ref, dmid_ref, gain_ref, dq_ref, dk_ref, dv_ref, *refs
):
    a_refs, b_refs, (ing_ref, dmsg_ref, sums_ref, total_ref) = refs[:4], refs[4:8], refs[8:]
    frames = x_ref.shape[0]
    j = pl.program_id(0)

    @pl.when(j == 0)
    def _():
        total_ref[...] = jnp.zeros_like(total_ref)

    weights = [halves(a_refs, 0, 0, 0), halves(a_refs, 0, 0, 1), halves(b_refs, 1, 0, 0)]
    for side in range(2):
        half = slice(side * D // 2, (side + 1) * D // 2)
        for f in range(frames):
            rows = jnp.zeros((ROWS, D // 2), f32)
            for ref, weight in zip((dq_ref, dk_ref, dv_ref), weights):
                rows += dot(ref[f], weight[side], NT)
            total_ref[f, :, half] += rows

    @pl.when(j == pl.num_programs(0) - 1)
    def _():
        gain_sum, shift_sum = jnp.zeros((1, D), f32), jnp.zeros((1, D), f32)
        for f in range(frames):
            rows = with_message(x_ref, msg_ref, info_ref, f)
            _, scaled, inverse = norm_rows(rows, 1.0, 0.0)
            grad = total_ref[f]
            gain_sum += jnp.sum(grad * scaled, 0, keepdims=True)
            shift_sum += jnp.sum(grad, 0, keepdims=True)
            back = norm_back(grad, scaled, inverse, gain_ref[...])
            ing_ref[f] = dmid_ref[f].astype(f32) + back
            dmsg_ref[f] = back[PATCHES : PATCHES + 1]
        sums_ref[...] = jnp.concatenate([gain_sum, shift_sum], 0)


def project_back(info, x, message, dmid, vec_rel, grads, attn):
    frames = x.shape[0]
    n, z, _, part, width = attn[0].shape
    block = pl.BlockSpec((frames, ROWS, width), lambda j, info_ref: (0, 0, j))
    a_spec = pl.BlockSpec((n, 1, 2, part, width), lambda j, info_ref: (0, j, 0, 0, 0))
    b_spec = pl.BlockSpec((n, 1, 1, part, width), lambda j, info_ref: (0, j, 0, 0, 0))
    return call(
        project_back_kernel,
        info,
        (x, message, dmid, vec_rel[0:1], *grads, *attn),
        (z,),
        [once(frames, ROWS, D), once(FRAMES, D), once(frames, ROWS, D), once(1, D)]
        + [block] * 3
        + [a_spec] * 4
        + [b_spec] * 4,
        [once(frames, ROWS, D), kept(frames, 1, D), kept(2, D)],
        [shaped(f32, frames, ROWS, D), shaped(f32, frames, 1, D), shaped(f32, 2, D)],
        "project_back",
        [pltpu.VMEM((frames, ROWS, D), f32)],
        6 * frames * ROWS * D * D,
    )


def message_halves(refs, which, i):
    part = D // (4 * refs[0].shape[0])
    return halves([ref.at[:, i * part : (i + 1) * part] for ref in refs], which)


def message_times(rows, refs, i):
    own, other = rows[:, : D // 2], rows[:, D // 2 :]
    cols = []
    for which in range(2):
        weights = message_halves(refs[4 * which : 4 * which + 4], which, i)
        cols.append(dot(own, weights[0]) + dot(other, weights[1]))
    return jnp.concatenate(cols, 1)


def message_times_t(rows, refs, i):
    left, right = rows[:, : D // 2], rows[:, D // 2 :]
    first, second = message_halves(refs[:4], 0, i), message_halves(refs[4:], 1, i)
    return jnp.concatenate(
        [dot(left, first[s], NT) + dot(right, second[s], NT) for s in range(2)], 1
    )


def by_head(rows):
    full = jnp.concatenate([rows.astype(f32)] * HEADS, 0)
    return jnp.where(head_mask(), full, 0.0).astype(bf16)


def head_mask():
    shape = (HEADS * FRAMES, D)
    head = lax.broadcasted_iota(jnp.int32, shape, 0) // FRAMES
    return head == lax.broadcasted_iota(jnp.int32, shape, 1) // HEAD


def over_heads(rows):
    rows = jnp.where(head_mask(), rows, 0.0)
    return jnp.sum(rows.reshape(HEADS, FRAMES, D), 0)


def message_probability(queries, keys):
    scores = dot(by_head(queries), keys, NT) * HEAD**-0.5
    shifted = jnp.exp(scores - jnp.max(scores, 1, keepdims=True))
    return shifted * (1.0 / jnp.sum(shifted, 1, keepdims=True))


def message_forward_kernel(info_ref, cls_ref, vec_ref, *refs):
    weights, (msg_ref, first_ref, pack_ref, hold_ref) = refs[:8], refs[8:]

    def relative(rows):
        hold_ref[...] = rows
        return permuted(hold_ref, info_ref, 0)

    first = message_times(relative(cls_ref[...]).astype(bf16), weights, 0) + vec_ref[6:7]
    normed = norm_rows(first, vec_ref[4:5], vec_ref[5:6])[0].astype(bf16).astype(f32)
    normed_rel = relative(normed).astype(bf16)
    queries = (message_times(normed_rel, weights, 1) + vec_ref[7:8]).astype(bf16)
    keys = message_times(normed_rel, weights, 2).astype(bf16)
    values = (message_times(normed_rel, weights, 3) + vec_ref[8:9]).astype(bf16)
    probability = message_probability(queries, keys).astype(bf16)
    mixed = over_heads(dot(probability, values)).astype(bf16).astype(f32)
    message = first + message_times(relative(mixed).astype(bf16), weights, 4) + vec_ref[9:10]
    msg_ref[...] = relative(message)
    first_ref[...] = first
    for i, rows in enumerate((normed, mixed, queries, keys, values)):
        pack_ref[i] = rows.astype(f32)


def message_forward(info, class_rows, vectors, weights):
    one = kept(FRAMES, D)
    return call(
        message_forward_kernel,
        info,
        (class_rows, vectors, *weights),
        (1,),
        [one, kept(*vectors.shape)] + [once(*w.shape) for w in weights],
        [one, one, kept(5, FRAMES, D)],
        [shaped(f32, FRAMES, D), shaped(f32, FRAMES, D), shaped(f32, 5, FRAMES, D)],
        "message_forward",
        [pltpu.VMEM((FRAMES, D), f32)],
        10 * FRAMES * D * D,
    )


def message_backward_kernel(info_ref, dmsg_ref, first_ref, pack_ref, vec_ref, *refs):
    weights, (class_ref, sent_ref, sums_ref, hold_ref) = refs[:8], refs[8:]
    frames = dmsg_ref.shape[1]
    for i in range(dmsg_ref.shape[0]):
        place = lax.bitwise_xor(info_ref[2 * BLOCKS], i)
        for f in range(frames):
            hold_ref[i * frames + f : i * frames + f + 1] = dmsg_ref[place, f : f + 1]
    dmsg = permuted(hold_ref, info_ref, BLOCKS)

    def plain(rows):
        hold_ref[...] = rows
        return permuted(hold_ref, info_ref, BLOCKS)

    queries, keys, values = (pack_ref[i].astype(bf16) for i in (2, 3, 4))
    grad_mixed = plain(message_times_t(dmsg.astype(bf16), weights, 4)).astype(bf16)
    probability = message_probability(queries, keys)
    grads_big = by_head(grad_mixed)
    grad_prob = dot(grads_big, values, NT)
    inner = jnp.sum(grad_prob * probability, 1, keepdims=True)
    grad_scores = (probability * (grad_prob - inner)).astype(bf16)
    dq = (over_heads(dot(grad_scores, keys)) * HEAD**-0.5).astype(bf16)
    dk = (dot(grad_scores, by_head(queries), TN) * HEAD**-0.5).astype(bf16)
    dv = dot(probability.astype(bf16), grads_big, TN).astype(bf16)
    grad = plain(
        message_times_t(dq, weights, 1)
        + message_times_t(dk, weights, 2)
        + message_times_t(dv, weights, 3)
    )
    _, scaled, inverse = norm_rows(first_ref[...], 1.0, 0.0)
    back = norm_back(grad, scaled, inverse, vec_ref[4:5])
    dfirst = (dmsg + back).astype(bf16)
    class_ref[...] = message_times_t(dfirst, weights, 0)
    sent = [rows.astype(f32) for rows in (dfirst, dq, dk, dv, dmsg)]
    for i, rows in enumerate(sent):
        sent_ref[i] = rows
    sums = [grad * scaled, grad, sent[0], sent[1], sent[3], dmsg]
    sums_ref[...] = jnp.concatenate([jnp.sum(rows, 0, keepdims=True) for rows in sums], 0)


def message_backward(info, dmsg, first, pack, vectors, weights):
    one = kept(FRAMES, D)
    return call(
        message_backward_kernel,
        info,
        (dmsg, first, pack, vectors, *weights),
        (1,),
        [kept(*dmsg.shape), one, kept(*pack.shape), kept(*vectors.shape)]
        + [once(*w.shape) for w in weights],
        [one, kept(5, FRAMES, D), kept(6, D)],
        [shaped(f32, FRAMES, D), shaped(f32, 5, FRAMES, D), shaped(f32, 6, D)],
        "message_backward",
        [pltpu.VMEM((FRAMES, D), f32)],
        10 * FRAMES * D * D,
    )


def relative_order():
    return lax.axis_size("dp") * BLOCK == D


def make_info():
    place = lax.iota(jnp.int32, BLOCKS)
    if relative_order():
        mine = lax.axis_index("dp")
        differs = place ^ mine
        places = mine ^ (2 * (place % 4) + place // 4)
        blocks = (differs % 2) * 4 + differs // 2
    else:
        places = blocks = place
    return jnp.concatenate([places, blocks, lax.axis_index("tensor")[None]]).astype(jnp.int32)


def swap(values, axis, bit):
    pairs = [(i, i ^ bit) for i in range(lax.axis_size(axis))]
    return lax.ppermute(values, axis, pairs)


def bits_of(axis):
    size = lax.axis_size(axis)
    return [1 << i for i in range(size.bit_length() - 1)]


def after(values, *earlier):
    return lax.optimization_barrier((values, earlier))[0]


def join_kernel(*refs):
    count = len(refs) // 3
    for i in range(count):
        out_ref = refs[2 * count + i]
        out_ref[0] = refs[2 * i][...]
        out_ref[1] = refs[2 * i + 1][...]


def join(*pairs):
    flat = [v.reshape(-1, v.shape[-1]) for pair in pairs for v in pair]
    specs = [pl.BlockSpec((v.shape[0] // 2, v.shape[1]), lambda i: (i, 0)) for v in flat]
    out = pl.pallas_call(
        join_kernel,
        grid=(2,),
        in_specs=specs,
        out_specs=[
            pl.BlockSpec((2, v.shape[0] // 2, v.shape[1]), lambda i: (0, i, 0)) for v in flat[::2]
        ],
        out_shape=[shaped(bf16, 2, *v.shape) for v in flat[::2]],
        compiler_params=pltpu.CompilerParams(vmem_limit_bytes=48 << 20),
        cost_estimate=cost(0, sum(2 * v.size for v in flat)),
        name="join",
    )(*flat)
    return [v.reshape((2,) + pair[0].shape) for v, pair in zip(out, pairs)]


class Gather:
    def __init__(self, *values):
        self.own, self.place = list(values), 0
        if relative_order():
            self.arrived = [swap(v, "dp", bit) for v, bit in zip(values, (2, 4))]
            return
        self.pieces = []
        for v in values:
            everything = lax.all_gather(v, "dp", axis=0)
            count = everything.shape[0] // 4
            self.pieces += [everything[i * count : (i + 1) * count] for i in range(4)]
        self.arrived = self.pieces

    def step(self):
        if not relative_order():
            return self.pieces
        self.place += 1
        if self.place == 1:
            self.own = join(*zip(self.own, self.arrived))
            self.arrived = [swap(v, "dp", bit) for v, bit in zip(self.own, (4, 2))]
            return self.own
        self.pieces = [v for pair in zip(self.own, self.arrived) for v in pair]
        self.arrived = [swap(v, "dp", 1) for v in self.pieces]
        return self.pieces

    def result(self):
        if not relative_order():
            return self.pieces
        return [v for i in (0, 2) for v in self.pieces[i : i + 2] + self.arrived[i : i + 2]]


def beside(outputs, *transfers):
    outputs, arrived = lax.optimization_barrier((outputs, [t.arrived for t in transfers]))
    for t, values in zip(transfers, arrived):
        t.arrived = values
    return outputs


def add_low(left_side, right_side):
    return (left_side.astype(f32) + right_side.astype(f32)).astype(bf16)


def add_kernel(axes, *refs):
    ins, outs = refs[: 2 * len(axes)], refs[2 * len(axes) :]
    for i, axis in enumerate(axes):
        for side in range(2):
            at = (side,) if axis == 0 else (slice(None), side)
            outs[2 * i + side][...] = add_low(ins[2 * i][at], ins[2 * i + 1][at])


def add_and_split(pairs, axes):
    lead = pairs[0][0].shape[:-2]
    rows, width = pairs[0][0].shape[-2:]
    steps = 4 if rows % 64 == 0 else 1
    zeros = (0,) * len(lead)
    spec = pl.BlockSpec((*lead, rows // steps, width), lambda i: (*zeros, i, 0))
    out = pl.BlockSpec((*lead[1:], rows // steps, width), lambda i: (*zeros[1:], i, 0))
    return pl.pallas_call(
        functools.partial(add_kernel, axes),
        grid=(steps,),
        in_specs=[spec] * (2 * len(pairs)),
        out_specs=[out] * (2 * len(pairs)),
        out_shape=[shaped(bf16, *lead[1:], rows, width)] * (2 * len(pairs)),
        compiler_params=pltpu.CompilerParams(vmem_limit_bytes=48 << 20),
        cost_estimate=cost(0, sum(4 * a.size for a, _ in pairs)),
        name="add",
    )(*[v for pair in pairs for v in pair])


class Scatter:
    def __init__(self, keep, send):
        self.place, self.shape = 0, keep[0].shape[1:]
        if not relative_order():
            self.held = [
                lax.psum_scatter(jnp.concatenate(v, 0), "dp", scatter_dimension=0, tiled=False)
                for v in zip(keep, send)
            ]
            self.arrived = [jnp.zeros_like(v) for v in self.held]
            return
        width = self.shape[-1]
        self.held = [v.reshape(2, 2, -1, width) for v in keep]
        self.arrived = [swap(v, "dp", 1).reshape(2, 2, -1, width) for v in send]

    def step(self):
        if not relative_order():
            return self.held
        axes, bits = ((0, 1), (4, 2)) if self.place == 0 else ((0, 0), (2, 4))
        self.place += 1
        sums = list(add_and_split(list(zip(self.held, self.arrived)), axes))
        self.held, going = sums[::2], sums[1::2]
        self.arrived = [swap(v, "dp", bit) for v, bit in zip(going, bits)]
        return going


def pair_kernel(info_ref, *refs):
    ins, outs = refs[:8], refs[8:]
    rows = ins[0].shape[1]
    for side in range(2):
        for i in range(2):
            total = add_low(ins[4 * i + side][0], ins[4 * i + 2 + side][0])
            outs[side][0, i * rows : (i + 1) * rows] = total


def add_and_pair(info, held, arrived):
    rows, width = held[0][0].size // held[0].shape[-1], held[0].shape[-1]
    own = pl.BlockSpec((1, rows, width), lambda h, ref: (2 * h + ref[2 * BLOCKS] % 2, 0, 0))
    other = pl.BlockSpec((1, rows, width), lambda h, ref: (2 * h + 1 - ref[2 * BLOCKS] % 2, 0, 0))
    flat = [v.reshape(4, rows, width) for pair in zip(held, arrived) for v in pair for _ in range(2)]
    out = pl.BlockSpec((1, 2 * rows, width), lambda h, ref: (h, 0, 0))
    return call(
        pair_kernel,
        info,
        flat,
        (2,),
        [own, other] * 4,
        [out] * 2,
        [shaped(bf16, 2, 2 * rows, width)] * 2,
        "add_and_pair",
    )


def single_kernel(info_ref, ho_ref, hp_ref, ao_ref, ap_ref, held_ref, going_ref):
    held_ref[...] = add_low(ho_ref[0], ao_ref[0])
    going_ref[...] = add_low(hp_ref[0], ap_ref[0])


def add_and_single(info, held, arrived):
    _, rows, width = held.shape
    own = pl.BlockSpec((1, rows, width), lambda i, ref: (ref[2 * BLOCKS] // 2, 0, 0))
    other = pl.BlockSpec((1, rows, width), lambda i, ref: (1 - ref[2 * BLOCKS] // 2, 0, 0))
    return call(
        single_kernel,
        info,
        (held, held, arrived, arrived),
        (1,),
        [own, other] * 2,
        [kept(rows, width)] * 2,
        [shaped(bf16, rows, width)] * 2,
        "add_and_single",
    )


class ScatterVideos:
    def __init__(self, info, sums):
        self.info, self.shape = info, sums.shape
        self.direct = lax.axis_size("tensor") != 4
        if self.direct:
            values = jnp.stack([add_low(h, a) for h, a in zip(sums.held, sums.arrived)], 1)
            self.held = lax.psum_scatter(values, "tensor", scatter_dimension=0, tiled=False)
            self.going, self.arrived = self.held, jnp.zeros_like(self.held)
            return
        held = [v.reshape(self.shape) for v in sums.held]
        arrived = [v.reshape(self.shape) for v in sums.arrived]
        self.held, self.going = add_and_pair(info, held, arrived)
        self.arrived = swap(self.going, "tensor", 1)

    def step(self):
        if self.direct:
            return self.held
        self.held, going = add_and_single(self.info, self.held, self.arrived)
        self.arrived = swap(going, "tensor", 2)
        return going

    def result(self):
        return add_low(self.held, self.arrived).reshape((2,) + self.shape[1:])


class GatherSmall:
    def __init__(self, values):
        self.values, self.bits = values[None], [2, 4, 1]
        if relative_order():
            self.arrived = swap(self.values, "dp", 2)
        else:
            self.values = self.arrived = lax.all_gather(values, "dp", axis=0)

    def step(self):
        if not relative_order():
            return self.values
        self.values = jnp.concatenate([self.values, self.arrived], 0)
        self.bits = self.bits[1:]
        if self.bits:
            self.arrived = swap(self.values, "dp", self.bits[0])
        return self.values


def sum_everywhere(values):
    for axis in ("dp", "tensor"):
        for bit in bits_of(axis):
            values = values + swap(values, axis, bit)
    return values


def gather_and_sum_videos(values, sums):
    values, count = values[None], sums.shape[0]
    for bit in bits_of("tensor"):
        rows = jnp.concatenate([sums, values.reshape(-1, D)], 0)
        arrived = swap(rows, "tensor", bit)
        sums = sums + arrived[:count]
        values = jnp.concatenate([values, arrived[count:].reshape(values.shape)], 0)
    return values, sums


def adam_step(weight, first_moment, second_moment, gradient, factor, step_rate, decay_rate):
    clipped = gradient * factor
    first_new = beta_one * first_moment + (1.0 - beta_one) * clipped
    second_new = beta_two * second_moment + (1.0 - beta_two) * clipped * clipped
    update = (
        first_new
        / (1.0 - beta_one**STEP)
        / (jnp.sqrt(second_new / (1.0 - beta_two**STEP)) + adam_eps)
    )
    weight_new = weight - step_rate * (update + decay_rate * weight)
    return (first_new, second_new, weight_new)


def on_device(
    tokens,
    cotangent,
    attn_master,
    attn_first,
    attn_second,
    attn_ema,
    mlp_master,
    mlp_first,
    mlp_second,
    mlp_ema,
    msg_master,
    msg_first,
    msg_second,
    msg_ema,
    vec_master,
    vec_first,
    vec_second,
    vec_ema,
):
    z_index = lax.axis_index("tensor")
    z_count = lax.axis_size("tensor")
    dp_index = lax.axis_index("dp")
    part = attn_master.shape[0]
    local_width = attn_master.shape[2]
    local_ff = mlp_master.shape[2]
    frames = tokens.shape[0] // PATCHES
    half_ff = local_ff // 2
    info = make_info()

    class_own = jnp.concatenate(
        [tokens[f * PATCHES : f * PATCHES + 1] for f in range(frames)], 0
    ).reshape(-1, local_width)
    attn_low = jnp.swapaxes(attn_master, 0, 1).astype(bf16).reshape(4 * part, local_width)
    attn_rows = pad_rows(jnp.concatenate([attn_low, class_own], 0), 4 * part + 16)
    attn_z = lax.all_gather(attn_rows, "tensor", axis=0)
    mlp_z = lax.all_gather(jnp.swapaxes(mlp_master, 0, 1).astype(bf16), "tensor", axis=0)
    class_rows = attn_z[:, 4 * part : 4 * part + class_own.shape[0]].reshape(FRAMES, D)
    attn_z = attn_z[:, : 4 * part].reshape(z_count, 4, part, local_width)

    msg_low = jnp.swapaxes(msg_master, 0, 1).astype(bf16).reshape(5 * part, D)
    vec_count = vec_master.shape[1]
    vec_low = jnp.pad(vec_master.astype(bf16).T, ((0, 32 - vec_count), (0, D // 2 - part)))
    msg_go = Gather(jnp.concatenate([msg_low[:, : D // 2], vec_low], 0), msg_low[:, D // 2 :])
    prepared = prepare(info, tokens, cotangent)
    x, grads, grads_t, grad_sum = beside(prepared, msg_go)
    sent_msg = msg_go.step()
    attn_z = after(attn_z, *sent_msg)
    attn_go = Gather(attn_z[:, :2], attn_z[:, 2:])
    sent_attn = attn_go.step()
    beside(sent_attn, msg_go)
    sent_msg = msg_go.step()
    mlp_z = after(mlp_z, *sent_msg)
    mlp_go = [
        Gather(*[mlp_z[:, i, :, j * half_ff : (j + 1) * half_ff] for i in range(2)])
        for j in range(2)
    ]
    msg_w = msg_go.result()
    vec_rel = jnp.concatenate(msg_w[:4], 0)[:, 5 * part : 5 * part + vec_count, :part]
    vec_rel = jnp.moveaxis(vec_rel, 0, 1).reshape(-1, D).astype(f32)
    vectors = plain_order(info, vec_rel)
    ff_bias = vectors[14:].reshape(z_count, 2, half_ff)

    sent_mlp = mlp_go[0].own + mlp_go[1].own
    message, first_msg, msg_pack = beside(
        message_forward(info, after(class_rows, *sent_mlp).astype(f32), vectors, msg_w), attn_go
    )
    attn_go.step()
    attn_w = attn_go.result()
    projected = project(info, x, message, vec_rel, vectors, attn_w)
    queries, key_rows, value_rows, normed_t = beside(projected, *mlp_go)
    sent_mlp = mlp_go[0].step() + mlp_go[1].step()
    attended, totals = beside(
        attend_forward(after(queries, *sent_mlp), key_rows, value_rows), mlp_go[0]
    )
    sent_mlp = mlp_go[0].step()
    middle, n2, n2_t = beside(
        combine(info, x, after(attended, *sent_mlp), vec_rel, attn_w), mlp_go[1]
    )
    sent_mlp = mlp_go[1].step()
    n2 = after(n2, *sent_mlp)

    def feed(j, n2):
        return feed_forward(n2, n2_t, grads, grads_t, ff_bias[:, j], mlp_go[j].result())

    out_0, dn2_0, *dw_0, db_0 = beside(feed(0, n2), mlp_go[1])
    sums_0 = Scatter(dw_0[::2], dw_0[1::2])
    out_1, dn2_1, *dw_1, db_1 = beside(feed(1, after(n2, db_0)), sums_0)
    sums_1 = Scatter(dw_1[::2], dw_1[1::2])
    going = sums_0.step()
    dmid, grad_attended, *grad_out_w, sums_two = beside(
        between(info, after(dn2_0, *going), dn2_1, middle, grads, attended, vec_rel, attn_w), sums_1
    )
    going = sums_1.step()
    pairs = HEADS // 2
    back = (queries, key_rows, value_rows, totals)
    grad_qkv = beside(
        attend_backward(*back, after(grad_attended, *going), 0, pairs // 2), sums_0
    )
    going = sums_0.step()
    grad_qkv = beside(
        attend_backward(
            *back, after(grad_attended, *going), pairs // 2, pairs - pairs // 2, grad_qkv
        ),
        sums_0,
        sums_1,
    )
    going = sums_1.step()
    mlp_0 = ScatterVideos(info, sums_0)
    dqk_keep, dqk_send, dvo_keep, dvo_send, sum_q, sum_v = beside(
        project_grads(
            info, after(normed_t, mlp_0.going, *going), grad_qkv, grad_out_w, attn_w
        ),
        sums_1,
        mlp_0,
    )
    sums_attn = Scatter([dqk_keep, dvo_keep], [dqk_send, dvo_send])
    going = mlp_0.step()
    mlp_1 = ScatterVideos(info, sums_1)
    block_output = beside(
        finish(
            info,
            [after(middle, going, mlp_1.going), out_0, out_1],
            vec_rel[13:14],
            "block_output",
        ),
        sums_attn,
        mlp_0,
        mlp_1,
    )
    going = sums_attn.step()
    going.append(mlp_1.step())
    mlp_0 = mlp_0.result()
    ing, dmsg, sums_one = beside(
        project_back(info, after(x, mlp_0, *going), message, dmid, vec_rel, grad_qkv, attn_w),
        sums_attn,
        mlp_1,
    )
    going = sums_attn.step()
    mlp_1 = mlp_1.result()

    ff_bias_grad = jnp.stack(
        [db.reshape(z_count, half_ff) for db in (db_0, db_1)], 1
    ).reshape(FF // D, D)
    table = jnp.concatenate([sums_one, sums_two, grad_sum, sum_q, sum_v, ff_bias_grad], 0)
    dmsg = dmsg[:, 0].astype(bf16).astype(f32)
    dmsg, table = beside(
        gather_and_sum_videos(after(dmsg, mlp_1, *going), table), sums_attn
    )
    attn_go = ScatterVideos(info, sums_attn)
    grad_class, sent, sums_msg = beside(
        message_backward(info, after(dmsg, attn_go.going), first_msg, msg_pack, vectors, msg_w),
        attn_go,
    )
    going = attn_go.step()

    plain = plain_order(info, table[:6])
    table = jnp.concatenate([plain[:4], sums_msg, table[6:8], plain[4:], table[8:]], 0)
    sent = jnp.concatenate([msg_pack[:2], sent], 0).astype(bf16).reshape(7 * FRAMES, D)
    sent = jnp.concatenate([class_rows, sent, table.astype(bf16)], 0)
    small = GatherSmall(after(sent, going))
    middle_block = BLOCKS // 2
    input_grad = beside(
        finish(info, [after(ing, small.values)], grad_class, "input_grad", 0, middle_block), small
    )
    rows = small.step()
    input_grad = beside(
        finish(
            info,
            [after(ing, rows)],
            grad_class,
            "input_grad",
            middle_block,
            BLOCKS - middle_block,
            [input_grad],
        ),
        small,
        attn_go,
    )
    small.step()
    attn_grad = attn_go.result()
    everyone = small.step()
    tables = lax.dynamic_slice_in_dim(everyone[:, 8 * FRAMES :], dp_index * part, part, 2)
    vec_grad = jnp.sum(tables.astype(f32), 0).T
    everyone = everyone[:, : 8 * FRAMES].reshape(-1, 8, FRAMES, D)
    everyone = jnp.moveaxis(everyone, 0, 1).reshape(8, -1, D)
    mine = lax.dynamic_slice_in_dim(everyone[:3], dp_index * part, part, 2)
    msg_grad = jnp.stack(
        [
            dot(mine[0], everyone[3], TN),
            dot(mine[1], everyone[4], TN),
            dot(mine[1], everyone[5], TN),
            dot(mine[1], everyone[6], TN),
            dot(mine[2], everyone[7], TN),
        ],
        1,
    )

    attn_grad = jnp.swapaxes(attn_grad.reshape(4, part, local_width), 0, 1).astype(f32)
    mlp_grad = jnp.swapaxes(jnp.concatenate([mlp_0, mlp_1], 2), 0, 1).astype(f32)

    keep_share = (z_index == 0).astype(f32)
    squares = (
        jnp.sum(attn_grad * attn_grad)
        + jnp.sum(mlp_grad * mlp_grad)
        + keep_share * (jnp.sum(msg_grad * msg_grad) + jnp.sum(vec_grad * vec_grad))
    )
    squares = sum_everywhere(jnp.broadcast_to(squares, (8, 128)))[0, 0]
    grad_norm = jnp.sqrt(squares)
    factor = clip_limit / jnp.maximum(grad_norm, clip_limit)

    def update(master, first, second, ema, grad, rate, decay):
        first_new, second_new, weight = adam_step(master, first, second, grad, factor, rate, decay)
        return grad, first_new, second_new, weight, ema_keep * ema + (1.0 - ema_keep) * weight

    return (
        block_output,
        input_grad,
        grad_norm,
        *update(attn_master, attn_first, attn_second, attn_ema, attn_grad, rate_mat, decay_mat),
        *update(mlp_master, mlp_first, mlp_second, mlp_ema, mlp_grad, rate_mat, decay_mat),
        *update(msg_master, msg_first, msg_second, msg_ema, msg_grad, rate_mat, decay_mat),
        *update(vec_master, vec_first, vec_second, vec_ema, vec_grad, rate_vec, 0.0),
    )


def solution(mesh):
    rows = P(("dp", "tensor"), None)
    split = P("dp", None, "tensor")
    copied = P("dp", None, None)
    table = P("dp", None)
    in_specs = (rows,) * 2 + (split,) * 8 + (copied,) * 4 + (table,) * 4
    out_specs = (rows,) * 2 + (P(),) + (split,) * 10 + (copied,) * 5 + (table,) * 5
    return jax.shard_map(
        on_device, mesh=mesh, in_specs=in_specs, out_specs=out_specs, check_vma=False
    )
```

```python
import functools

import jax
import jax.numpy as jnp
from jax import lax
from jax.experimental import pallas as pl
from jax.experimental.pallas import tpu as pltpu
from jax.sharding import PartitionSpec as P

D = 1024
HEADS = 16
HEAD = 64
FF = 4096
PATCHES = 577
FRAMES = 8
STEP = 10
ROWS = 592


norm_eps = 1e-05
beta_one = 0.9
beta_two = 0.95
adam_eps = 1e-08
decay_mat = 0.05
ema_keep = 0.7
clip_limit = 1.0
rate_mat = 0.02
rate_vec = 0.4
far_below = -1e30
COST_PART = 16
bf16 = jnp.bfloat16
f32 = jnp.float32
NN = (((1,), (0,)), ((), ()))
NT = (((1,), (1,)), ((), ()))
TN = (((0,), (0,)), ((), ()))


def dot(left_side, right_side, dims=NN):
    return lax.dot_general(left_side, right_side, dims, preferred_element_type=f32)


def norm_rows(values, gain_row, shift_row):
    centre = values - jnp.mean(values, -1, keepdims=True)
    spread = jnp.mean(centre * centre, -1, keepdims=True)
    inverse = lax.rsqrt(spread + norm_eps)
    scaled = centre * inverse
    return (scaled * gain_row + shift_row, scaled, inverse)


def norm_back(gradient, scaled, inverse, gain_row):
    inner = gradient * gain_row
    return inverse * (
        inner
        - jnp.mean(inner, -1, keepdims=True)
        - scaled * jnp.mean(inner * scaled, -1, keepdims=True)
    )


def pad_rows(values, count):
    if values.shape[0] == count:
        return values
    extra = jnp.zeros((count - values.shape[0],) + values.shape[1:], values.dtype)
    return jnp.concatenate([values, extra], 0)


def head_pair(queries, key_rows, head):
    lane = lax.broadcasted_iota(jnp.int32, queries.shape, 1)
    key_lane = lax.broadcasted_iota(jnp.int32, key_rows.shape, 1)
    key_row = lax.broadcasted_iota(jnp.int32, key_rows.shape, 0)
    spare = HEAD * (1 - head)
    mask = jnp.where(
        (key_lane == spare) & (key_row > PATCHES), jnp.asarray(far_below, bf16), jnp.asarray(0, bf16)
    )
    keys_one = jnp.where((key_lane // HEAD) == head, key_rows, mask)
    queries_one = jnp.where(lane == spare, jnp.asarray(1, bf16), queries)
    return queries_one, keys_one


def each_head(values):
    lane = lax.broadcasted_iota(jnp.int32, values.shape, 1)
    zero = jnp.zeros_like(values)
    return jnp.concatenate(
        [jnp.where(lane < HEAD, values, zero), jnp.where(lane < HEAD, zero, values)], 0
    )


def attend_forward_kernel(q_ref, k_ref, v_ref, out_ref, total_ref):
    rows, width = q_ref.shape[1:]
    key_count = -(-rows // 128) * 128
    lane = lax.broadcasted_iota(jnp.int32, (rows, 128), 1)
    out_of = lax.broadcasted_iota(jnp.int32, (rows, 128), 1) > PATCHES - (key_count - 128)
    pairs = width // 128

    def score(pair):
        lanes = slice(pair * 128, (pair + 1) * 128)
        queries = q_ref[0, :, lanes] * jnp.asarray(HEAD**-0.5, bf16)
        return dot(queries, each_head(pad_rows(k_ref[0, :, lanes], key_count)), NT)

    waiting = [score(0)]
    for pair in range(pairs):
        if pair + 1 < pairs:
            waiting.append(score(pair + 1))
        both = waiting.pop(0)
        shares, totals, sums = [], [], []
        for head in range(2):
            scores = both[:, head * key_count : (head + 1) * key_count]
            tail = jnp.where(out_of, far_below, scores[:, key_count - 128 :])
            scores = jnp.concatenate([scores[:, : key_count - 128], tail], 1)
            highest = jnp.max(scores, 1, keepdims=True)
            shifted = jnp.exp(scores - highest)
            total = jnp.sum(shifted, 1, keepdims=True)
            shares.append(shifted.astype(bf16))
            sums.append(1.0 / total)
            totals.append(highest + jnp.log(total))
        lanes = slice(pair * 128, (pair + 1) * 128)
        out = dot(jnp.concatenate(shares, 1), each_head(pad_rows(v_ref[0, :, lanes], key_count)))
        out_ref[0, :, lanes] = (out * jnp.where(lane < HEAD, *sums)).astype(bf16)
        logs = jnp.where(lane < HEAD, *totals).T
        total_ref[0, pair] = jnp.concatenate([logs[0:1], logs[HEAD : HEAD + 1]], 0)


def attend_backward_kernel(q_ref, k_ref, v_ref, total_ref, grad_ref, *rest):
    dq_ref, dk_ref, dv_ref = rest[-3:]
    rows, width = q_ref.shape[1:]
    count = -(-rows // 128) * 128
    pairs = width // 128
    tail = rows // 16 * 16 - 16
    out_of = lax.broadcasted_iota(jnp.int32, (rows - tail, count), 0) > PATCHES - tail

    def swapped(values):
        return jnp.concatenate([values[:, HEAD:], values[:, :HEAD]], 1)

    def load(pair):
        lanes = slice(pair * 128, (pair + 1) * 128)
        queries = pad_rows(q_ref[0, :, lanes], count) * jnp.asarray(HEAD**-0.5, bf16)
        return lanes, queries, pad_rows(grad_ref[0, :, lanes], count)

    def start(pair):
        lanes, queries, grads = load(pair)
        keys, values = k_ref[0, :, lanes], swapped(v_ref[0, :, lanes])
        first = lax.broadcasted_iota(jnp.int32, (rows, 128), 1) < HEAD
        queries, grads = each_head(queries), each_head(swapped(grads))
        products = []
        for head in range(2):
            mixed = jnp.where(first, keys, values) if head == 0 else jnp.where(first, values, keys)
            right = [
                queries[head * count : (head + 1) * count],
                grads[(1 - head) * count : (2 - head) * count],
            ]
            products.append(dot(mixed, jnp.concatenate(right, 0), NT))
        return products

    waiting = [start(0)]
    for pair in range(pairs):
        if pair + 1 < pairs:
            waiting.append(start(pair + 1))
        products = waiting.pop(0)
        lanes, queries, grads = load(pair)
        shares, grad_scores = [], []
        for head in range(2):
            total = total_ref[0, pair, head : head + 1, :]
            total = jnp.concatenate([total, jnp.zeros((1, count - rows), f32)], 1)
            share = jnp.exp(products[head][:, :count] - total)
            share = jnp.concatenate([share[:tail], jnp.where(out_of, 0.0, share[tail:])], 0)
            grad_share = products[head][:, count:]
            inner = jnp.sum(grad_share * share, 0, keepdims=True)
            grad_scores.append((share * (grad_share - inner)).astype(bf16))
            shares.append(share.astype(bf16))
        dv_ref[0, :, lanes] = dot(jnp.concatenate(shares, 1), each_head(grads)).astype(bf16)
        dk_ref[0, :, lanes] = dot(jnp.concatenate(grad_scores, 1), each_head(queries)).astype(bf16)
        keys_t = pad_rows(k_ref[0, :, lanes], count).astype(f32).T.astype(bf16)
        back = [
            dot(keys_t[HEAD * head : HEAD * (head + 1)], pad_rows(grad_scores[head], count))
            for head in range(2)
        ]
        dq_ref[0, :, lanes] = (jnp.concatenate(back, 0) * HEAD**-0.5).T[:rows].astype(bf16)


def cost(flops, moved):
    return pl.CostEstimate(
        flops=flops // COST_PART, bytes_accessed=moved // COST_PART, transcendentals=0
    )


def attend_cost(frames, rows, width, matmuls):
    return cost(2 * matmuls * frames * rows * rows * width, 4 * matmuls * frames * rows * width)


def attend_forward(queries, key_rows, value_rows):
    frames, rows, width = queries.shape
    spec = pl.BlockSpec((1, rows, width), lambda f: (f, 0, 0))
    return pl.pallas_call(
        attend_forward_kernel,
        grid=(frames,),
        in_specs=[spec] * 3,
        out_specs=[spec, pl.BlockSpec((1, width // 128, 2, rows), lambda f: (f, 0, 0, 0))],
        out_shape=[
            jax.ShapeDtypeStruct((frames, rows, width), bf16),
            jax.ShapeDtypeStruct((frames, width // 128, 2, rows), f32),
        ],
        compiler_params=pltpu.CompilerParams(vmem_limit_bytes=48 << 20),
        cost_estimate=attend_cost(frames, rows, width, 4),
        name="attend_forward",
    )(queries, key_rows, value_rows)


def attend_backward(queries, key_rows, value_rows, totals, grads, begin, count, earlier=()):
    frames, rows, width = queries.shape
    at = begin // count
    spec = pl.BlockSpec((1, rows, 128 * count), lambda f: (f, 0, at))
    total_spec = pl.BlockSpec((1, count, 2, rows), lambda f: (f, at, 0, 0))
    return pl.pallas_call(
        attend_backward_kernel,
        grid=(frames,),
        in_specs=[spec] * 3 + [total_spec, spec] + [pl.BlockSpec(memory_space=pl.ANY)] * len(earlier),
        out_specs=[spec] * 3,
        out_shape=[jax.ShapeDtypeStruct((frames, rows, width), bf16)] * 3,
        input_output_aliases={5 + i: i for i in range(len(earlier))},
        compiler_params=pltpu.CompilerParams(vmem_limit_bytes=48 << 20),
        cost_estimate=attend_cost(frames, rows, count * 128, 8),
        name="attend_backward",
    )(queries, key_rows, value_rows, totals, grads, *earlier)


def feed_kernel(
    n2_ref,
    n2t_ref,
    g_ref,
    gt_ref,
    bias_ref,
    *refs,
):
    up_refs, down_refs = refs[:4], refs[4:8]
    out_ref, dn2_ref, dup_own_ref, dup_other_ref, ddown_own_ref, ddown_other_ref = refs[8:14]
    db_ref, act_ref, dpre_ref = refs[14:]
    frames, rows = n2_ref.shape[:2]
    blocks, _, part, chunk = dup_own_ref.shape
    half = blocks * part

    @pl.when(pl.program_id(0) == 0)
    def _():
        out_ref[...] = jnp.zeros_like(out_ref)
        dn2_ref[...] = jnp.zeros_like(dn2_ref)
        act_ref[...] = jnp.zeros_like(act_ref)
        dpre_ref[...] = jnp.zeros_like(dpre_ref)

    first = jnp.concatenate(halves(up_refs, 0, 0), 0)
    second = jnp.concatenate(halves(down_refs, 1, 0), 0)
    bias_sum = jnp.zeros((1, chunk), f32)
    for frame in range(frames):
        place = pl.ds(frame * FRAME_LANES, rows)
        pre = dot(n2_ref[frame], first) + bias_ref[0]
        sigma = 0.5 + 0.5 * jnp.tanh(0.851 * pre)
        act = (pre * sigma).astype(bf16)
        act_ref[place] = act
        out_ref[frame] += dot(act, second, NT)
        grad_act = dot(g_ref[frame], second)
        grad_pre = grad_act * (sigma * (1.0 + 1.702 * pre * (1.0 - sigma)))
        grad_low = grad_pre.astype(bf16)
        dpre_ref[place] = grad_low
        bias_sum += jnp.sum(grad_low.astype(f32), 0, keepdims=True)
        dn2_ref[frame] += dot(grad_low, first, NT)
    db_ref[0] = bias_sum

    def place_grad(left_ref, right_ref, own_ref, other_ref):
        grad = dot(left_ref[...], right_ref[...]).astype(bf16)
        own_ref[:, 0] = grad[:half].reshape(blocks, part, chunk)
        other_ref[:, 0] = grad[half:].reshape(blocks, part, chunk)

    place_grad(n2t_ref, dpre_ref, dup_own_ref, dup_other_ref)
    place_grad(gt_ref, act_ref, ddown_own_ref, ddown_other_ref)


def feed_forward(n2, n2t, grads, grads_t, bias, weights):
    frames, rows, _ = n2.shape
    blocks, ff_blocks, part, local = weights[0].shape
    blocks = 2 * blocks
    chunk = min(512, local)
    per = local // chunk
    steps = ff_blocks * per
    deep = n2t.shape[1]
    whole3 = lambda n: (0, 0, 0)
    whole2 = lambda n: (0, 0)
    single = pl.Buffered(1)
    w_spec = pl.BlockSpec((blocks // 2, 1, part, chunk), lambda n: (0, n // per, 0, n % per))
    dw_spec = pl.BlockSpec((blocks, 1, part, chunk), lambda n: (0, n // per, 0, n % per))
    dw_shape = jax.ShapeDtypeStruct((blocks, ff_blocks, part, local), bf16)
    return pl.pallas_call(
        feed_kernel,
        grid=(steps,),
        in_specs=[
            pl.BlockSpec((frames, rows, D), whole3, pipeline_mode=single),
            pl.BlockSpec((D, deep), whole2, pipeline_mode=single),
            pl.BlockSpec((frames, rows, D), whole3, pipeline_mode=single),
            pl.BlockSpec((D, deep), whole2, pipeline_mode=single),
            pl.BlockSpec((1, 1, chunk), lambda n: (n, 0, 0)),
        ]
        + [w_spec] * 8,
        out_specs=[pl.BlockSpec((frames, rows, D), whole3)] * 2
        + [dw_spec] * 4
        + [pl.BlockSpec((1, 1, chunk), lambda n: (n, 0, 0))],
        out_shape=[jax.ShapeDtypeStruct((frames, rows, D), f32)] * 2
        + [dw_shape] * 4
        + [jax.ShapeDtypeStruct((steps, 1, chunk), f32)],
        scratch_shapes=[pltpu.VMEM((deep, chunk), bf16), pltpu.VMEM((deep, chunk), bf16)],
        compiler_params=pltpu.CompilerParams(vmem_limit_bytes=60 << 20),
        cost_estimate=cost(
            12 * frames * rows * D * ff_blocks * local,
            8 * D * ff_blocks * local + 16 * frames * rows * D,
        ),
        name="feed_forward",
    )(n2, n2t, grads, grads_t, bias.reshape(steps, 1, chunk), *weights)


BLOCK = 128
BLOCKS = D // BLOCK


def permuted(ref, info_ref, first):
    return jnp.concatenate(
        [
            ref[:, pl.ds(pl.multiple_of(info_ref[first + i] * BLOCK, BLOCK), BLOCK)]
            for i in range(BLOCKS)
        ],
        1,
    )


def call(
    kernel, info, args, grid, in_specs, out_specs, out_shape, name, scratch=(), flops=0, vmem=56, aliases=None
):
    moved = sum(a.size * a.dtype.itemsize for a in args)
    moved += sum(o.size * o.dtype.itemsize for o in out_shape)
    return pl.pallas_call(
        kernel,
        grid_spec=pltpu.PrefetchScalarGridSpec(
            num_scalar_prefetch=1,
            grid=grid,
            in_specs=in_specs,
            out_specs=out_specs,
            scratch_shapes=list(scratch),
        ),
        out_shape=out_shape,
        input_output_aliases=aliases or {},
        compiler_params=pltpu.CompilerParams(vmem_limit_bytes=vmem << 20),
        cost_estimate=cost(flops, moved),
        name=name,
    )(info, *args)


def shaped(dtype, *shape):
    return jax.ShapeDtypeStruct(shape, dtype)


def once(*block, at=None):
    index = at or (0,) * len(block)
    return pl.BlockSpec(block, lambda *_: index, pipeline_mode=pl.Buffered(1))


def kept(*block):
    index = (0,) * len(block)
    return pl.BlockSpec(block, lambda *_: index)


FRAME_LANES = -(-ROWS // 128) * 128


def row_count(frames):
    return frames * FRAME_LANES


def prepare_kernel(info_ref, tokens_ref, cot_ref, x_ref, g_ref, gt_ref, gsum_ref, hold_ref):
    frames = x_ref.shape[0]
    count = tokens_ref.shape[0]
    inside = lax.broadcasted_iota(jnp.int32, (ROWS, BLOCK), 0) < PATCHES
    hold_ref[...] = jnp.zeros_like(hold_ref)

    def padded(ref):
        hold_ref[0:count] = ref[...].astype(f32)
        return [
            jnp.where(inside, hold_ref[pl.ds(f * PATCHES, ROWS)], 0.0) for f in range(frames)
        ]

    for f, rows in enumerate(padded(tokens_ref)):
        x_ref[f] = rows.astype(bf16)
    grads = padded(cot_ref)
    for f, rows in enumerate(grads):
        g_ref[f] = rows.astype(bf16)
    full = jnp.concatenate([pad_rows(rows, FRAME_LANES) for rows in grads], 0)
    gt_ref[...] = full.T.astype(bf16)
    gsum_ref[...] = jnp.sum(full, 0, keepdims=True)


def prepare(info, tokens, cotangent):
    count = tokens.shape[0]
    frames = count // PATCHES
    deep = row_count(frames)
    taken = pl.BlockSpec((count, BLOCK), lambda r, info_ref: (0, info_ref[r]))
    placed = pl.BlockSpec((frames, ROWS, BLOCK), lambda r, info_ref: (0, 0, r))
    return call(
        prepare_kernel,
        info,
        (tokens, cotangent),
        (BLOCKS,),
        [taken] * 2,
        [
            placed,
            placed,
            pl.BlockSpec((BLOCK, deep), lambda r, info_ref: (r, 0)),
            pl.BlockSpec((1, BLOCK), lambda r, info_ref: (0, r)),
        ],
        [
            shaped(bf16, frames, ROWS, D),
            shaped(bf16, frames, ROWS, D),
            shaped(bf16, D, deep),
            shaped(f32, 1, D),
        ],
        "prepare",
        [pltpu.VMEM((-(-((frames - 1) * PATCHES + ROWS) // 8) * 8, BLOCK), f32)],
    )


def plain_order_kernel(info_ref, in_ref, out_ref):
    out_ref[...] = permuted(in_ref, info_ref, BLOCKS)


def plain_order(info, values):
    return call(
        plain_order_kernel,
        info,
        (values,),
        (1,),
        [kept(*values.shape)],
        [kept(*values.shape)],
        [shaped(f32, *values.shape)],
        "plain_order",
    )[0]


def finish_kernel(count, info_ref, *refs):
    in_refs, row_ref, out_ref = refs[:count], refs[count], refs[-1]
    frames = in_refs[0].shape[0]
    for f in range(frames):
        rows = in_refs[0][f]
        for ref in in_refs[1:]:
            rows = rows + ref[f]
        if row_ref.shape[0] == 1:
            rows = rows + row_ref[...]
        else:
            class_row = row_ref[pl.ds(info_ref[2 * BLOCKS] * frames + f, 1)]
            first = lax.broadcasted_iota(jnp.int32, (ROWS, BLOCK), 0) == 0
            rows = rows + jnp.where(first, class_row, 0.0)
        out_ref[pl.ds(f * PATCHES, PATCHES)] = rows[:PATCHES]


def finish(info, parts, row, name, begin=0, count=BLOCKS, earlier=()):
    frames = parts[0].shape[0]
    at = lambda d, info_ref: info_ref[BLOCKS + begin + d]
    taken = pl.BlockSpec((frames, ROWS, BLOCK), lambda d, info_ref: (0, 0, at(d, info_ref)))
    row_spec = pl.BlockSpec((row.shape[0], BLOCK), lambda d, info_ref: (0, at(d, info_ref)))
    return call(
        functools.partial(finish_kernel, len(parts)),
        info,
        (*parts, row, *earlier),
        (count,),
        [taken] * len(parts) + [row_spec] + [pl.BlockSpec(memory_space=pl.ANY)] * len(earlier),
        [pl.BlockSpec((frames * PATCHES, BLOCK), lambda d, info_ref: (0, begin + d))],
        [shaped(f32, frames * PATCHES, D)],
        name,
        aliases={len(parts) + 2: 0} if earlier else {},
    )[0]


def with_message(x_ref, msg_ref, info_ref, f):
    frames = x_ref.shape[0]
    message = msg_ref[pl.ds(info_ref[2 * BLOCKS] * frames + f, 1)]
    place = lax.broadcasted_iota(jnp.int32, (ROWS, D), 0) == PATCHES
    return jnp.where(place, message, x_ref[f].astype(f32))


def put_transposed(ref, rows, f):
    for c in range(BLOCKS):
        block = pad_rows(rows[:, c * BLOCK : (c + 1) * BLOCK].astype(f32), FRAME_LANES)
        place = slice(f * FRAME_LANES, (f + 1) * FRAME_LANES)
        ref[c * BLOCK : (c + 1) * BLOCK, place] = block.T.astype(bf16)


def halves(refs, which, *at):
    sides = []
    for pair in (refs[:2], refs[2:]):
        first, second = (ref[(slice(None), *at)] for ref in pair)
        part, width = first.shape[-2:]
        if which and part == BLOCK:
            blocks = [first[0], second[0], first[1], second[1]]
        else:
            blocks = [v.reshape(-1, width) for v in (first, second)]
        sides.append(jnp.concatenate(blocks, 0))
    return sides


def project_kernel(
    info_ref, x_ref, msg_ref, gain_ref, shift_ref, bq_ref, bv_ref, *refs
):
    a_refs, b_refs, (q_ref, k_ref, v_ref, h_ref) = refs[:4], refs[4:8], refs[8:]
    frames = x_ref.shape[0]

    @pl.when(pl.program_id(0) == 0)
    def _():
        for f in range(frames):
            rows = with_message(x_ref, msg_ref, info_ref, f)
            normed = norm_rows(rows, gain_ref[...], shift_ref[...])[0].astype(bf16)
            h_ref[pl.ds(f * ROWS, ROWS)] = normed

    for out_ref, weights, bias in (
        (q_ref, halves(a_refs, 0, 0, 0), bq_ref[...]),
        (k_ref, halves(a_refs, 0, 0, 1), 0.0),
        (v_ref, halves(b_refs, 1, 0, 0), bv_ref[...]),
    ):
        rows = dot(h_ref[...], jnp.concatenate(weights, 0)) + bias
        for f in range(frames):
            out_ref[f] = rows[f * ROWS : (f + 1) * ROWS].astype(bf16)


def project(info, x, message, vec_rel, vectors, attn):
    frames = x.shape[0]
    n, z, _, part, width = attn[0].shape
    bias = pl.BlockSpec((1, width), lambda j, info_ref: (0, j))
    a_spec = pl.BlockSpec((n, 1, 2, part, width), lambda j, info_ref: (0, j, 0, 0, 0))
    b_spec = pl.BlockSpec((n, 1, 1, part, width), lambda j, info_ref: (0, j, 0, 0, 0))
    out = pl.BlockSpec((frames, ROWS, width), lambda j, info_ref: (0, 0, j))
    return call(
        project_kernel,
        info,
        (x, message, vec_rel[0:1], vec_rel[1:2], vectors[10:11], vectors[11:12], *attn),
        (z,),
        [once(frames, ROWS, D), once(FRAMES, D), once(1, D), once(1, D), bias, bias]
        + [a_spec] * 4
        + [b_spec] * 4,
        [out] * 3 + [kept(frames * ROWS, D)],
        [shaped(bf16, frames, ROWS, D)] * 3 + [shaped(bf16, frames * ROWS, D)],
        "project",
        (),
        6 * frames * ROWS * D * D,
    )


def transpose_kernel(info_ref, in_ref, out_ref):
    put_transposed(out_ref, in_ref[...], 0)


def transposed(info, rows):
    frames = rows.shape[0] // ROWS
    return call(
        transpose_kernel,
        info,
        (rows,),
        (frames,),
        [pl.BlockSpec((ROWS, D), lambda f, info_ref: (f, 0))],
        [pl.BlockSpec((D, FRAME_LANES), lambda f, info_ref: (0, f))],
        [shaped(bf16, D, row_count(frames))],
        "transposed",
    )[0]


def combine_kernel(
    info_ref, x_ref, a_ref, bias_ref, gain_ref, shift_ref, *refs
):
    b_refs, (mid_ref, n2_ref, n2t_ref) = refs[:4], refs[4:]
    weight = whole_out(b_refs)
    middle = x_ref[0].astype(f32) + bias_ref[...] + dot(a_ref[0], weight, NT)
    mid_ref[0] = middle
    low = middle.astype(bf16).astype(f32)
    normed = norm_rows(low, gain_ref[...], shift_ref[...])[0].astype(bf16)
    n2_ref[0] = normed
    put_transposed(n2t_ref, normed, 0)


def whole_out(b_refs):
    parts = [jnp.concatenate(halves(b_refs, 1, j, 0), 0) for j in range(b_refs[0].shape[1])]
    return jnp.concatenate(parts, 1)


def combine(info, x, attended, vec_rel, attn):
    frames = x.shape[0]
    n, z, _, part, width = attn[4].shape
    frame = pl.BlockSpec((1, ROWS, D), lambda f, info_ref: (f, 0, 0))
    weight = once(n, z, 1, part, width, at=(0, 0, 1, 0, 0))
    return call(
        combine_kernel,
        info,
        (x, attended, vec_rel[12:13], vec_rel[2:3], vec_rel[3:4], *attn[4:]),
        (frames,),
        [frame] * 2 + [once(1, D)] * 3 + [weight] * 4,
        [frame, frame, pl.BlockSpec((D, FRAME_LANES), lambda f, info_ref: (0, f))],
        [
            shaped(f32, frames, ROWS, D),
            shaped(bf16, frames, ROWS, D),
            shaped(bf16, D, row_count(frames)),
        ],
        "combine",
        (),
        2 * frames * ROWS * D * D,
    )


def between_kernel(
    info_ref, ea_ref, eb_ref, mid_ref, g_ref, a_ref, gain_ref, *refs
):
    b_refs, (dmid_ref, da_ref, keep_ref, send_ref, sums_ref, total_ref, dmt_ref) = refs[:4], refs[4:]
    f = pl.program_id(0)
    n, z, part, width = keep_ref.shape
    grad = ea_ref[0] + eb_ref[0]
    low = mid_ref[0].astype(bf16).astype(f32)
    _, scaled, inverse = norm_rows(low, 1.0, 0.0)
    back = norm_back(grad, scaled, inverse, gain_ref[...])
    dmid = (g_ref[0].astype(f32) + back).astype(bf16)
    dmid_ref[0] = dmid
    sums = jnp.concatenate(
        [
            jnp.sum(grad * scaled, 0, keepdims=True),
            jnp.sum(grad, 0, keepdims=True),
            jnp.sum(dmid.astype(f32), 0, keepdims=True),
        ],
        0,
    )

    @pl.when(f == 0)
    def _():
        sums_ref[...] = jnp.zeros_like(sums_ref)
        total_ref[...] = jnp.zeros_like(total_ref)

    sums_ref[...] += sums
    da_ref[0] = dot(dmid, whole_out(b_refs)).astype(bf16)
    put_transposed(dmt_ref, dmid, 0)
    total_ref[...] += dot(dmt_ref[...], pad_rows(a_ref[0], FRAME_LANES))

    @pl.when(f == pl.num_programs(0) - 1)
    def _():
        for j in range(z):
            lanes = slice(j * width, (j + 1) * width)
            for at, ref in ((0, keep_ref), (D // 2, send_ref)):
                ref[:, j] = total_ref[at : at + D // 2, lanes].astype(bf16).reshape(n, part, width)


def between(info, ea, eb, middle, grads, attended, vec_rel, attn):
    frames = ea.shape[0]
    n, z, _, part, width = attn[4].shape
    frame = pl.BlockSpec((1, ROWS, D), lambda f, info_ref: (f, 0, 0))
    weight = once(n, z, 1, part, width, at=(0, 0, 1, 0, 0))
    return call(
        between_kernel,
        info,
        (ea, eb, middle, grads, attended, vec_rel[2:3], *attn[4:]),
        (frames,),
        [frame] * 5 + [once(1, D)] + [weight] * 4,
        [frame, frame, kept(2 * n, z, part, width), kept(2 * n, z, part, width), kept(3, D)],
        [shaped(bf16, frames, ROWS, D)] * 2
        + [shaped(bf16, 2 * n, z, part, width)] * 2
        + [shaped(f32, 3, D)],
        "between",
        [pltpu.VMEM((D, D), f32), pltpu.VMEM((D, row_count(1)), bf16)],
        4 * frames * ROWS * D * D,
    )


def project_grads_kernel(
    info_ref, ht_ref, dq_ref, dk_ref, dv_ref, ok_ref, os_ref, ak_ref, as_ref, bk_ref, bs_ref, sq_ref, sv_ref
):
    frames = dq_ref.shape[0]
    n, _, _, part, width = bk_ref.shape
    bk_ref[:, 0, 1] = ok_ref[:, 0]
    bs_ref[:, 0, 1] = os_ref[:, 0]
    for w, ref in enumerate((dq_ref, dk_ref, dv_ref)):
        rows = jnp.concatenate([pad_rows(ref[f], FRAME_LANES) for f in range(frames)], 0)
        full = dot(ht_ref[...], rows).astype(bf16)
        for at, a_ref, b_ref in ((0, ak_ref, bk_ref), (D // 2, as_ref, bs_ref)):
            grad = full[at : at + D // 2].reshape(n, part, width)
            if w < 2:
                a_ref[:, 0, w] = grad
            else:
                b_ref[:, 0, 0] = grad
        if w != 1:
            (sq_ref if w == 0 else sv_ref)[...] = jnp.sum(rows.astype(f32), 0, keepdims=True)


def project_grads(info, normed_t, grads, out_grads, attn):
    frames = grads[0].shape[0]
    n, z, _, part, width = attn[0].shape
    n = 2 * n
    block = pl.BlockSpec((frames, ROWS, width), lambda j, info_ref: (0, 0, j))
    spec = pl.BlockSpec((n, 1, 2, part, width), lambda j, info_ref: (0, j, 0, 0, 0))
    o_spec = pl.BlockSpec((n, 1, part, width), lambda j, info_ref: (0, j, 0, 0))
    row = pl.BlockSpec((1, width), lambda j, info_ref: (0, j))
    return call(
        project_grads_kernel,
        info,
        (normed_t, *grads, *out_grads),
        (z,),
        [once(*normed_t.shape)] + [block] * 3 + [o_spec] * 2,
        [spec] * 4 + [row] * 2,
        [shaped(bf16, n, z, 2, part, width)] * 4 + [shaped(f32, 1, D)] * 2,
        "project_grads",
        (),
        6 * frames * ROWS * D * D,
    )


def project_back_kernel(
    info_ref, x_ref, msg_ref, dmid_ref, gain_ref, dq_ref, dk_ref, dv_ref, *refs
):
    a_refs, b_refs, (ing_ref, dmsg_ref, sums_ref, total_ref) = refs[:4], refs[4:8], refs[8:]
    frames = x_ref.shape[0]
    j = pl.program_id(0)

    @pl.when(j == 0)
    def _():
        total_ref[...] = jnp.zeros_like(total_ref)

    parts = [halves(a_refs, 0, 0, 0), halves(a_refs, 0, 0, 1), halves(b_refs, 1, 0, 0)]
    weight = jnp.concatenate([jnp.concatenate(v, 0) for v in parts], 1)
    for f in range(frames):
        rows = jnp.concatenate([dq_ref[f], dk_ref[f], dv_ref[f]], 1)
        total_ref[f] += dot(rows, weight, NT)

    @pl.when(j == pl.num_programs(0) - 1)
    def _():
        gain_sum, shift_sum = jnp.zeros((1, D), f32), jnp.zeros((1, D), f32)
        for f in range(frames):
            rows = with_message(x_ref, msg_ref, info_ref, f)
            _, scaled, inverse = norm_rows(rows, 1.0, 0.0)
            grad = total_ref[f]
            gain_sum += jnp.sum(grad * scaled, 0, keepdims=True)
            shift_sum += jnp.sum(grad, 0, keepdims=True)
            back = norm_back(grad, scaled, inverse, gain_ref[...])
            ing_ref[f] = dmid_ref[f].astype(f32) + back
            dmsg_ref[f] = back[PATCHES : PATCHES + 1]
        sums_ref[...] = jnp.concatenate([gain_sum, shift_sum], 0)


def project_back(info, x, message, dmid, vec_rel, grads, attn):
    frames = x.shape[0]
    n, z, _, part, width = attn[0].shape
    block = pl.BlockSpec((frames, ROWS, width), lambda j, info_ref: (0, 0, j))
    a_spec = pl.BlockSpec((n, 1, 2, part, width), lambda j, info_ref: (0, j, 0, 0, 0))
    b_spec = pl.BlockSpec((n, 1, 1, part, width), lambda j, info_ref: (0, j, 0, 0, 0))
    return call(
        project_back_kernel,
        info,
        (x, message, dmid, vec_rel[0:1], *grads, *attn),
        (z,),
        [once(frames, ROWS, D), once(FRAMES, D), once(frames, ROWS, D), once(1, D)]
        + [block] * 3
        + [a_spec] * 4
        + [b_spec] * 4,
        [once(frames, ROWS, D), kept(frames, 1, D), kept(2, D)],
        [shaped(f32, frames, ROWS, D), shaped(f32, frames, 1, D), shaped(f32, 2, D)],
        "project_back",
        [pltpu.VMEM((frames, ROWS, D), f32)],
        6 * frames * ROWS * D * D,
    )


def message_halves(refs, which, i):
    part = D // (4 * refs[0].shape[0])
    return halves([ref.at[:, i * part : (i + 1) * part] for ref in refs], which)


def message_times(rows, refs, i):
    own, other = rows[:, : D // 2], rows[:, D // 2 :]
    cols = []
    for which in range(2):
        weights = message_halves(refs[4 * which : 4 * which + 4], which, i)
        cols.append(dot(own, weights[0]) + dot(other, weights[1]))
    return jnp.concatenate(cols, 1)


def message_times_t(rows, refs, i):
    left, right = rows[:, : D // 2], rows[:, D // 2 :]
    first, second = message_halves(refs[:4], 0, i), message_halves(refs[4:], 1, i)
    return jnp.concatenate(
        [dot(left, first[s], NT) + dot(right, second[s], NT) for s in range(2)], 1
    )


def by_head(rows):
    full = jnp.concatenate([rows.astype(f32)] * HEADS, 0)
    return jnp.where(head_mask(), full, 0.0).astype(bf16)


def head_mask():
    shape = (HEADS * FRAMES, D)
    head = lax.broadcasted_iota(jnp.int32, shape, 0) // FRAMES
    return head == lax.broadcasted_iota(jnp.int32, shape, 1) // HEAD


def over_heads(rows):
    rows = jnp.where(head_mask(), rows, 0.0)
    return jnp.sum(rows.reshape(HEADS, FRAMES, D), 0)


def message_probability(queries, keys):
    scores = dot(by_head(queries), keys, NT) * HEAD**-0.5
    shifted = jnp.exp(scores - jnp.max(scores, 1, keepdims=True))
    return shifted * (1.0 / jnp.sum(shifted, 1, keepdims=True))


def message_forward_kernel(info_ref, cls_ref, rel_ref, *refs):
    weights, (vec_ref, msg_ref, first_ref, pack_ref, hold_ref) = refs[:8], refs[8:]
    vec_ref[...] = permuted(rel_ref, info_ref, BLOCKS)

    def relative(rows):
        hold_ref[...] = rows
        return permuted(hold_ref, info_ref, 0)

    first = message_times(relative(cls_ref[...]).astype(bf16), weights, 0) + vec_ref[6:7]
    normed = norm_rows(first, vec_ref[4:5], vec_ref[5:6])[0].astype(bf16).astype(f32)
    normed_rel = relative(normed).astype(bf16)
    queries = (message_times(normed_rel, weights, 1) + vec_ref[7:8]).astype(bf16)
    keys = message_times(normed_rel, weights, 2).astype(bf16)
    values = (message_times(normed_rel, weights, 3) + vec_ref[8:9]).astype(bf16)
    probability = message_probability(queries, keys).astype(bf16)
    mixed = over_heads(dot(probability, values)).astype(bf16).astype(f32)
    message = first + message_times(relative(mixed).astype(bf16), weights, 4) + vec_ref[9:10]
    msg_ref[...] = relative(message)
    first_ref[...] = first
    for i, rows in enumerate((normed, mixed, queries, keys, values)):
        pack_ref[i] = rows.astype(f32)


def message_forward(info, class_rows, vec_rel, weights):
    one = kept(FRAMES, D)
    return call(
        message_forward_kernel,
        info,
        (class_rows, vec_rel, *weights),
        (1,),
        [one, kept(*vec_rel.shape)] + [once(*w.shape) for w in weights],
        [kept(*vec_rel.shape), one, one, kept(5, FRAMES, D)],
        [
            shaped(f32, *vec_rel.shape),
            shaped(f32, FRAMES, D),
            shaped(f32, FRAMES, D),
            shaped(f32, 5, FRAMES, D),
        ],
        "message_forward",
        [pltpu.VMEM((FRAMES, D), f32)],
        10 * FRAMES * D * D,
    )


def message_backward_kernel(info_ref, dmsg_ref, first_ref, pack_ref, vec_ref, *refs):
    weights, (class_ref, sent_ref, sums_ref, hold_ref) = refs[:8], refs[8:]
    frames = dmsg_ref.shape[1]
    for i in range(dmsg_ref.shape[0]):
        place = lax.bitwise_xor(info_ref[2 * BLOCKS], i)
        for f in range(frames):
            hold_ref[i * frames + f : i * frames + f + 1] = dmsg_ref[place, f : f + 1]
    dmsg = permuted(hold_ref, info_ref, BLOCKS)

    def plain(rows):
        hold_ref[...] = rows
        return permuted(hold_ref, info_ref, BLOCKS)

    queries, keys, values = (pack_ref[i].astype(bf16) for i in (2, 3, 4))
    grad_mixed = plain(message_times_t(dmsg.astype(bf16), weights, 4)).astype(bf16)
    probability = message_probability(queries, keys)
    grads_big = by_head(grad_mixed)
    grad_prob = dot(grads_big, values, NT)
    inner = jnp.sum(grad_prob * probability, 1, keepdims=True)
    grad_scores = (probability * (grad_prob - inner)).astype(bf16)
    dq = (over_heads(dot(grad_scores, keys)) * HEAD**-0.5).astype(bf16)
    dk = (dot(grad_scores, by_head(queries), TN) * HEAD**-0.5).astype(bf16)
    dv = dot(probability.astype(bf16), grads_big, TN).astype(bf16)
    grad = plain(
        message_times_t(dq, weights, 1)
        + message_times_t(dk, weights, 2)
        + message_times_t(dv, weights, 3)
    )
    _, scaled, inverse = norm_rows(first_ref[...], 1.0, 0.0)
    back = norm_back(grad, scaled, inverse, vec_ref[4:5])
    dfirst = (dmsg + back).astype(bf16)
    class_ref[...] = message_times_t(dfirst, weights, 0)
    sent = [rows.astype(f32) for rows in (dfirst, dq, dk, dv, dmsg)]
    for i, rows in enumerate(sent):
        sent_ref[i] = rows
    sums = [grad * scaled, grad, sent[0], sent[1], sent[3], dmsg]
    sums_ref[...] = jnp.concatenate([jnp.sum(rows, 0, keepdims=True) for rows in sums], 0)


def message_backward(info, dmsg, first, pack, vectors, weights):
    one = kept(FRAMES, D)
    return call(
        message_backward_kernel,
        info,
        (dmsg, first, pack, vectors, *weights),
        (1,),
        [kept(*dmsg.shape), one, kept(*pack.shape), kept(*vectors.shape)]
        + [once(*w.shape) for w in weights],
        [one, kept(5, FRAMES, D), kept(6, D)],
        [shaped(f32, FRAMES, D), shaped(f32, 5, FRAMES, D), shaped(f32, 6, D)],
        "message_backward",
        [pltpu.VMEM((FRAMES, D), f32)],
        10 * FRAMES * D * D,
    )


def relative_order():
    return lax.axis_size("dp") * BLOCK == D


def make_info():
    place = lax.iota(jnp.int32, BLOCKS)
    if relative_order():
        mine = lax.axis_index("dp")
        differs = place ^ mine
        places = mine ^ (2 * (place % 4) + place // 4)
        blocks = (differs % 2) * 4 + differs // 2
    else:
        places = blocks = place
    return jnp.concatenate([places, blocks, lax.axis_index("tensor")[None]]).astype(jnp.int32)


def swap(values, axis, bit):
    pairs = [(i, i ^ bit) for i in range(lax.axis_size(axis))]
    return lax.ppermute(values, axis, pairs)


def bits_of(axis):
    size = lax.axis_size(axis)
    return [1 << i for i in range(size.bit_length() - 1)]


def after(values, *earlier):
    return lax.optimization_barrier((values, earlier))[0]


def join_kernel(*refs):
    count = len(refs) // 3
    for i in range(count):
        out_ref = refs[2 * count + i]
        out_ref[0] = refs[2 * i][...]
        out_ref[1] = refs[2 * i + 1][...]


def join(*pairs):
    flat = [v.reshape(-1, v.shape[-1]) for pair in pairs for v in pair]
    specs = [pl.BlockSpec((v.shape[0] // 2, v.shape[1]), lambda i: (i, 0)) for v in flat]
    out = pl.pallas_call(
        join_kernel,
        grid=(2,),
        in_specs=specs,
        out_specs=[
            pl.BlockSpec((2, v.shape[0] // 2, v.shape[1]), lambda i: (0, i, 0)) for v in flat[::2]
        ],
        out_shape=[shaped(bf16, 2, *v.shape) for v in flat[::2]],
        compiler_params=pltpu.CompilerParams(vmem_limit_bytes=48 << 20),
        cost_estimate=cost(0, sum(2 * v.size for v in flat)),
        name="join",
    )(*flat)
    return [v.reshape((2,) + pair[0].shape) for v, pair in zip(out, pairs)]


class Gather:
    def __init__(self, *values):
        self.own, self.place = list(values), 0
        if relative_order():
            self.arrived = [swap(v, "dp", bit) for v, bit in zip(values, (2, 4))]
            return
        self.pieces = []
        for v in values:
            everything = lax.all_gather(v, "dp", axis=0)
            count = everything.shape[0] // 4
            self.pieces += [everything[i * count : (i + 1) * count] for i in range(4)]
        self.arrived = self.pieces

    def step(self):
        if not relative_order():
            return self.pieces
        self.place += 1
        if self.place == 1:
            self.own = join(*zip(self.own, self.arrived))
            self.arrived = [swap(v, "dp", bit) for v, bit in zip(self.own, (4, 2))]
            return self.own
        self.pieces = [v for pair in zip(self.own, self.arrived) for v in pair]
        self.arrived = [swap(v, "dp", 1) for v in self.pieces]
        return self.pieces

    def result(self):
        if not relative_order():
            return self.pieces
        return [v for i in (0, 2) for v in self.pieces[i : i + 2] + self.arrived[i : i + 2]]


def beside(outputs, *transfers):
    outputs, arrived = lax.optimization_barrier((outputs, [t.arrived for t in transfers]))
    for t, values in zip(transfers, arrived):
        t.arrived = values
    return outputs


def add_low(left_side, right_side):
    return (left_side.astype(f32) + right_side.astype(f32)).astype(bf16)


def add_kernel(axes, *refs):
    ins, outs = refs[: 2 * len(axes)], refs[2 * len(axes) :]
    for i, axis in enumerate(axes):
        for side in range(2):
            at = (side,) if axis == 0 else (slice(None), side)
            outs[2 * i + side][...] = add_low(ins[2 * i][at], ins[2 * i + 1][at])


def add_and_split(pairs, axes):
    lead = pairs[0][0].shape[:-2]
    rows, width = pairs[0][0].shape[-2:]
    steps = 2 if rows % 32 == 0 else 1
    zeros = (0,) * len(lead)
    spec = pl.BlockSpec((*lead, rows // steps, width), lambda i: (*zeros, i, 0))
    out = pl.BlockSpec((*lead[1:], rows // steps, width), lambda i: (*zeros[1:], i, 0))
    return pl.pallas_call(
        functools.partial(add_kernel, axes),
        grid=(steps,),
        in_specs=[spec] * (2 * len(pairs)),
        out_specs=[out] * (2 * len(pairs)),
        out_shape=[shaped(bf16, *lead[1:], rows, width)] * (2 * len(pairs)),
        compiler_params=pltpu.CompilerParams(vmem_limit_bytes=48 << 20),
        cost_estimate=cost(0, sum(4 * a.size for a, _ in pairs)),
        name="add",
    )(*[v for pair in pairs for v in pair])


class Scatter:
    def __init__(self, keep, send):
        self.place, self.shape = 0, keep[0].shape[1:]
        if not relative_order():
            self.held = [
                lax.psum_scatter(jnp.concatenate(v, 0), "dp", scatter_dimension=0, tiled=False)
                for v in zip(keep, send)
            ]
            self.arrived = [jnp.zeros_like(v) for v in self.held]
            return
        width = self.shape[-1]
        self.held = [v.reshape(2, 2, -1, width) for v in keep]
        self.arrived = [swap(v, "dp", 1).reshape(2, 2, -1, width) for v in send]

    def step(self):
        if not relative_order():
            return list(self.held)
        axes, bits = ((0, 1), (4, 2)) if self.place == 0 else ((0, 0), (2, 4))
        self.place += 1
        sums = list(add_and_split(list(zip(self.held, self.arrived)), axes))
        self.held, going = sums[::2], sums[1::2]
        self.arrived = [swap(v, "dp", bit) for v, bit in zip(going, bits)]
        return going


def pair_kernel(info_ref, *refs):
    ins, outs = refs[:-2], refs[-2:]
    rows = ins[0].shape[1]
    for side in range(2):
        for i in range(len(ins) // 4):
            total = add_low(ins[4 * i + side][0], ins[4 * i + 2 + side][0])
            outs[side][0, i * rows : (i + 1) * rows] = total


def add_and_pair(info, held, arrived):
    count = len(held)
    rows, width = held[0][0].size // held[0].shape[-1], held[0].shape[-1]
    own = pl.BlockSpec((1, rows, width), lambda h, ref: (2 * h + ref[2 * BLOCKS] % 2, 0, 0))
    other = pl.BlockSpec((1, rows, width), lambda h, ref: (2 * h + 1 - ref[2 * BLOCKS] % 2, 0, 0))
    flat = [v.reshape(4, rows, width) for pair in zip(held, arrived) for v in pair for _ in range(2)]
    out = pl.BlockSpec((1, count * rows, width), lambda h, ref: (h, 0, 0))
    return call(
        pair_kernel,
        info,
        flat,
        (2,),
        [own, other] * (2 * count),
        [out] * 2,
        [shaped(bf16, 2, count * rows, width)] * 2,
        "add_and_pair",
    )


def single_kernel(info_ref, ho_ref, hp_ref, ao_ref, ap_ref, held_ref, going_ref):
    held_ref[...] = add_low(ho_ref[0], ao_ref[0])
    going_ref[...] = add_low(hp_ref[0], ap_ref[0])


def add_and_single(info, held, arrived):
    _, rows, width = held.shape
    own = pl.BlockSpec((1, rows, width), lambda i, ref: (ref[2 * BLOCKS] // 2, 0, 0))
    other = pl.BlockSpec((1, rows, width), lambda i, ref: (1 - ref[2 * BLOCKS] // 2, 0, 0))
    return call(
        single_kernel,
        info,
        (held, held, arrived, arrived),
        (1,),
        [own, other] * 2,
        [kept(rows, width)] * 2,
        [shaped(bf16, rows, width)] * 2,
        "add_and_single",
    )


class ScatterVideos:
    def __init__(self, info, *scatters):
        self.info, self.shape = info, scatters[0].shape
        self.direct = lax.axis_size("tensor") != 4
        held = [v.reshape(self.shape) for s in scatters for v in s.held]
        arrived = [v.reshape(self.shape) for s in scatters for v in s.arrived]
        if self.direct:
            values = jnp.stack([add_low(h, a) for h, a in zip(held, arrived)], 1)
            self.held = lax.psum_scatter(values, "tensor", scatter_dimension=0, tiled=False)
            self.going, self.arrived = self.held, jnp.zeros_like(self.held)
            return
        self.held, self.going = add_and_pair(info, held, arrived)
        self.arrived = swap(self.going, "tensor", 1)

    def step(self):
        if self.direct:
            return self.held
        self.held, going = add_and_single(self.info, self.held, self.arrived)
        self.arrived = swap(going, "tensor", 2)
        return going

    def result(self):
        return add_low(self.held, self.arrived).reshape((-1,) + self.shape[1:])


class GatherSmall:
    def __init__(self, values):
        self.values, self.bits = values[None], [2, 4, 1]
        if relative_order():
            self.arrived = swap(self.values, "dp", 2)
        else:
            self.values = self.arrived = lax.all_gather(values, "dp", axis=0)

    def step(self):
        if not relative_order():
            return self.values
        self.values = jnp.concatenate([self.values, self.arrived], 0)
        self.bits = self.bits[1:]
        if self.bits:
            self.arrived = swap(self.values, "dp", self.bits[0])
        return self.values


def sum_everywhere(values):
    rounds = [("dp", bits_of("dp")[:1])]
    for axis, bits in (("dp", bits_of("dp")[1:]), ("tensor", bits_of("tensor"))):
        rounds += [(axis, bits[i : i + 2]) for i in range(0, len(bits), 2)]
    for axis, bits in rounds:
        if len(bits) == 1:
            values = values + swap(values, axis, bits[0])
            continue
        first, second, both = (swap(values, axis, b) for b in (*bits, sum(bits)))
        values = (values + first) + (second + both)
    return values


def gather_and_sum_videos(values, sums):
    values, count = values[None], sums.shape[0]
    for bit in bits_of("tensor"):
        rows = jnp.concatenate([sums, values.reshape(-1, D)], 0)
        arrived = swap(rows, "tensor", bit)
        sums = sums + arrived[:count]
        values = jnp.concatenate([values, arrived[count:].reshape(values.shape)], 0)
    return values, sums


def adam_step(weight, first_moment, second_moment, gradient, factor, step_rate, decay_rate):
    clipped = gradient * factor
    first_new = beta_one * first_moment + (1.0 - beta_one) * clipped
    second_new = beta_two * second_moment + (1.0 - beta_two) * clipped * clipped
    update = (
        first_new
        / (1.0 - beta_one**STEP)
        / (jnp.sqrt(second_new / (1.0 - beta_two**STEP)) + adam_eps)
    )
    weight_new = weight - step_rate * (update + decay_rate * weight)
    return (first_new, second_new, weight_new)


def on_device(
    tokens,
    cotangent,
    attn_master,
    attn_first,
    attn_second,
    attn_ema,
    mlp_master,
    mlp_first,
    mlp_second,
    mlp_ema,
    msg_master,
    msg_first,
    msg_second,
    msg_ema,
    vec_master,
    vec_first,
    vec_second,
    vec_ema,
):
    z_index = lax.axis_index("tensor")
    z_count = lax.axis_size("tensor")
    dp_index = lax.axis_index("dp")
    part = attn_master.shape[0]
    local_width = attn_master.shape[2]
    local_ff = mlp_master.shape[2]
    frames = tokens.shape[0] // PATCHES
    half_ff = local_ff // 2
    info = make_info()

    class_own = jnp.concatenate(
        [tokens[f * PATCHES : f * PATCHES + 1] for f in range(frames)], 0
    ).reshape(-1, local_width)
    attn_low = jnp.swapaxes(attn_master, 0, 1).astype(bf16).reshape(4 * part, local_width)
    attn_rows = pad_rows(jnp.concatenate([attn_low, class_own], 0), 4 * part + 16)
    attn_z = lax.all_gather(attn_rows, "tensor", axis=0)
    mlp_z = lax.all_gather(jnp.swapaxes(mlp_master, 0, 1).astype(bf16), "tensor", axis=0)
    class_rows = attn_z[:, 4 * part : 4 * part + class_own.shape[0]].reshape(FRAMES, D)
    attn_z = attn_z[:, : 4 * part].reshape(z_count, 4, part, local_width)

    msg_low = jnp.swapaxes(msg_master, 0, 1).astype(bf16).reshape(5 * part, D)
    vec_count = vec_master.shape[1]
    vec_low = jnp.pad(vec_master.astype(bf16).T, ((0, 32 - vec_count), (0, D // 2 - part)))
    msg_go = Gather(jnp.concatenate([msg_low[:, : D // 2], vec_low], 0), msg_low[:, D // 2 :])
    prepared = prepare(info, tokens, cotangent)
    x, grads, grads_t, grad_sum = beside(prepared, msg_go)
    sent_msg = msg_go.step()
    attn_z = after(attn_z, *sent_msg)
    attn_go = Gather(attn_z[:, :2], attn_z[:, 2:])
    sent_attn = attn_go.step()
    beside(sent_attn, msg_go)
    sent_msg = msg_go.step()
    mlp_z = after(mlp_z, *sent_msg)
    mlp_go = [
        Gather(*[mlp_z[:, i, :, j * half_ff : (j + 1) * half_ff] for i in range(2)])
        for j in range(2)
    ]
    msg_w = msg_go.result()
    vec_rel = jnp.concatenate(msg_w[:4], 0)[:, 5 * part : 5 * part + vec_count, :part]
    vec_rel = jnp.moveaxis(vec_rel, 0, 1).reshape(-1, D).astype(f32)

    sent_mlp = mlp_go[0].own + mlp_go[1].own
    vectors, message, first_msg, msg_pack = beside(
        message_forward(info, after(class_rows, *sent_mlp).astype(f32), vec_rel, msg_w), attn_go
    )
    ff_bias = vectors[14:].reshape(z_count, 2, half_ff)
    attn_go.step()
    attn_w = attn_go.result()
    projected = project(info, x, message, vec_rel, vectors, attn_w)
    queries, key_rows, value_rows, normed = beside(projected, *mlp_go)
    sent_mlp = mlp_go[0].step()
    attended, totals = beside(
        attend_forward(after(queries, *sent_mlp), key_rows, value_rows), mlp_go[0]
    )
    sent_mlp = mlp_go[0].step() + mlp_go[1].step()
    middle, n2, n2_t = beside(
        combine(info, x, after(attended, *sent_mlp), vec_rel, attn_w), mlp_go[0]
    )

    def feed(j, n2):
        return feed_forward(n2, n2_t, grads, grads_t, ff_bias[:, j], mlp_go[j].result())

    out_0, dn2_0, *dw_0, db_0 = beside(feed(0, n2), mlp_go[1])
    sent_mlp = mlp_go[1].step()
    normed_t = beside(transposed(info, after(normed, *sent_mlp)), mlp_go[1])
    dw_0 = after(dw_0, normed_t)
    sums_0 = Scatter(dw_0[::2], dw_0[1::2])
    out_1, dn2_1, *dw_1, db_1 = beside(feed(1, after(n2, normed_t)), sums_0)
    sums_1 = Scatter(dw_1[::2], dw_1[1::2])
    going = sums_0.step()
    dmid, grad_attended, *grad_out_w, sums_two = beside(
        between(info, after(dn2_0, *going), dn2_1, middle, grads, attended, vec_rel, attn_w), sums_1
    )
    going = sums_1.step()
    pairs = HEADS // 2
    back = (queries, key_rows, value_rows, totals)
    grad_qkv = beside(
        attend_backward(*back, after(grad_attended, *going), 0, pairs // 2), sums_0
    )
    going = sums_0.step()
    grad_qkv = beside(
        attend_backward(
            *back, after(grad_attended, *going), pairs // 2, pairs - pairs // 2, grad_qkv
        ),
        sums_0,
        sums_1,
    )
    going = sums_1.step()
    dqk_keep, dqk_send, dvo_keep, dvo_send, sum_q, sum_v = beside(
        project_grads(info, after(normed_t, *going), grad_qkv, grad_out_w, attn_w), sums_1
    )
    sums_attn = Scatter([dqk_keep, dvo_keep], [dqk_send, dvo_send])
    mlp_go = ScatterVideos(info, sums_0, sums_1)
    block_output = beside(
        finish(info, [after(middle, mlp_go.going), out_0, out_1], vec_rel[13:14], "block_output"),
        sums_attn,
    )
    going = sums_attn.step()
    ing, dmsg, sums_one = beside(
        project_back(info, after(x, *going), message, dmid, vec_rel, grad_qkv, attn_w),
        sums_attn,
        mlp_go,
    )
    going = sums_attn.step()

    ff_bias_grad = jnp.stack(
        [db.reshape(z_count, half_ff) for db in (db_0, db_1)], 1
    ).reshape(FF // D, D)
    table = jnp.concatenate([sums_one, sums_two, grad_sum, sum_q, sum_v, ff_bias_grad], 0)
    dmsg = dmsg[:, 0].astype(bf16).astype(f32)
    dmsg, table = gather_and_sum_videos(after(dmsg, *going), table)
    mlp_go.arrived = after(mlp_go.arrived, dmsg)
    sent_mlp = mlp_go.step()
    dmsg = beside(after(dmsg, sent_mlp), sums_attn)
    attn_go = ScatterVideos(info, sums_attn)
    grad_class, sent, sums_msg = beside(
        message_backward(info, after(dmsg, attn_go.going), first_msg, msg_pack, vectors, msg_w),
        attn_go,
        mlp_go,
    )
    mlp_sum = mlp_go.result()
    going = attn_go.step()

    plain = plain_order(info, table[:6])
    table = jnp.concatenate([plain[:4], sums_msg, table[6:8], plain[4:], table[8:]], 0)
    sent = jnp.concatenate([msg_pack[:2], sent], 0).astype(bf16).reshape(7 * FRAMES, D)
    sent = jnp.concatenate([class_rows, sent, table.astype(bf16)], 0)
    small = GatherSmall(after(sent, going))
    input_grad = beside(
        finish(info, [after(ing, small.values)], grad_class, "input_grad"), small, attn_go
    )
    small.step()
    attn_grad = attn_go.result()
    small.step()
    everyone = small.step()
    tables = lax.dynamic_slice_in_dim(everyone[:, 8 * FRAMES :], dp_index * part, part, 2)
    vec_grad = jnp.sum(tables.astype(f32), 0).T
    everyone = everyone[:, : 8 * FRAMES].reshape(-1, 8, FRAMES, D)
    everyone = jnp.moveaxis(everyone, 0, 1).reshape(8, -1, D)
    mine = lax.dynamic_slice_in_dim(everyone[:3], dp_index * part, part, 2)
    msg_grad = jnp.stack(
        [
            dot(mine[0], everyone[3], TN),
            dot(mine[1], everyone[4], TN),
            dot(mine[1], everyone[5], TN),
            dot(mine[1], everyone[6], TN),
            dot(mine[2], everyone[7], TN),
        ],
        1,
    )

    attn_grad = jnp.swapaxes(attn_grad.reshape(4, part, local_width), 0, 1).astype(f32)
    mlp_grad = jnp.concatenate([mlp_sum[:2], mlp_sum[2:]], 2)
    mlp_grad = jnp.swapaxes(mlp_grad, 0, 1).astype(f32)

    keep_share = (z_index == 0).astype(f32)
    squares = (
        jnp.sum(attn_grad * attn_grad)
        + jnp.sum(mlp_grad * mlp_grad)
        + keep_share * (jnp.sum(msg_grad * msg_grad) + jnp.sum(vec_grad * vec_grad))
    )
    squares = sum_everywhere(jnp.broadcast_to(squares, (8, 128)))[0, 0]
    grad_norm = jnp.sqrt(squares)
    factor = clip_limit / jnp.maximum(grad_norm, clip_limit)

    def update(master, first, second, ema, grad, rate, decay):
        first_new, second_new, weight = adam_step(master, first, second, grad, factor, rate, decay)
        return grad, first_new, second_new, weight, ema_keep * ema + (1.0 - ema_keep) * weight

    return (
        block_output,
        input_grad,
        grad_norm,
        *update(attn_master, attn_first, attn_second, attn_ema, attn_grad, rate_mat, decay_mat),
        *update(mlp_master, mlp_first, mlp_second, mlp_ema, mlp_grad, rate_mat, decay_mat),
        *update(msg_master, msg_first, msg_second, msg_ema, msg_grad, rate_mat, decay_mat),
        *update(vec_master, vec_first, vec_second, vec_ema, vec_grad, rate_vec, 0.0),
    )


def solution(mesh):
    rows = P(("dp", "tensor"), None)
    split = P("dp", None, "tensor")
    copied = P("dp", None, None)
    table = P("dp", None)
    in_specs = (rows,) * 2 + (split,) * 8 + (copied,) * 4 + (table,) * 4
    out_specs = (rows,) * 2 + (P(),) + (split,) * 10 + (copied,) * 5 + (table,) * 5
    return jax.shard_map(
        on_device, mesh=mesh, in_specs=in_specs, out_specs=out_specs, check_vma=False
    )
```

```python
import functools

import jax
import jax.numpy as jnp
from jax import lax
from jax.experimental import pallas as pl
from jax.experimental.pallas import tpu as pltpu
from jax.sharding import PartitionSpec as P

D = 1024
HEADS = 16
HEAD = 64
FF = 4096
PATCHES = 577
FRAMES = 8
STEP = 10
ROWS = 592


norm_eps = 1e-05
beta_one = 0.9
beta_two = 0.95
adam_eps = 1e-08
decay_mat = 0.05
ema_keep = 0.7
clip_limit = 1.0
rate_mat = 0.02
rate_vec = 0.4
far_below = -1e30
COST_PART = 16
bf16 = jnp.bfloat16
f32 = jnp.float32
NN = (((1,), (0,)), ((), ()))
NT = (((1,), (1,)), ((), ()))
TN = (((0,), (0,)), ((), ()))


def dot(left_side, right_side, dims=NN):
    return lax.dot_general(left_side, right_side, dims, preferred_element_type=f32)


def norm_rows(values, gain_row, shift_row):
    centre = values - jnp.mean(values, -1, keepdims=True)
    spread = jnp.mean(centre * centre, -1, keepdims=True)
    inverse = lax.rsqrt(spread + norm_eps)
    scaled = centre * inverse
    return (scaled * gain_row + shift_row, scaled, inverse)


def norm_back(gradient, scaled, inverse, gain_row):
    inner = gradient * gain_row
    return inverse * (
        inner
        - jnp.mean(inner, -1, keepdims=True)
        - scaled * jnp.mean(inner * scaled, -1, keepdims=True)
    )


def pad_rows(values, count):
    if values.shape[0] == count:
        return values
    extra = jnp.zeros((count - values.shape[0],) + values.shape[1:], values.dtype)
    return jnp.concatenate([values, extra], 0)


def head_pair(queries, key_rows, head):
    lane = lax.broadcasted_iota(jnp.int32, queries.shape, 1)
    key_lane = lax.broadcasted_iota(jnp.int32, key_rows.shape, 1)
    key_row = lax.broadcasted_iota(jnp.int32, key_rows.shape, 0)
    spare = HEAD * (1 - head)
    mask = jnp.where(
        (key_lane == spare) & (key_row > PATCHES), jnp.asarray(far_below, bf16), jnp.asarray(0, bf16)
    )
    keys_one = jnp.where((key_lane // HEAD) == head, key_rows, mask)
    queries_one = jnp.where(lane == spare, jnp.asarray(1, bf16), queries)
    return queries_one, keys_one


def each_head(values):
    lane = lax.broadcasted_iota(jnp.int32, values.shape, 1)
    zero = jnp.zeros_like(values)
    return jnp.concatenate(
        [jnp.where(lane < HEAD, values, zero), jnp.where(lane < HEAD, zero, values)], 0
    )


def attend_forward_kernel(q_ref, k_ref, v_ref, out_ref, total_ref):
    rows, width = q_ref.shape[1:]
    key_count = -(-rows // 128) * 128
    lane = lax.broadcasted_iota(jnp.int32, (rows, 128), 1)
    out_of = lax.broadcasted_iota(jnp.int32, (rows, 128), 1) > PATCHES - (key_count - 128)
    pairs = width // 128

    def score(pair):
        lanes = slice(pair * 128, (pair + 1) * 128)
        queries = q_ref[0, :, lanes] * jnp.asarray(HEAD**-0.5, bf16)
        return dot(queries, each_head(pad_rows(k_ref[0, :, lanes], key_count)), NT)

    waiting = [score(0)]
    for pair in range(pairs):
        if pair + 1 < pairs:
            waiting.append(score(pair + 1))
        both = waiting.pop(0)
        shares, totals, sums = [], [], []
        for head in range(2):
            scores = both[:, head * key_count : (head + 1) * key_count]
            tail = jnp.where(out_of, far_below, scores[:, key_count - 128 :])
            scores = jnp.concatenate([scores[:, : key_count - 128], tail], 1)
            highest = jnp.max(scores, 1, keepdims=True)
            shifted = jnp.exp(scores - highest)
            total = jnp.sum(shifted, 1, keepdims=True)
            shares.append(shifted.astype(bf16))
            sums.append(1.0 / total)
            totals.append(highest + jnp.log(total))
        lanes = slice(pair * 128, (pair + 1) * 128)
        out = dot(jnp.concatenate(shares, 1), each_head(pad_rows(v_ref[0, :, lanes], key_count)))
        out_ref[0, :, lanes] = (out * jnp.where(lane < HEAD, *sums)).astype(bf16)
        logs = jnp.where(lane < HEAD, *totals).T
        total_ref[0, pair] = jnp.concatenate([logs[0:1], logs[HEAD : HEAD + 1]], 0)


def attend_backward_kernel(q_ref, k_ref, v_ref, total_ref, grad_ref, *rest):
    dq_ref, dk_ref, dv_ref = rest[-3:]
    rows, width = q_ref.shape[1:]
    count = -(-rows // 128) * 128
    pairs = width // 128
    tail = rows // 16 * 16 - 16
    out_of = lax.broadcasted_iota(jnp.int32, (rows - tail, count), 0) > PATCHES - tail

    def swapped(values):
        return jnp.concatenate([values[:, HEAD:], values[:, :HEAD]], 1)

    def load(pair):
        lanes = slice(pair * 128, (pair + 1) * 128)
        queries = pad_rows(q_ref[0, :, lanes], count) * jnp.asarray(HEAD**-0.5, bf16)
        return lanes, queries, pad_rows(grad_ref[0, :, lanes], count)

    def start(pair):
        lanes, queries, grads = load(pair)
        keys, values = k_ref[0, :, lanes], swapped(v_ref[0, :, lanes])
        first = lax.broadcasted_iota(jnp.int32, (rows, 128), 1) < HEAD
        queries, grads = each_head(queries), each_head(swapped(grads))
        products = []
        for head in range(2):
            mixed = jnp.where(first, keys, values) if head == 0 else jnp.where(first, values, keys)
            right = [
                queries[head * count : (head + 1) * count],
                grads[(1 - head) * count : (2 - head) * count],
            ]
            products.append(dot(mixed, jnp.concatenate(right, 0), NT))
        return products

    waiting = [start(0)]
    for pair in range(pairs):
        if pair + 1 < pairs:
            waiting.append(start(pair + 1))
        products = waiting.pop(0)
        lanes, queries, grads = load(pair)
        shares, grad_scores = [], []
        for head in range(2):
            total = total_ref[0, pair, head : head + 1, :]
            total = jnp.concatenate([total, jnp.zeros((1, count - rows), f32)], 1)
            share = jnp.exp(products[head][:, :count] - total)
            share = jnp.concatenate([share[:tail], jnp.where(out_of, 0.0, share[tail:])], 0)
            grad_share = products[head][:, count:]
            inner = jnp.sum(grad_share * share, 0, keepdims=True)
            grad_scores.append((share * (grad_share - inner)).astype(bf16))
            shares.append(share.astype(bf16))
        dv_ref[0, :, lanes] = dot(jnp.concatenate(shares, 1), each_head(grads)).astype(bf16)
        dk_ref[0, :, lanes] = dot(jnp.concatenate(grad_scores, 1), each_head(queries)).astype(bf16)
        keys_t = pad_rows(k_ref[0, :, lanes], count).astype(f32).T.astype(bf16)
        back = [
            dot(keys_t[HEAD * head : HEAD * (head + 1)], pad_rows(grad_scores[head], count))
            for head in range(2)
        ]
        dq_ref[0, :, lanes] = (jnp.concatenate(back, 0) * HEAD**-0.5).T[:rows].astype(bf16)


def cost(flops, moved):
    return pl.CostEstimate(
        flops=flops // COST_PART, bytes_accessed=moved // COST_PART, transcendentals=0
    )


def attend_cost(frames, rows, width, matmuls):
    return cost(2 * matmuls * frames * rows * rows * width, 4 * matmuls * frames * rows * width)


def attend_forward(queries, key_rows, value_rows):
    frames, rows, width = queries.shape
    spec = pl.BlockSpec((1, rows, width), lambda f: (f, 0, 0))
    return pl.pallas_call(
        attend_forward_kernel,
        grid=(frames,),
        in_specs=[spec] * 3,
        out_specs=[spec, pl.BlockSpec((1, width // 128, 2, rows), lambda f: (f, 0, 0, 0))],
        out_shape=[
            jax.ShapeDtypeStruct((frames, rows, width), bf16),
            jax.ShapeDtypeStruct((frames, width // 128, 2, rows), f32),
        ],
        compiler_params=pltpu.CompilerParams(vmem_limit_bytes=48 << 20),
        cost_estimate=attend_cost(frames, rows, width, 4),
        name="attend_forward",
    )(queries, key_rows, value_rows)


def attend_backward(queries, key_rows, value_rows, totals, grads, begin, count, earlier=()):
    frames, rows, width = queries.shape
    at = begin // count
    spec = pl.BlockSpec((1, rows, 128 * count), lambda f: (f, 0, at))
    total_spec = pl.BlockSpec((1, count, 2, rows), lambda f: (f, at, 0, 0))
    return pl.pallas_call(
        attend_backward_kernel,
        grid=(frames,),
        in_specs=[spec] * 3 + [total_spec, spec] + [pl.BlockSpec(memory_space=pl.ANY)] * len(earlier),
        out_specs=[spec] * 3,
        out_shape=[jax.ShapeDtypeStruct((frames, rows, width), bf16)] * 3,
        input_output_aliases={5 + i: i for i in range(len(earlier))},
        compiler_params=pltpu.CompilerParams(vmem_limit_bytes=48 << 20),
        cost_estimate=attend_cost(frames, rows, count * 128, 8),
        name="attend_backward",
    )(queries, key_rows, value_rows, totals, grads, *earlier)


def feed_kernel(
    n2_ref,
    n2t_ref,
    g_ref,
    gt_ref,
    bias_ref,
    *refs,
):
    up_refs, down_refs = refs[:4], refs[4:8]
    out_ref, dn2_ref, dup_own_ref, dup_other_ref, ddown_own_ref, ddown_other_ref = refs[8:14]
    db_ref, act_ref, dpre_ref = refs[14:]
    frames, rows = n2_ref.shape[:2]
    blocks, _, part, chunk = dup_own_ref.shape
    half = blocks * part

    @pl.when(pl.program_id(0) == 0)
    def _():
        out_ref[...] = jnp.zeros_like(out_ref)
        dn2_ref[...] = jnp.zeros_like(dn2_ref)
        act_ref[...] = jnp.zeros_like(act_ref)
        dpre_ref[...] = jnp.zeros_like(dpre_ref)

    first = jnp.concatenate(halves(up_refs, 0, 0), 0)
    second = jnp.concatenate(halves(down_refs, 1, 0), 0)
    bias_sum = jnp.zeros((1, chunk), f32)
    for frame in range(frames):
        place = pl.ds(frame * FRAME_LANES, rows)
        pre = dot(n2_ref[frame], first) + bias_ref[0]
        sigma = 0.5 + 0.5 * jnp.tanh(0.851 * pre)
        act = (pre * sigma).astype(bf16)
        act_ref[place] = act
        out_ref[frame] += dot(act, second, NT)
        grad_act = dot(g_ref[frame], second)
        grad_pre = grad_act * (sigma * (1.0 + 1.702 * pre * (1.0 - sigma)))
        grad_low = grad_pre.astype(bf16)
        dpre_ref[place] = grad_low
        bias_sum += jnp.sum(grad_low.astype(f32), 0, keepdims=True)
        dn2_ref[frame] += dot(grad_low, first, NT)
    db_ref[0] = bias_sum

    def place_grad(left_ref, right_ref, own_ref, other_ref):
        grad = dot(left_ref[...], right_ref[...]).astype(bf16)
        own_ref[:, 0] = grad[:half].reshape(blocks, part, chunk)
        other_ref[:, 0] = grad[half:].reshape(blocks, part, chunk)

    place_grad(n2t_ref, dpre_ref, dup_own_ref, dup_other_ref)
    place_grad(gt_ref, act_ref, ddown_own_ref, ddown_other_ref)


def feed_forward(n2, n2t, grads, grads_t, bias, weights):
    frames, rows, _ = n2.shape
    blocks, ff_blocks, part, local = weights[0].shape
    blocks = 2 * blocks
    chunk = min(512, local)
    per = local // chunk
    steps = ff_blocks * per
    deep = n2t.shape[1]
    whole3 = lambda n: (0, 0, 0)
    whole2 = lambda n: (0, 0)
    single = pl.Buffered(1)
    w_spec = pl.BlockSpec((blocks // 2, 1, part, chunk), lambda n: (0, n // per, 0, n % per))
    dw_spec = pl.BlockSpec((blocks, 1, part, chunk), lambda n: (0, n // per, 0, n % per))
    dw_shape = jax.ShapeDtypeStruct((blocks, ff_blocks, part, local), bf16)
    return pl.pallas_call(
        feed_kernel,
        grid=(steps,),
        in_specs=[
            pl.BlockSpec((frames, rows, D), whole3, pipeline_mode=single),
            pl.BlockSpec((D, deep), whole2, pipeline_mode=single),
            pl.BlockSpec((frames, rows, D), whole3, pipeline_mode=single),
            pl.BlockSpec((D, deep), whole2, pipeline_mode=single),
            pl.BlockSpec((1, 1, chunk), lambda n: (n, 0, 0)),
        ]
        + [w_spec] * 8,
        out_specs=[pl.BlockSpec((frames, rows, D), whole3)] * 2
        + [dw_spec] * 4
        + [pl.BlockSpec((1, 1, chunk), lambda n: (n, 0, 0))],
        out_shape=[jax.ShapeDtypeStruct((frames, rows, D), f32)] * 2
        + [dw_shape] * 4
        + [jax.ShapeDtypeStruct((steps, 1, chunk), f32)],
        scratch_shapes=[pltpu.VMEM((deep, chunk), bf16), pltpu.VMEM((deep, chunk), bf16)],
        compiler_params=pltpu.CompilerParams(vmem_limit_bytes=60 << 20),
        cost_estimate=cost(
            12 * frames * rows * D * ff_blocks * local,
            8 * D * ff_blocks * local + 16 * frames * rows * D,
        ),
        name="feed_forward",
    )(n2, n2t, grads, grads_t, bias.reshape(steps, 1, chunk), *weights)


BLOCK = 128
BLOCKS = D // BLOCK


def permuted(ref, info_ref, first):
    return jnp.concatenate(
        [
            ref[:, pl.ds(pl.multiple_of(info_ref[first + i] * BLOCK, BLOCK), BLOCK)]
            for i in range(BLOCKS)
        ],
        1,
    )


def call(
    kernel, info, args, grid, in_specs, out_specs, out_shape, name, scratch=(), flops=0, vmem=56, aliases=None
):
    moved = sum(a.size * a.dtype.itemsize for a in args)
    moved += sum(o.size * o.dtype.itemsize for o in out_shape)
    return pl.pallas_call(
        kernel,
        grid_spec=pltpu.PrefetchScalarGridSpec(
            num_scalar_prefetch=1,
            grid=grid,
            in_specs=in_specs,
            out_specs=out_specs,
            scratch_shapes=list(scratch),
        ),
        out_shape=out_shape,
        input_output_aliases=aliases or {},
        compiler_params=pltpu.CompilerParams(vmem_limit_bytes=vmem << 20),
        cost_estimate=cost(flops, moved),
        name=name,
    )(info, *args)


def shaped(dtype, *shape):
    return jax.ShapeDtypeStruct(shape, dtype)


def once(*block, at=None):
    index = at or (0,) * len(block)
    return pl.BlockSpec(block, lambda *_: index, pipeline_mode=pl.Buffered(1))


def kept(*block):
    index = (0,) * len(block)
    return pl.BlockSpec(block, lambda *_: index)


FRAME_LANES = -(-ROWS // 128) * 128


def row_count(frames):
    return frames * FRAME_LANES


def prepare_kernel(info_ref, tokens_ref, cot_ref, x_ref, g_ref, gt_ref, gsum_ref, hold_ref):
    frames = x_ref.shape[0]
    count = tokens_ref.shape[0]
    inside = lax.broadcasted_iota(jnp.int32, (ROWS, BLOCK), 0) < PATCHES
    hold_ref[...] = jnp.zeros_like(hold_ref)

    def padded(ref):
        hold_ref[0:count] = ref[...].astype(f32)
        return [
            jnp.where(inside, hold_ref[pl.ds(f * PATCHES, ROWS)], 0.0) for f in range(frames)
        ]

    for f, rows in enumerate(padded(tokens_ref)):
        x_ref[f] = rows.astype(bf16)
    grads = padded(cot_ref)
    for f, rows in enumerate(grads):
        g_ref[f] = rows.astype(bf16)
    full = jnp.concatenate([pad_rows(rows, FRAME_LANES) for rows in grads], 0)
    gt_ref[...] = full.T.astype(bf16)
    gsum_ref[...] = jnp.sum(full, 0, keepdims=True)


def prepare(info, tokens, cotangent):
    count = tokens.shape[0]
    frames = count // PATCHES
    deep = row_count(frames)
    taken = pl.BlockSpec((count, BLOCK), lambda r, info_ref: (0, info_ref[r]))
    placed = pl.BlockSpec((frames, ROWS, BLOCK), lambda r, info_ref: (0, 0, r))
    return call(
        prepare_kernel,
        info,
        (tokens, cotangent),
        (BLOCKS,),
        [taken] * 2,
        [
            placed,
            placed,
            pl.BlockSpec((BLOCK, deep), lambda r, info_ref: (r, 0)),
            pl.BlockSpec((1, BLOCK), lambda r, info_ref: (0, r)),
        ],
        [
            shaped(bf16, frames, ROWS, D),
            shaped(bf16, frames, ROWS, D),
            shaped(bf16, D, deep),
            shaped(f32, 1, D),
        ],
        "prepare",
        [pltpu.VMEM((-(-((frames - 1) * PATCHES + ROWS) // 8) * 8, BLOCK), f32)],
    )


def finish_kernel(count, info_ref, *refs):
    in_refs, row_ref, out_ref = refs[:count], refs[count], refs[-1]
    frames = in_refs[0].shape[0]
    for f in range(frames):
        rows = in_refs[0][f]
        for ref in in_refs[1:]:
            rows = rows + ref[f]
        if row_ref.shape[0] == 1:
            rows = rows + row_ref[...]
        else:
            class_row = row_ref[pl.ds(info_ref[2 * BLOCKS] * frames + f, 1)]
            first = lax.broadcasted_iota(jnp.int32, (ROWS, BLOCK), 0) == 0
            rows = rows + jnp.where(first, class_row, 0.0)
        out_ref[pl.ds(f * PATCHES, PATCHES)] = rows[:PATCHES]


def finish(info, parts, row, name, begin=0, count=BLOCKS, earlier=()):
    frames = parts[0].shape[0]
    at = lambda d, info_ref: info_ref[BLOCKS + begin + d]
    taken = pl.BlockSpec((frames, ROWS, BLOCK), lambda d, info_ref: (0, 0, at(d, info_ref)))
    row_spec = pl.BlockSpec((row.shape[0], BLOCK), lambda d, info_ref: (0, at(d, info_ref)))
    return call(
        functools.partial(finish_kernel, len(parts)),
        info,
        (*parts, row, *earlier),
        (count,),
        [taken] * len(parts) + [row_spec] + [pl.BlockSpec(memory_space=pl.ANY)] * len(earlier),
        [pl.BlockSpec((frames * PATCHES, BLOCK), lambda d, info_ref: (0, begin + d))],
        [shaped(f32, frames * PATCHES, D)],
        name,
        aliases={len(parts) + 2: 0} if earlier else {},
    )[0]


def with_message(x_ref, msg_ref, info_ref, f):
    frames = x_ref.shape[0]
    message = msg_ref[pl.ds(info_ref[2 * BLOCKS] * frames + f, 1)]
    place = lax.broadcasted_iota(jnp.int32, (ROWS, D), 0) == PATCHES
    return jnp.where(place, message, x_ref[f].astype(f32))


def put_transposed(ref, rows, f):
    for c in range(BLOCKS):
        block = pad_rows(rows[:, c * BLOCK : (c + 1) * BLOCK].astype(f32), FRAME_LANES)
        place = slice(f * FRAME_LANES, (f + 1) * FRAME_LANES)
        ref[c * BLOCK : (c + 1) * BLOCK, place] = block.T.astype(bf16)


def halves(refs, which, *at):
    sides = []
    for pair in (refs[:2], refs[2:]):
        first, second = (ref[(slice(None), *at)] for ref in pair)
        part, width = first.shape[-2:]
        if which and part == BLOCK:
            blocks = [first[0], second[0], first[1], second[1]]
        else:
            blocks = [v.reshape(-1, width) for v in (first, second)]
        sides.append(jnp.concatenate(blocks, 0))
    return sides


def project_kernel(
    info_ref, x_ref, msg_ref, rel_ref, bias_ref, *refs
):
    a_refs, b_refs, (q_ref, k_ref, v_ref, h_ref) = refs[:4], refs[4:8], refs[8:]
    frames = x_ref.shape[0]

    @pl.when(pl.program_id(0) == 0)
    def _():
        for f in range(frames):
            rows = with_message(x_ref, msg_ref, info_ref, f)
            normed = norm_rows(rows, rel_ref[0:1], rel_ref[1:2])[0].astype(bf16)
            h_ref[pl.ds(f * ROWS, ROWS)] = normed

    for out_ref, weights, bias in (
        (q_ref, halves(a_refs, 0, 0, 0), bias_ref[10:11]),
        (k_ref, halves(a_refs, 0, 0, 1), 0.0),
        (v_ref, halves(b_refs, 1, 0, 0), bias_ref[11:12]),
    ):
        rows = dot(h_ref[...], jnp.concatenate(weights, 0)) + bias
        for f in range(frames):
            out_ref[f] = rows[f * ROWS : (f + 1) * ROWS].astype(bf16)


def project(info, x, message, vec_rel, vectors, attn):
    frames = x.shape[0]
    n, z, _, part, width = attn[0].shape
    columns = vectors.shape[0]
    bias = pl.BlockSpec((columns, width), lambda j, info_ref: (0, j))
    a_spec = pl.BlockSpec((n, 1, 2, part, width), lambda j, info_ref: (0, j, 0, 0, 0))
    b_spec = pl.BlockSpec((n, 1, 1, part, width), lambda j, info_ref: (0, j, 0, 0, 0))
    out = pl.BlockSpec((frames, ROWS, width), lambda j, info_ref: (0, 0, j))
    return call(
        project_kernel,
        info,
        (x, message, vec_rel, vectors, *attn),
        (z,),
        [once(frames, ROWS, D), once(FRAMES, D), once(columns, D), bias]
        + [a_spec] * 4
        + [b_spec] * 4,
        [out] * 3 + [kept(frames * ROWS, D)],
        [shaped(bf16, frames, ROWS, D)] * 3 + [shaped(bf16, frames * ROWS, D)],
        "project",
        (),
        6 * frames * ROWS * D * D,
    )


def transpose_kernel(info_ref, in_ref, out_ref):
    put_transposed(out_ref, in_ref[...], 0)


def transposed(info, rows):
    frames = rows.shape[0] // ROWS
    return call(
        transpose_kernel,
        info,
        (rows,),
        (frames,),
        [pl.BlockSpec((ROWS, D), lambda f, info_ref: (f, 0))],
        [pl.BlockSpec((D, FRAME_LANES), lambda f, info_ref: (0, f))],
        [shaped(bf16, D, row_count(frames))],
        "transposed",
    )[0]


def combine_kernel(
    info_ref, x_ref, a_ref, bias_ref, gain_ref, shift_ref, *refs
):
    b_refs, (mid_ref, n2_ref, n2t_ref) = refs[:4], refs[4:]
    weight = whole_out(b_refs)
    middle = x_ref[0].astype(f32) + bias_ref[...] + dot(a_ref[0], weight, NT)
    mid_ref[0] = middle
    low = middle.astype(bf16).astype(f32)
    normed = norm_rows(low, gain_ref[...], shift_ref[...])[0].astype(bf16)
    n2_ref[0] = normed
    put_transposed(n2t_ref, normed, 0)


def whole_out(b_refs):
    parts = [jnp.concatenate(halves(b_refs, 1, j, 0), 0) for j in range(b_refs[0].shape[1])]
    return jnp.concatenate(parts, 1)


def combine(info, x, attended, vec_rel, attn):
    frames = x.shape[0]
    n, z, _, part, width = attn[4].shape
    frame = pl.BlockSpec((1, ROWS, D), lambda f, info_ref: (f, 0, 0))
    weight = once(n, z, 1, part, width, at=(0, 0, 1, 0, 0))
    return call(
        combine_kernel,
        info,
        (x, attended, vec_rel[12:13], vec_rel[2:3], vec_rel[3:4], *attn[4:]),
        (frames,),
        [frame] * 2 + [once(1, D)] * 3 + [weight] * 4,
        [frame, frame, pl.BlockSpec((D, FRAME_LANES), lambda f, info_ref: (0, f))],
        [
            shaped(f32, frames, ROWS, D),
            shaped(bf16, frames, ROWS, D),
            shaped(bf16, D, row_count(frames)),
        ],
        "combine",
        (),
        2 * frames * ROWS * D * D,
    )


def between_kernel(
    info_ref, ea_ref, eb_ref, mid_ref, g_ref, a_ref, gain_ref, *refs
):
    b_refs, (dmid_ref, da_ref, keep_ref, send_ref, sums_ref, total_ref, dmt_ref) = refs[:4], refs[4:]
    f = pl.program_id(0)
    n, z, part, width = keep_ref.shape
    grad = ea_ref[0] + eb_ref[0]
    low = mid_ref[0].astype(bf16).astype(f32)
    _, scaled, inverse = norm_rows(low, 1.0, 0.0)
    back = norm_back(grad, scaled, inverse, gain_ref[...])
    dmid = (g_ref[0].astype(f32) + back).astype(bf16)
    dmid_ref[0] = dmid
    sums = jnp.concatenate(
        [
            jnp.sum(grad * scaled, 0, keepdims=True),
            jnp.sum(grad, 0, keepdims=True),
            jnp.sum(dmid.astype(f32), 0, keepdims=True),
        ],
        0,
    )

    @pl.when(f == 0)
    def _():
        sums_ref[...] = jnp.zeros_like(sums_ref)
        total_ref[...] = jnp.zeros_like(total_ref)

    sums_ref[...] += sums
    da_ref[0] = dot(dmid, whole_out(b_refs)).astype(bf16)
    put_transposed(dmt_ref, dmid, 0)
    total_ref[...] += dot(dmt_ref[...], pad_rows(a_ref[0], FRAME_LANES))

    @pl.when(f == pl.num_programs(0) - 1)
    def _():
        for j in range(z):
            lanes = slice(j * width, (j + 1) * width)
            for at, ref in ((0, keep_ref), (D // 2, send_ref)):
                ref[:, j] = total_ref[at : at + D // 2, lanes].astype(bf16).reshape(n, part, width)


def between(info, ea, eb, middle, grads, attended, vec_rel, attn):
    frames = ea.shape[0]
    n, z, _, part, width = attn[4].shape
    frame = pl.BlockSpec((1, ROWS, D), lambda f, info_ref: (f, 0, 0))
    weight = once(n, z, 1, part, width, at=(0, 0, 1, 0, 0))
    return call(
        between_kernel,
        info,
        (ea, eb, middle, grads, attended, vec_rel[2:3], *attn[4:]),
        (frames,),
        [frame] * 5 + [once(1, D)] + [weight] * 4,
        [frame, frame, kept(2 * n, z, part, width), kept(2 * n, z, part, width), kept(3, D)],
        [shaped(bf16, frames, ROWS, D)] * 2
        + [shaped(bf16, 2 * n, z, part, width)] * 2
        + [shaped(f32, 3, D)],
        "between",
        [pltpu.VMEM((D, D), f32), pltpu.VMEM((D, row_count(1)), bf16)],
        4 * frames * ROWS * D * D,
    )


def project_grads_kernel(
    info_ref, ht_ref, dq_ref, dk_ref, dv_ref, ok_ref, os_ref, ak_ref, as_ref, bk_ref, bs_ref, sq_ref, sv_ref
):
    frames = dq_ref.shape[0]
    n, _, _, part, width = bk_ref.shape
    bk_ref[:, 0, 1] = ok_ref[:, 0]
    bs_ref[:, 0, 1] = os_ref[:, 0]
    for w, ref in enumerate((dq_ref, dk_ref, dv_ref)):
        rows = jnp.concatenate([pad_rows(ref[f], FRAME_LANES) for f in range(frames)], 0)
        full = dot(ht_ref[...], rows).astype(bf16)
        for at, a_ref, b_ref in ((0, ak_ref, bk_ref), (D // 2, as_ref, bs_ref)):
            grad = full[at : at + D // 2].reshape(n, part, width)
            if w < 2:
                a_ref[:, 0, w] = grad
            else:
                b_ref[:, 0, 0] = grad
        if w != 1:
            (sq_ref if w == 0 else sv_ref)[...] = jnp.sum(rows.astype(f32), 0, keepdims=True)


def project_grads(info, normed_t, grads, out_grads, attn):
    frames = grads[0].shape[0]
    n, z, _, part, width = attn[0].shape
    n = 2 * n
    block = pl.BlockSpec((frames, ROWS, width), lambda j, info_ref: (0, 0, j))
    spec = pl.BlockSpec((n, 1, 2, part, width), lambda j, info_ref: (0, j, 0, 0, 0))
    o_spec = pl.BlockSpec((n, 1, part, width), lambda j, info_ref: (0, j, 0, 0))
    row = pl.BlockSpec((1, width), lambda j, info_ref: (0, j))
    return call(
        project_grads_kernel,
        info,
        (normed_t, *grads, *out_grads),
        (z,),
        [once(*normed_t.shape)] + [block] * 3 + [o_spec] * 2,
        [spec] * 4 + [row] * 2,
        [shaped(bf16, n, z, 2, part, width)] * 4 + [shaped(f32, 1, D)] * 2,
        "project_grads",
        (),
        6 * frames * ROWS * D * D,
    )


def project_back_kernel(
    info_ref, x_ref, msg_ref, dmid_ref, gain_ref, dq_ref, dk_ref, dv_ref, *refs
):
    a_refs, b_refs, (ing_ref, dmsg_ref, sums_ref, total_ref) = refs[:4], refs[4:8], refs[8:]
    frames = x_ref.shape[0]
    j = pl.program_id(0)

    @pl.when(j == 0)
    def _():
        total_ref[...] = jnp.zeros_like(total_ref)

    parts = [halves(a_refs, 0, 0, 0), halves(a_refs, 0, 0, 1), halves(b_refs, 1, 0, 0)]
    weight = jnp.concatenate([jnp.concatenate(v, 0) for v in parts], 1)
    for f in range(frames):
        rows = jnp.concatenate([dq_ref[f], dk_ref[f], dv_ref[f]], 1)
        total_ref[f] += dot(rows, weight, NT)

    @pl.when(j == pl.num_programs(0) - 1)
    def _():
        gain_sum, shift_sum = jnp.zeros((1, D), f32), jnp.zeros((1, D), f32)
        for f in range(frames):
            rows = with_message(x_ref, msg_ref, info_ref, f)
            _, scaled, inverse = norm_rows(rows, 1.0, 0.0)
            grad = total_ref[f]
            gain_sum += jnp.sum(grad * scaled, 0, keepdims=True)
            shift_sum += jnp.sum(grad, 0, keepdims=True)
            back = norm_back(grad, scaled, inverse, gain_ref[...])
            ing_ref[f] = dmid_ref[f].astype(f32) + back
            dmsg_ref[f] = back[PATCHES : PATCHES + 1]
        sums_ref[...] = jnp.concatenate([gain_sum, shift_sum], 0)


def project_back(info, x, message, dmid, vec_rel, grads, attn):
    frames = x.shape[0]
    n, z, _, part, width = attn[0].shape
    block = pl.BlockSpec((frames, ROWS, width), lambda j, info_ref: (0, 0, j))
    a_spec = pl.BlockSpec((n, 1, 2, part, width), lambda j, info_ref: (0, j, 0, 0, 0))
    b_spec = pl.BlockSpec((n, 1, 1, part, width), lambda j, info_ref: (0, j, 0, 0, 0))
    return call(
        project_back_kernel,
        info,
        (x, message, dmid, vec_rel[0:1], *grads, *attn),
        (z,),
        [once(frames, ROWS, D), once(FRAMES, D), once(frames, ROWS, D), once(1, D)]
        + [block] * 3
        + [a_spec] * 4
        + [b_spec] * 4,
        [once(frames, ROWS, D), kept(frames, 1, D), kept(2, D)],
        [shaped(f32, frames, ROWS, D), shaped(f32, frames, 1, D), shaped(f32, 2, D)],
        "project_back",
        [pltpu.VMEM((frames, ROWS, D), f32)],
        6 * frames * ROWS * D * D,
    )


def message_halves(refs, which, i):
    part = D // (4 * refs[0].shape[0])
    return halves([ref.at[:, i * part : (i + 1) * part] for ref in refs], which)


def message_times(rows, refs, i):
    own, other = rows[:, : D // 2], rows[:, D // 2 :]
    cols = []
    for which in range(2):
        weights = message_halves(refs[4 * which : 4 * which + 4], which, i)
        cols.append(dot(own, weights[0]) + dot(other, weights[1]))
    return jnp.concatenate(cols, 1)


def message_times_t(rows, refs, i):
    left, right = rows[:, : D // 2], rows[:, D // 2 :]
    first, second = message_halves(refs[:4], 0, i), message_halves(refs[4:], 1, i)
    return jnp.concatenate(
        [dot(left, first[s], NT) + dot(right, second[s], NT) for s in range(2)], 1
    )


def by_head(rows):
    full = jnp.concatenate([rows.astype(f32)] * HEADS, 0)
    return jnp.where(head_mask(), full, 0.0).astype(bf16)


def head_mask():
    shape = (HEADS * FRAMES, D)
    head = lax.broadcasted_iota(jnp.int32, shape, 0) // FRAMES
    return head == lax.broadcasted_iota(jnp.int32, shape, 1) // HEAD


def over_heads(rows):
    rows = jnp.where(head_mask(), rows, 0.0)
    return jnp.sum(rows.reshape(HEADS, FRAMES, D), 0)


def message_probability(queries, keys):
    scores = dot(by_head(queries), keys, NT) * HEAD**-0.5
    shifted = jnp.exp(scores - jnp.max(scores, 1, keepdims=True))
    return shifted * (1.0 / jnp.sum(shifted, 1, keepdims=True))


def message_forward_kernel(info_ref, cls_ref, rel_ref, *refs):
    weights, (vec_ref, msg_ref, first_ref, pack_ref, hold_ref) = refs[:8], refs[8:]
    vec_ref[...] = permuted(rel_ref, info_ref, BLOCKS)

    def relative(rows):
        hold_ref[...] = rows
        return permuted(hold_ref, info_ref, 0)

    first = message_times(relative(cls_ref[...]).astype(bf16), weights, 0) + vec_ref[6:7]
    normed = norm_rows(first, vec_ref[4:5], vec_ref[5:6])[0].astype(bf16).astype(f32)
    normed_rel = relative(normed).astype(bf16)
    queries = (message_times(normed_rel, weights, 1) + vec_ref[7:8]).astype(bf16)
    keys = message_times(normed_rel, weights, 2).astype(bf16)
    values = (message_times(normed_rel, weights, 3) + vec_ref[8:9]).astype(bf16)
    probability = message_probability(queries, keys).astype(bf16)
    mixed = over_heads(dot(probability, values)).astype(bf16).astype(f32)
    message = first + message_times(relative(mixed).astype(bf16), weights, 4) + vec_ref[9:10]
    msg_ref[...] = relative(message)
    first_ref[...] = first
    for i, rows in enumerate((normed, mixed, queries, keys, values)):
        pack_ref[i] = rows.astype(f32)


def message_forward(info, class_rows, vec_rel, weights):
    one = kept(FRAMES, D)
    return call(
        message_forward_kernel,
        info,
        (class_rows, vec_rel, *weights),
        (1,),
        [one, kept(*vec_rel.shape)] + [once(*w.shape) for w in weights],
        [kept(*vec_rel.shape), one, one, kept(5, FRAMES, D)],
        [
            shaped(f32, *vec_rel.shape),
            shaped(f32, FRAMES, D),
            shaped(f32, FRAMES, D),
            shaped(f32, 5, FRAMES, D),
        ],
        "message_forward",
        [pltpu.VMEM((FRAMES, D), f32)],
        10 * FRAMES * D * D,
    )


def message_backward_kernel(info_ref, dmsg_ref, table_ref, cls_ref, first_ref, pack_ref, vec_ref, *refs):
    weights, (class_ref, sent_ref, hold_ref, rows_ref) = refs[:8], refs[8:]
    frames = dmsg_ref.shape[1]
    for i in range(dmsg_ref.shape[0]):
        place = lax.bitwise_xor(info_ref[2 * BLOCKS], i)
        for f in range(frames):
            hold_ref[i * frames + f : i * frames + f + 1] = dmsg_ref[place, f : f + 1]
    dmsg = permuted(hold_ref, info_ref, BLOCKS)

    def plain(rows):
        hold_ref[...] = rows
        return permuted(hold_ref, info_ref, BLOCKS)

    queries, keys, values = (pack_ref[i].astype(bf16) for i in (2, 3, 4))
    grad_mixed = plain(message_times_t(dmsg.astype(bf16), weights, 4)).astype(bf16)
    probability = message_probability(queries, keys)
    grads_big = by_head(grad_mixed)
    grad_prob = dot(grads_big, values, NT)
    inner = jnp.sum(grad_prob * probability, 1, keepdims=True)
    grad_scores = (probability * (grad_prob - inner)).astype(bf16)
    dq = (over_heads(dot(grad_scores, keys)) * HEAD**-0.5).astype(bf16)
    dk = (dot(grad_scores, by_head(queries), TN) * HEAD**-0.5).astype(bf16)
    dv = dot(probability.astype(bf16), grads_big, TN).astype(bf16)
    grad = plain(
        message_times_t(dq, weights, 1)
        + message_times_t(dk, weights, 2)
        + message_times_t(dv, weights, 3)
    )
    _, scaled, inverse = norm_rows(first_ref[...], 1.0, 0.0)
    back = norm_back(grad, scaled, inverse, vec_ref[4:5])
    dfirst = (dmsg + back).astype(bf16)
    class_ref[...] = message_times_t(dfirst, weights, 0)
    sent = [rows.astype(f32) for rows in (dfirst, dq, dk, dv, dmsg)]
    hold_ref[...] = jnp.zeros_like(hold_ref)
    hold_ref[0:TABLE_REL] = table_ref[0:TABLE_REL]
    table = permuted(hold_ref, info_ref, BLOCKS)
    rows_ref[...] = jnp.zeros_like(rows_ref)
    for i, rows in enumerate([cls_ref[...], pack_ref[0], pack_ref[1]] + sent):
        rows_ref[i * FRAMES : (i + 1) * FRAMES] = rows
    sums = [grad * scaled, grad, sent[0], sent[1], sent[3], dmsg]
    sums = [jnp.sum(rows, 0, keepdims=True) for rows in sums]
    here = [table[i : i + 1] for i in range(TABLE_REL)]
    given = [table_ref[i : i + 1] for i in range(TABLE_REL, table_ref.shape[0])]
    for i, row in enumerate(here[:4] + sums + given[:2] + here[4:] + given[2:]):
        rows_ref[8 * FRAMES + i : 8 * FRAMES + i + 1] = row
    sent_ref[...] = rows_ref[...].astype(bf16)


TABLE_REL = 6
SENT_ROWS = 96


def message_backward(info, dmsg, table, class_rows, first, pack, vectors, weights):
    one = kept(FRAMES, D)
    return call(
        message_backward_kernel,
        info,
        (dmsg, table, class_rows, first, pack, vectors, *weights),
        (1,),
        [kept(*dmsg.shape), kept(*table.shape), one, one, kept(*pack.shape), kept(*vectors.shape)]
        + [once(*w.shape) for w in weights],
        [one, kept(SENT_ROWS, D)],
        [shaped(f32, FRAMES, D), shaped(bf16, SENT_ROWS, D)],
        "message_backward",
        [pltpu.VMEM((FRAMES, D), f32), pltpu.VMEM((SENT_ROWS, D), f32)],
        10 * FRAMES * D * D,
    )


def relative_order():
    return lax.axis_size("dp") * BLOCK == D


def make_info():
    place = lax.iota(jnp.int32, BLOCKS)
    if relative_order():
        mine = lax.axis_index("dp")
        differs = place ^ mine
        places = mine ^ (2 * (place % 4) + place // 4)
        blocks = (differs % 2) * 4 + differs // 2
    else:
        places = blocks = place
    return jnp.concatenate([places, blocks, lax.axis_index("tensor")[None]]).astype(jnp.int32)


def swap(values, axis, bit):
    pairs = [(i, i ^ bit) for i in range(lax.axis_size(axis))]
    return lax.ppermute(values, axis, pairs)


def bits_of(axis):
    size = lax.axis_size(axis)
    return [1 << i for i in range(size.bit_length() - 1)]


def after(values, *earlier):
    return lax.optimization_barrier((values, earlier))[0]


def join_kernel(*refs):
    count = len(refs) // 3
    for i in range(count):
        out_ref = refs[2 * count + i]
        out_ref[0] = refs[2 * i][...]
        out_ref[1] = refs[2 * i + 1][...]


def join(*pairs):
    flat = [v.reshape(-1, v.shape[-1]) for pair in pairs for v in pair]
    specs = [pl.BlockSpec((v.shape[0] // 2, v.shape[1]), lambda i: (i, 0)) for v in flat]
    out = pl.pallas_call(
        join_kernel,
        grid=(2,),
        in_specs=specs,
        out_specs=[
            pl.BlockSpec((2, v.shape[0] // 2, v.shape[1]), lambda i: (0, i, 0)) for v in flat[::2]
        ],
        out_shape=[shaped(bf16, 2, *v.shape) for v in flat[::2]],
        compiler_params=pltpu.CompilerParams(vmem_limit_bytes=48 << 20),
        cost_estimate=cost(0, sum(2 * v.size for v in flat)),
        name="join",
    )(*flat)
    return [v.reshape((2,) + pair[0].shape) for v, pair in zip(out, pairs)]


class Gather:
    def __init__(self, *values):
        self.own, self.place = list(values), 0
        if relative_order():
            self.arrived = [swap(v, "dp", bit) for v, bit in zip(values, (2, 4))]
            return
        self.pieces = []
        for v in values:
            everything = lax.all_gather(v, "dp", axis=0)
            count = everything.shape[0] // 4
            self.pieces += [everything[i * count : (i + 1) * count] for i in range(4)]
        self.arrived = self.pieces

    def step(self):
        if not relative_order():
            return self.pieces
        self.place += 1
        if self.place == 1:
            self.own = join(*zip(self.own, self.arrived))
            self.arrived = [swap(v, "dp", bit) for v, bit in zip(self.own, (4, 2))]
            return self.own
        self.pieces = [v for pair in zip(self.own, self.arrived) for v in pair]
        self.arrived = [swap(v, "dp", 1) for v in self.pieces]
        return self.pieces

    def result(self):
        if not relative_order():
            return self.pieces
        return [v for i in (0, 2) for v in self.pieces[i : i + 2] + self.arrived[i : i + 2]]


def beside(outputs, *transfers):
    outputs, arrived = lax.optimization_barrier((outputs, [t.arrived for t in transfers]))
    for t, values in zip(transfers, arrived):
        t.arrived = values
    return outputs


def add_low(left_side, right_side):
    return (left_side.astype(f32) + right_side.astype(f32)).astype(bf16)


def add_kernel(axes, *refs):
    ins, outs = refs[: 2 * len(axes)], refs[2 * len(axes) :]
    for i, axis in enumerate(axes):
        for side in range(2):
            at = (side,) if axis == 0 else (slice(None), side)
            outs[2 * i + side][...] = add_low(ins[2 * i][at], ins[2 * i + 1][at])


def add_and_split(pairs, axes):
    lead = pairs[0][0].shape[:-2]
    rows, width = pairs[0][0].shape[-2:]
    steps = 2 if rows % 32 == 0 else 1
    zeros = (0,) * len(lead)
    spec = pl.BlockSpec((*lead, rows // steps, width), lambda i: (*zeros, i, 0))
    out = pl.BlockSpec((*lead[1:], rows // steps, width), lambda i: (*zeros[1:], i, 0))
    return pl.pallas_call(
        functools.partial(add_kernel, axes),
        grid=(steps,),
        in_specs=[spec] * (2 * len(pairs)),
        out_specs=[out] * (2 * len(pairs)),
        out_shape=[shaped(bf16, *lead[1:], rows, width)] * (2 * len(pairs)),
        compiler_params=pltpu.CompilerParams(vmem_limit_bytes=48 << 20),
        cost_estimate=cost(0, sum(4 * a.size for a, _ in pairs)),
        name="add",
    )(*[v for pair in pairs for v in pair])


class Scatter:
    def __init__(self, keep, send):
        self.place, self.shape = 0, keep[0].shape[1:]
        if not relative_order():
            self.held = [
                lax.psum_scatter(jnp.concatenate(v, 0), "dp", scatter_dimension=0, tiled=False)
                for v in zip(keep, send)
            ]
            self.arrived = [jnp.zeros_like(v) for v in self.held]
            return
        width = self.shape[-1]
        self.held = [v.reshape(2, 2, -1, width) for v in keep]
        self.arrived = [swap(v, "dp", 1).reshape(2, 2, -1, width) for v in send]

    def step(self):
        if not relative_order():
            return list(self.held)
        axes, bits = ((0, 1), (4, 2)) if self.place == 0 else ((0, 0), (2, 4))
        self.place += 1
        sums = list(add_and_split(list(zip(self.held, self.arrived)), axes))
        self.held, going = sums[::2], sums[1::2]
        self.arrived = [swap(v, "dp", bit) for v, bit in zip(going, bits)]
        return going


def pair_kernel(info_ref, *refs):
    ins, outs = refs[:-2], refs[-2:]
    rows = ins[0].shape[1]
    for side in range(2):
        for i in range(len(ins) // 4):
            total = add_low(ins[4 * i + side][0], ins[4 * i + 2 + side][0])
            outs[side][0, i * rows : (i + 1) * rows] = total


def add_and_pair(info, held, arrived):
    count = len(held)
    rows, width = held[0][0].size // held[0].shape[-1], held[0].shape[-1]
    own = pl.BlockSpec((1, rows, width), lambda h, ref: (2 * h + ref[2 * BLOCKS] % 2, 0, 0))
    other = pl.BlockSpec((1, rows, width), lambda h, ref: (2 * h + 1 - ref[2 * BLOCKS] % 2, 0, 0))
    flat = [v.reshape(4, rows, width) for pair in zip(held, arrived) for v in pair for _ in range(2)]
    out = pl.BlockSpec((1, count * rows, width), lambda h, ref: (h, 0, 0))
    return call(
        pair_kernel,
        info,
        flat,
        (2,),
        [own, other] * (2 * count),
        [out] * 2,
        [shaped(bf16, 2, count * rows, width)] * 2,
        "add_and_pair",
    )


def single_kernel(info_ref, ho_ref, hp_ref, ao_ref, ap_ref, held_ref, going_ref):
    held_ref[...] = add_low(ho_ref[0], ao_ref[0])
    going_ref[...] = add_low(hp_ref[0], ap_ref[0])


def add_and_single(info, held, arrived):
    _, rows, width = held.shape
    own = pl.BlockSpec((1, rows, width), lambda i, ref: (ref[2 * BLOCKS] // 2, 0, 0))
    other = pl.BlockSpec((1, rows, width), lambda i, ref: (1 - ref[2 * BLOCKS] // 2, 0, 0))
    return call(
        single_kernel,
        info,
        (held, held, arrived, arrived),
        (1,),
        [own, other] * 2,
        [kept(rows, width)] * 2,
        [shaped(bf16, rows, width)] * 2,
        "add_and_single",
    )


class ScatterVideos:
    def __init__(self, info, *scatters):
        self.info, self.shape = info, scatters[0].shape
        self.direct = lax.axis_size("tensor") != 4
        held = [v.reshape(self.shape) for s in scatters for v in s.held]
        arrived = [v.reshape(self.shape) for s in scatters for v in s.arrived]
        if self.direct:
            values = jnp.stack([add_low(h, a) for h, a in zip(held, arrived)], 1)
            self.held = lax.psum_scatter(values, "tensor", scatter_dimension=0, tiled=False)
            self.going, self.arrived = self.held, jnp.zeros_like(self.held)
            return
        self.held, self.going = add_and_pair(info, held, arrived)
        self.arrived = swap(self.going, "tensor", 1)

    def step(self):
        self.add()
        return self.send()

    def add(self):
        if not self.direct:
            self.held, self.going = add_and_single(self.info, self.held, self.arrived)
        return self.held, self.going

    def send(self, *earlier):
        if not self.direct:
            self.going = after(self.going, *earlier) if earlier else self.going
            self.arrived = swap(self.going, "tensor", 2)
        return self.going

    def result(self):
        return add_low(self.held, self.arrived).reshape((-1,) + self.shape[1:])


class GatherSmall:
    def __init__(self, values):
        half = values.shape[0] // 2
        self.bits = [(2, 4), (4, 2), (1, 1)]
        if relative_order():
            self.values = [values[None, :half], values[None, half:]]
            self.send()
        else:
            self.values = self.arrived = [lax.all_gather(values, "dp", axis=0)]

    def send(self):
        self.arrived = [swap(v, "dp", bit) for v, bit in zip(self.values, self.bits[0])]

    def step(self):
        if relative_order():
            pairs = zip(self.values, self.arrived)
            self.values = [jnp.concatenate(pair, 0) for pair in pairs]
            self.bits = self.bits[1:]
            if self.bits:
                self.send()
        return self.values

    def result(self):
        if not relative_order():
            return self.values[0]
        first, second = self.values
        order = (0, 2, 1, 3, 4, 6, 5, 7)
        return jnp.concatenate([first, jnp.stack([second[i] for i in order])], 1)


def sum_everywhere(values):
    rounds = [("dp", bits_of("dp")[:1])]
    for axis, bits in (("dp", bits_of("dp")[1:]), ("tensor", bits_of("tensor"))):
        rounds += [(axis, bits[i : i + 2]) for i in range(0, len(bits), 2)]
    for axis, bits in rounds:
        if len(bits) == 1:
            values = values + swap(values, axis, bits[0])
            continue
        first, second, both = (swap(values, axis, b) for b in (*bits, sum(bits)))
        values = (values + first) + (second + both)
    return values


class VideoRows:
    def __init__(self, values, sums):
        self.values, self.sums, self.bits = values[None], sums, bits_of("tensor")
        self.send()

    def send(self):
        rows = jnp.concatenate([self.sums, self.values.reshape(-1, D)], 0)
        self.arrived = swap(rows, "tensor", self.bits[0])

    def step(self):
        count = self.sums.shape[0]
        self.sums = self.sums + self.arrived[:count]
        others = self.arrived[count:].reshape(self.values.shape)
        self.values = jnp.concatenate([self.values, others], 0)
        self.bits = self.bits[1:]
        if self.bits:
            self.send()


def adam_step(weight, first_moment, second_moment, gradient, factor, step_rate, decay_rate):
    clipped = gradient * factor
    first_new = beta_one * first_moment + (1.0 - beta_one) * clipped
    second_new = beta_two * second_moment + (1.0 - beta_two) * clipped * clipped
    update = (
        first_new
        / (1.0 - beta_one**STEP)
        / (jnp.sqrt(second_new / (1.0 - beta_two**STEP)) + adam_eps)
    )
    weight_new = weight - step_rate * (update + decay_rate * weight)
    return (first_new, second_new, weight_new)


def on_device(
    tokens,
    cotangent,
    attn_master,
    attn_first,
    attn_second,
    attn_ema,
    mlp_master,
    mlp_first,
    mlp_second,
    mlp_ema,
    msg_master,
    msg_first,
    msg_second,
    msg_ema,
    vec_master,
    vec_first,
    vec_second,
    vec_ema,
):
    z_index = lax.axis_index("tensor")
    z_count = lax.axis_size("tensor")
    dp_index = lax.axis_index("dp")
    part = attn_master.shape[0]
    local_width = attn_master.shape[2]
    local_ff = mlp_master.shape[2]
    frames = tokens.shape[0] // PATCHES
    half_ff = local_ff // 2
    info = make_info()

    class_own = jnp.concatenate(
        [tokens[f * PATCHES : f * PATCHES + 1] for f in range(frames)], 0
    ).reshape(-1, local_width)
    attn_low = jnp.swapaxes(attn_master, 0, 1).astype(bf16).reshape(4 * part, local_width)
    attn_rows = pad_rows(jnp.concatenate([attn_low, class_own], 0), 4 * part + 16)
    attn_z = lax.all_gather(attn_rows, "tensor", axis=0)
    mlp_z = lax.all_gather(jnp.swapaxes(mlp_master, 0, 1).astype(bf16), "tensor", axis=0)
    class_rows = attn_z[:, 4 * part : 4 * part + class_own.shape[0]].reshape(FRAMES, D)
    attn_z = attn_z[:, : 4 * part].reshape(z_count, 4, part, local_width)

    msg_low = jnp.swapaxes(msg_master, 0, 1).astype(bf16).reshape(5 * part, D)
    vec_count = vec_master.shape[1]
    vec_low = jnp.pad(vec_master.astype(bf16).T, ((0, 32 - vec_count), (0, D // 2 - part)))
    msg_go = Gather(jnp.concatenate([msg_low[:, : D // 2], vec_low], 0), msg_low[:, D // 2 :])
    prepared = prepare(info, tokens, cotangent)
    x, grads, grads_t, grad_sum = beside(prepared, msg_go)
    sent_msg = msg_go.step()
    attn_z = after(attn_z, *sent_msg)
    attn_go = Gather(attn_z[:, :2], attn_z[:, 2:])
    sent_attn = attn_go.step()
    beside(sent_attn, msg_go)
    sent_msg = msg_go.step()
    mlp_z = after(mlp_z, *sent_msg)
    mlp_half = [
        [mlp_z[:, i, :, j * half_ff : (j + 1) * half_ff] for i in range(2)] for j in range(2)
    ]
    mlp_go = [Gather(*mlp_half[0])]
    msg_w = msg_go.result()
    vec_rel = jnp.concatenate(msg_w[:4], 0)[:, 5 * part : 5 * part + vec_count, :part]
    vec_rel = jnp.moveaxis(vec_rel, 0, 1).reshape(-1, D).astype(f32)

    sent_mlp = mlp_go[0].own + mlp_half[1]
    vectors, message, first_msg, msg_pack = beside(
        message_forward(info, after(class_rows, *sent_mlp).astype(f32), vec_rel, msg_w), attn_go
    )
    ff_bias = vectors[14:].reshape(z_count, 2, half_ff)
    attn_go.step()
    attn_w = attn_go.result()
    projected = project(info, x, message, vec_rel, vectors, attn_w)
    queries, key_rows, value_rows, normed = beside(projected, mlp_go[0])
    sent_mlp = mlp_go[0].step()
    attended, totals = beside(
        attend_forward(after(queries, *sent_mlp), key_rows, value_rows), mlp_go[0]
    )
    sent_mlp = mlp_go[0].step()
    mlp_go.append(Gather(*after(mlp_half[1], attended)))
    middle, n2, n2_t = beside(
        combine(info, x, after(attended, *sent_mlp), vec_rel, attn_w), *mlp_go
    )
    sent_mlp = mlp_go[1].step()
    n2 = after(n2, *sent_mlp)

    def feed(j, n2):
        return feed_forward(n2, n2_t, grads, grads_t, ff_bias[:, j], mlp_go[j].result())

    out_0, dn2_0, *dw_0, db_0 = beside(feed(0, n2), mlp_go[1])
    sent_mlp = mlp_go[1].step()
    normed_t = beside(transposed(info, after(normed, *sent_mlp)), mlp_go[1])
    dw_0 = after(dw_0, normed_t)
    sums_0 = Scatter(dw_0[::2], dw_0[1::2])
    out_1, dn2_1, *dw_1, db_1 = beside(feed(1, after(n2, normed_t)), sums_0)
    sums_1 = Scatter(dw_1[::2], dw_1[1::2])
    going = sums_0.step()
    dmid, grad_attended, *grad_out_w, sums_two = beside(
        between(info, after(dn2_0, *going), dn2_1, middle, grads, attended, vec_rel, attn_w), sums_1
    )
    going = sums_1.step()
    pairs = HEADS // 2
    back = (queries, key_rows, value_rows, totals)
    grad_qkv = beside(
        attend_backward(*back, after(grad_attended, *going), 0, pairs // 2), sums_0
    )
    going = sums_0.step()
    grad_qkv = beside(
        attend_backward(
            *back, after(grad_attended, *going), pairs // 2, pairs - pairs // 2, grad_qkv
        ),
        sums_0,
        sums_1,
    )
    going = sums_1.step()
    dqk_keep, dqk_send, dvo_keep, dvo_send, sum_q, sum_v = beside(
        project_grads(info, after(normed_t, *going), grad_qkv, grad_out_w, attn_w), sums_1
    )
    sums_attn = Scatter([dqk_keep, dvo_keep], [dqk_send, dvo_send])
    mlp_go = ScatterVideos(info, sums_0, sums_1)
    block_output = beside(
        finish(info, [after(middle, mlp_go.going), out_0, out_1], vec_rel[13:14], "block_output"),
        sums_attn,
    )
    going = sums_attn.step()
    ing, dmsg, sums_one = beside(
        project_back(info, after(x, *going), message, dmid, vec_rel, grad_qkv, attn_w),
        sums_attn,
        mlp_go,
    )
    going = sums_attn.step()

    ff_bias_grad = jnp.stack(
        [db.reshape(z_count, half_ff) for db in (db_0, db_1)], 1
    ).reshape(FF // D, D)
    table = jnp.concatenate([sums_one, sums_two, grad_sum, sum_q, sum_v, ff_bias_grad], 0)
    dmsg = dmsg[:, 0].astype(bf16).astype(f32)
    rows = VideoRows(after(dmsg, *going), table)
    mlp_go.held, mlp_go.going = beside(mlp_go.add(), rows)
    rows.step()
    rows.arrived = after(rows.arrived, mlp_go.going)
    rows.step()
    sent_mlp = mlp_go.send(rows.values)
    dmsg = beside(after(rows.values, sent_mlp), sums_attn)
    attn_go = ScatterVideos(info, sums_attn)
    grad_class, sent = beside(
        message_backward(
            info,
            after(dmsg, attn_go.going),
            rows.sums,
            class_rows.astype(f32),
            first_msg,
            msg_pack,
            vectors,
            msg_w,
        ),
        attn_go,
        mlp_go,
    )
    mlp_sum = mlp_go.result()
    going = attn_go.step()

    small = GatherSmall(after(sent, going))
    input_grad = beside(
        finish(info, [after(ing, *small.values)], grad_class, "input_grad"), small, attn_go
    )
    small.step()
    attn_grad = attn_go.result()
    mlp_grad = jnp.concatenate([mlp_sum[:2], mlp_sum[2:]], 2)
    mlp_grad = jnp.swapaxes(mlp_grad, 0, 1).astype(f32)
    attn_grad = jnp.swapaxes(attn_grad.reshape(4, part, local_width), 0, 1).astype(f32)
    squares = jnp.sum(attn_grad * attn_grad) + jnp.sum(mlp_grad * mlp_grad)
    squares = beside(squares, small)
    small.step()
    small.step()
    everyone = small.result()
    tables = everyone[:, 8 * FRAMES : 8 * FRAMES + vec_count]
    tables = lax.dynamic_slice_in_dim(tables, dp_index * part, part, 2)
    vec_grad = jnp.sum(tables.astype(f32), 0).T
    everyone = everyone[:, : 8 * FRAMES].reshape(-1, 8, FRAMES, D)
    everyone = jnp.moveaxis(everyone, 0, 1).reshape(8, -1, D)
    mine = lax.dynamic_slice_in_dim(everyone[:3], dp_index * part, part, 2)
    msg_grad = jnp.stack(
        [
            dot(mine[0], everyone[3], TN),
            dot(mine[1], everyone[4], TN),
            dot(mine[1], everyone[5], TN),
            dot(mine[1], everyone[6], TN),
            dot(mine[2], everyone[7], TN),
        ],
        1,
    )

    keep_share = (z_index == 0).astype(f32)
    squares = squares + keep_share * (
        jnp.sum(msg_grad * msg_grad) + jnp.sum(vec_grad * vec_grad)
    )
    squares = sum_everywhere(jnp.broadcast_to(squares, (8, 128)))[0, 0]
    grad_norm = jnp.sqrt(squares)
    factor = clip_limit / jnp.maximum(grad_norm, clip_limit)

    def update(master, first, second, ema, grad, rate, decay):
        first_new, second_new, weight = adam_step(master, first, second, grad, factor, rate, decay)
        return grad, first_new, second_new, weight, ema_keep * ema + (1.0 - ema_keep) * weight

    return (
        block_output,
        input_grad,
        grad_norm,
        *update(attn_master, attn_first, attn_second, attn_ema, attn_grad, rate_mat, decay_mat),
        *update(mlp_master, mlp_first, mlp_second, mlp_ema, mlp_grad, rate_mat, decay_mat),
        *update(msg_master, msg_first, msg_second, msg_ema, msg_grad, rate_mat, decay_mat),
        *update(vec_master, vec_first, vec_second, vec_ema, vec_grad, rate_vec, 0.0),
    )


def solution(mesh):
    rows = P(("dp", "tensor"), None)
    split = P("dp", None, "tensor")
    copied = P("dp", None, None)
    table = P("dp", None)
    in_specs = (rows,) * 2 + (split,) * 8 + (copied,) * 4 + (table,) * 4
    out_specs = (rows,) * 2 + (P(),) + (split,) * 10 + (copied,) * 5 + (table,) * 5
    return jax.shard_map(
        on_device, mesh=mesh, in_specs=in_specs, out_specs=out_specs, check_vma=False
    )
```

```python
import functools

import jax
import jax.numpy as jnp
from jax import lax
from jax.experimental import pallas as pl
from jax.experimental.pallas import tpu as pltpu
from jax.sharding import PartitionSpec as P

D = 1024
HEADS = 16
HEAD = 64
FF = 4096
PATCHES = 577
FRAMES = 8
STEP = 10
ROWS = 592


norm_eps = 1e-05
beta_one = 0.9
beta_two = 0.95
adam_eps = 1e-08
decay_mat = 0.05
ema_keep = 0.7
clip_limit = 1.0
rate_mat = 0.02
rate_vec = 0.4
far_below = -1e30
COST_PART = 16
bf16 = jnp.bfloat16
f32 = jnp.float32
NN = (((1,), (0,)), ((), ()))
NT = (((1,), (1,)), ((), ()))
TN = (((0,), (0,)), ((), ()))


def dot(left_side, right_side, dims=NN):
    return lax.dot_general(left_side, right_side, dims, preferred_element_type=f32)


def norm_rows(values, gain_row, shift_row):
    centre = values - jnp.mean(values, -1, keepdims=True)
    spread = jnp.mean(centre * centre, -1, keepdims=True)
    inverse = lax.rsqrt(spread + norm_eps)
    scaled = centre * inverse
    return (scaled * gain_row + shift_row, scaled, inverse)


def norm_back(gradient, scaled, inverse, gain_row):
    inner = gradient * gain_row
    return inverse * (
        inner
        - jnp.mean(inner, -1, keepdims=True)
        - scaled * jnp.mean(inner * scaled, -1, keepdims=True)
    )


def pad_rows(values, count):
    if values.shape[0] == count:
        return values
    extra = jnp.zeros((count - values.shape[0],) + values.shape[1:], values.dtype)
    return jnp.concatenate([values, extra], 0)


def head_pair(queries, key_rows, head):
    lane = lax.broadcasted_iota(jnp.int32, queries.shape, 1)
    key_lane = lax.broadcasted_iota(jnp.int32, key_rows.shape, 1)
    key_row = lax.broadcasted_iota(jnp.int32, key_rows.shape, 0)
    spare = HEAD * (1 - head)
    mask = jnp.where(
        (key_lane == spare) & (key_row > PATCHES), jnp.asarray(far_below, bf16), jnp.asarray(0, bf16)
    )
    keys_one = jnp.where((key_lane // HEAD) == head, key_rows, mask)
    queries_one = jnp.where(lane == spare, jnp.asarray(1, bf16), queries)
    return queries_one, keys_one


def each_head(values):
    lane = lax.broadcasted_iota(jnp.int32, values.shape, 1)
    zero = jnp.zeros_like(values)
    return jnp.concatenate(
        [jnp.where(lane < HEAD, values, zero), jnp.where(lane < HEAD, zero, values)], 0
    )


def attend_forward_kernel(q_ref, k_ref, v_ref, out_ref, total_ref):
    rows, width = q_ref.shape[1:]
    key_count = -(-rows // 128) * 128
    lane = lax.broadcasted_iota(jnp.int32, (rows, 128), 1)
    out_of = lax.broadcasted_iota(jnp.int32, (rows, 128), 1) > PATCHES - (key_count - 128)
    pairs = width // 128

    def score(pair):
        lanes = slice(pair * 128, (pair + 1) * 128)
        queries = q_ref[0, :, lanes] * jnp.asarray(HEAD**-0.5, bf16)
        return dot(queries, each_head(pad_rows(k_ref[0, :, lanes], key_count)), NT)

    waiting = [score(0)]
    for pair in range(pairs):
        if pair + 1 < pairs:
            waiting.append(score(pair + 1))
        both = waiting.pop(0)
        shares, totals, sums = [], [], []
        for head in range(2):
            scores = both[:, head * key_count : (head + 1) * key_count]
            tail = jnp.where(out_of, far_below, scores[:, key_count - 128 :])
            scores = jnp.concatenate([scores[:, : key_count - 128], tail], 1)
            highest = jnp.max(scores, 1, keepdims=True)
            shifted = jnp.exp(scores - highest)
            total = jnp.sum(shifted, 1, keepdims=True)
            shares.append(shifted.astype(bf16))
            sums.append(1.0 / total)
            totals.append(highest + jnp.log(total))
        lanes = slice(pair * 128, (pair + 1) * 128)
        out = dot(jnp.concatenate(shares, 1), each_head(pad_rows(v_ref[0, :, lanes], key_count)))
        out_ref[0, :, lanes] = (out * jnp.where(lane < HEAD, *sums)).astype(bf16)
        logs = jnp.where(lane < HEAD, *totals).T
        total_ref[0, pair] = jnp.concatenate([logs[0:1], logs[HEAD : HEAD + 1]], 0)


def attend_backward_kernel(q_ref, k_ref, v_ref, total_ref, grad_ref, *rest):
    dq_ref, dk_ref, dv_ref = rest[-3:]
    rows, width = q_ref.shape[1:]
    count = -(-rows // 128) * 128
    pairs = width // 128
    tail = rows // 16 * 16 - 16
    out_of = lax.broadcasted_iota(jnp.int32, (rows - tail, count), 0) > PATCHES - tail

    def swapped(values):
        return jnp.concatenate([values[:, HEAD:], values[:, :HEAD]], 1)

    def load(pair):
        lanes = slice(pair * 128, (pair + 1) * 128)
        queries = pad_rows(q_ref[0, :, lanes], count) * jnp.asarray(HEAD**-0.5, bf16)
        return lanes, queries, pad_rows(grad_ref[0, :, lanes], count)

    def start(pair):
        lanes, queries, grads = load(pair)
        keys, values = k_ref[0, :, lanes], swapped(v_ref[0, :, lanes])
        first = lax.broadcasted_iota(jnp.int32, (rows, 128), 1) < HEAD
        queries, grads = each_head(queries), each_head(swapped(grads))
        products = []
        for head in range(2):
            mixed = jnp.where(first, keys, values) if head == 0 else jnp.where(first, values, keys)
            right = [
                queries[head * count : (head + 1) * count],
                grads[(1 - head) * count : (2 - head) * count],
            ]
            products.append(dot(mixed, jnp.concatenate(right, 0), NT))
        return products

    waiting = [start(0)]
    for pair in range(pairs):
        if pair + 1 < pairs:
            waiting.append(start(pair + 1))
        products = waiting.pop(0)
        lanes, queries, grads = load(pair)
        shares, grad_scores = [], []
        for head in range(2):
            total = total_ref[0, pair, head : head + 1, :]
            total = jnp.concatenate([total, jnp.zeros((1, count - rows), f32)], 1)
            share = jnp.exp(products[head][:, :count] - total)
            share = jnp.concatenate([share[:tail], jnp.where(out_of, 0.0, share[tail:])], 0)
            grad_share = products[head][:, count:]
            inner = jnp.sum(grad_share * share, 0, keepdims=True)
            grad_scores.append((share * (grad_share - inner)).astype(bf16))
            shares.append(share.astype(bf16))
        dv_ref[0, :, lanes] = dot(jnp.concatenate(shares, 1), each_head(grads)).astype(bf16)
        dk_ref[0, :, lanes] = dot(jnp.concatenate(grad_scores, 1), each_head(queries)).astype(bf16)
        keys_t = pad_rows(k_ref[0, :, lanes], count).astype(f32).T.astype(bf16)
        back = [
            dot(keys_t[HEAD * head : HEAD * (head + 1)], pad_rows(grad_scores[head], count))
            for head in range(2)
        ]
        dq_ref[0, :, lanes] = (jnp.concatenate(back, 0) * HEAD**-0.5).T[:rows].astype(bf16)


def cost(flops, moved):
    return pl.CostEstimate(
        flops=flops // COST_PART, bytes_accessed=moved // COST_PART, transcendentals=0
    )


def attend_cost(frames, rows, width, matmuls):
    return cost(2 * matmuls * frames * rows * rows * width, 4 * matmuls * frames * rows * width)


def attend_forward(queries, key_rows, value_rows):
    frames, rows, width = queries.shape
    spec = pl.BlockSpec((1, rows, width), lambda f: (f, 0, 0))
    return pl.pallas_call(
        attend_forward_kernel,
        grid=(frames,),
        in_specs=[spec] * 3,
        out_specs=[spec, pl.BlockSpec((1, width // 128, 2, rows), lambda f: (f, 0, 0, 0))],
        out_shape=[
            jax.ShapeDtypeStruct((frames, rows, width), bf16),
            jax.ShapeDtypeStruct((frames, width // 128, 2, rows), f32),
        ],
        compiler_params=pltpu.CompilerParams(vmem_limit_bytes=48 << 20),
        cost_estimate=attend_cost(frames, rows, width, 4),
        name="attend_forward",
    )(queries, key_rows, value_rows)


def attend_backward(queries, key_rows, value_rows, totals, grads, begin, count, earlier=()):
    frames, rows, width = queries.shape
    at = begin // count
    spec = pl.BlockSpec((1, rows, 128 * count), lambda f: (f, 0, at))
    total_spec = pl.BlockSpec((1, count, 2, rows), lambda f: (f, at, 0, 0))
    return pl.pallas_call(
        attend_backward_kernel,
        grid=(frames,),
        in_specs=[spec] * 3 + [total_spec, spec] + [pl.BlockSpec(memory_space=pl.ANY)] * len(earlier),
        out_specs=[spec] * 3,
        out_shape=[jax.ShapeDtypeStruct((frames, rows, width), bf16)] * 3,
        input_output_aliases={5 + i: i for i in range(len(earlier))},
        compiler_params=pltpu.CompilerParams(vmem_limit_bytes=48 << 20),
        cost_estimate=attend_cost(frames, rows, count * 128, 8),
        name="attend_backward",
    )(queries, key_rows, value_rows, totals, grads, *earlier)


def feed_kernel(
    n2_ref,
    n2t_ref,
    g_ref,
    gt_ref,
    bias_ref,
    *refs,
):
    up_refs, down_refs = refs[:4], refs[4:8]
    out_ref, dn2_ref, dup_own_ref, dup_other_ref, ddown_own_ref, ddown_other_ref = refs[8:14]
    db_ref, act_ref, dpre_ref = refs[14:]
    frames, rows = n2_ref.shape[:2]
    blocks, _, part, chunk = dup_own_ref.shape
    half = blocks * part

    @pl.when(pl.program_id(0) == 0)
    def _():
        out_ref[...] = jnp.zeros_like(out_ref)
        dn2_ref[...] = jnp.zeros_like(dn2_ref)
        act_ref[...] = jnp.zeros_like(act_ref)
        dpre_ref[...] = jnp.zeros_like(dpre_ref)

    first = jnp.concatenate(halves(up_refs, 0, 0), 0)
    second = jnp.concatenate(halves(down_refs, 1, 0), 0)
    bias_sum = jnp.zeros((1, chunk), f32)
    for frame in range(frames):
        place = pl.ds(frame * FRAME_LANES, rows)
        pre = dot(n2_ref[frame], first) + bias_ref[0]
        sigma = 0.5 + 0.5 * jnp.tanh(0.851 * pre)
        act = (pre * sigma).astype(bf16)
        act_ref[place] = act
        out_ref[frame] += dot(act, second, NT)
        grad_act = dot(g_ref[frame], second)
        grad_pre = grad_act * (sigma * (1.0 + 1.702 * pre * (1.0 - sigma)))
        grad_low = grad_pre.astype(bf16)
        dpre_ref[place] = grad_low
        bias_sum += jnp.sum(grad_low.astype(f32), 0, keepdims=True)
        dn2_ref[frame] += dot(grad_low, first, NT)
    db_ref[0] = bias_sum

    def place_grad(left_ref, right_ref, own_ref, other_ref):
        grad = dot(left_ref[...], right_ref[...]).astype(bf16)
        own_ref[:, 0] = grad[:half].reshape(blocks, part, chunk)
        other_ref[:, 0] = grad[half:].reshape(blocks, part, chunk)

    place_grad(n2t_ref, dpre_ref, dup_own_ref, dup_other_ref)
    place_grad(gt_ref, act_ref, ddown_own_ref, ddown_other_ref)


def feed_forward(n2, n2t, grads, grads_t, bias, weights):
    frames, rows, _ = n2.shape
    blocks, ff_blocks, part, local = weights[0].shape
    blocks = 2 * blocks
    chunk = min(512, local)
    per = local // chunk
    steps = ff_blocks * per
    deep = n2t.shape[1]
    whole3 = lambda n: (0, 0, 0)
    whole2 = lambda n: (0, 0)
    single = pl.Buffered(1)
    w_spec = pl.BlockSpec((blocks // 2, 1, part, chunk), lambda n: (0, n // per, 0, n % per))
    dw_spec = pl.BlockSpec((blocks, 1, part, chunk), lambda n: (0, n // per, 0, n % per))
    dw_shape = jax.ShapeDtypeStruct((blocks, ff_blocks, part, local), bf16)
    return pl.pallas_call(
        feed_kernel,
        grid=(steps,),
        in_specs=[
            pl.BlockSpec((frames, rows, D), whole3, pipeline_mode=single),
            pl.BlockSpec((D, deep), whole2, pipeline_mode=single),
            pl.BlockSpec((frames, rows, D), whole3, pipeline_mode=single),
            pl.BlockSpec((D, deep), whole2, pipeline_mode=single),
            pl.BlockSpec((1, 1, chunk), lambda n: (n, 0, 0)),
        ]
        + [w_spec] * 8,
        out_specs=[pl.BlockSpec((frames, rows, D), whole3)] * 2
        + [dw_spec] * 4
        + [pl.BlockSpec((1, 1, chunk), lambda n: (n, 0, 0))],
        out_shape=[jax.ShapeDtypeStruct((frames, rows, D), f32)] * 2
        + [dw_shape] * 4
        + [jax.ShapeDtypeStruct((steps, 1, chunk), f32)],
        scratch_shapes=[pltpu.VMEM((deep, chunk), bf16), pltpu.VMEM((deep, chunk), bf16)],
        compiler_params=pltpu.CompilerParams(vmem_limit_bytes=60 << 20),
        cost_estimate=cost(
            12 * frames * rows * D * ff_blocks * local,
            8 * D * ff_blocks * local + 16 * frames * rows * D,
        ),
        name="feed_forward",
    )(n2, n2t, grads, grads_t, bias.reshape(steps, 1, chunk), *weights)


BLOCK = 128
BLOCKS = D // BLOCK


def permuted(ref, info_ref, first):
    return jnp.concatenate(
        [
            ref[:, pl.ds(pl.multiple_of(info_ref[first + i] * BLOCK, BLOCK), BLOCK)]
            for i in range(BLOCKS)
        ],
        1,
    )


def call(
    kernel, info, args, grid, in_specs, out_specs, out_shape, name, scratch=(), flops=0, vmem=56, aliases=None
):
    moved = sum(a.size * a.dtype.itemsize for a in args)
    moved += sum(o.size * o.dtype.itemsize for o in out_shape)
    return pl.pallas_call(
        kernel,
        grid_spec=pltpu.PrefetchScalarGridSpec(
            num_scalar_prefetch=1,
            grid=grid,
            in_specs=in_specs,
            out_specs=out_specs,
            scratch_shapes=list(scratch),
        ),
        out_shape=out_shape,
        input_output_aliases=aliases or {},
        compiler_params=pltpu.CompilerParams(vmem_limit_bytes=vmem << 20),
        cost_estimate=cost(flops, moved),
        name=name,
    )(info, *args)


def shaped(dtype, *shape):
    return jax.ShapeDtypeStruct(shape, dtype)


def once(*block, at=None):
    index = at or (0,) * len(block)
    return pl.BlockSpec(block, lambda *_: index, pipeline_mode=pl.Buffered(1))


def kept(*block):
    index = (0,) * len(block)
    return pl.BlockSpec(block, lambda *_: index)


FRAME_LANES = -(-ROWS // 128) * 128


def row_count(frames):
    return frames * FRAME_LANES


def prepare_kernel(info_ref, tokens_ref, cot_ref, x_ref, g_ref, gt_ref, gsum_ref, hold_ref):
    frames = x_ref.shape[0]
    count = tokens_ref.shape[0]
    inside = lax.broadcasted_iota(jnp.int32, (ROWS, BLOCK), 0) < PATCHES
    hold_ref[...] = jnp.zeros_like(hold_ref)

    def padded(ref):
        hold_ref[0:count] = ref[...].astype(f32)
        return [
            jnp.where(inside, hold_ref[pl.ds(f * PATCHES, ROWS)], 0.0) for f in range(frames)
        ]

    for f, rows in enumerate(padded(tokens_ref)):
        x_ref[f] = rows.astype(bf16)
    grads = padded(cot_ref)
    for f, rows in enumerate(grads):
        g_ref[f] = rows.astype(bf16)
    full = jnp.concatenate([pad_rows(rows, FRAME_LANES) for rows in grads], 0)
    gt_ref[...] = full.T.astype(bf16)
    gsum_ref[...] = jnp.sum(full, 0, keepdims=True)


def prepare(info, tokens, cotangent):
    count = tokens.shape[0]
    frames = count // PATCHES
    deep = row_count(frames)
    taken = pl.BlockSpec((count, BLOCK), lambda r, info_ref: (0, info_ref[r]))
    placed = pl.BlockSpec((frames, ROWS, BLOCK), lambda r, info_ref: (0, 0, r))
    return call(
        prepare_kernel,
        info,
        (tokens, cotangent),
        (BLOCKS,),
        [taken] * 2,
        [
            placed,
            placed,
            pl.BlockSpec((BLOCK, deep), lambda r, info_ref: (r, 0)),
            pl.BlockSpec((1, BLOCK), lambda r, info_ref: (0, r)),
        ],
        [
            shaped(bf16, frames, ROWS, D),
            shaped(bf16, frames, ROWS, D),
            shaped(bf16, D, deep),
            shaped(f32, 1, D),
        ],
        "prepare",
        [pltpu.VMEM((-(-((frames - 1) * PATCHES + ROWS) // 8) * 8, BLOCK), f32)],
    )


def finish_kernel(count, info_ref, *refs):
    in_refs, row_ref, out_ref = refs[:count], refs[count], refs[-1]
    frames = in_refs[0].shape[0]
    for f in range(frames):
        rows = in_refs[0][f]
        for ref in in_refs[1:]:
            rows = rows + ref[f]
        if row_ref.shape[0] == 1:
            rows = rows + row_ref[...]
        else:
            class_row = row_ref[pl.ds(info_ref[2 * BLOCKS] * frames + f, 1)]
            first = lax.broadcasted_iota(jnp.int32, (ROWS, BLOCK), 0) == 0
            rows = rows + jnp.where(first, class_row, 0.0)
        out_ref[pl.ds(f * PATCHES, PATCHES)] = rows[:PATCHES]


def finish(info, parts, row, name, begin=0, count=BLOCKS, earlier=()):
    frames = parts[0].shape[0]
    at = lambda d, info_ref: info_ref[BLOCKS + begin + d]
    taken = pl.BlockSpec((frames, ROWS, BLOCK), lambda d, info_ref: (0, 0, at(d, info_ref)))
    row_spec = pl.BlockSpec((row.shape[0], BLOCK), lambda d, info_ref: (0, at(d, info_ref)))
    return call(
        functools.partial(finish_kernel, len(parts)),
        info,
        (*parts, row, *earlier),
        (count,),
        [taken] * len(parts) + [row_spec] + [pl.BlockSpec(memory_space=pl.ANY)] * len(earlier),
        [pl.BlockSpec((frames * PATCHES, BLOCK), lambda d, info_ref: (0, begin + d))],
        [shaped(f32, frames * PATCHES, D)],
        name,
        aliases={len(parts) + 2: 0} if earlier else {},
    )[0]


def with_message(x_ref, msg_ref, info_ref, f):
    frames = x_ref.shape[0]
    message = msg_ref[pl.ds(info_ref[2 * BLOCKS] * frames + f, 1)]
    place = lax.broadcasted_iota(jnp.int32, (ROWS, D), 0) == PATCHES
    return jnp.where(place, message, x_ref[f].astype(f32))


def put_transposed(ref, rows, f):
    for c in range(BLOCKS):
        block = pad_rows(rows[:, c * BLOCK : (c + 1) * BLOCK].astype(f32), FRAME_LANES)
        place = slice(f * FRAME_LANES, (f + 1) * FRAME_LANES)
        ref[c * BLOCK : (c + 1) * BLOCK, place] = block.T.astype(bf16)


def halves(refs, which, *at):
    sides = []
    for pair in (refs[:2], refs[2:]):
        first, second = (ref[(slice(None), *at)] for ref in pair)
        part, width = first.shape[-2:]
        if which and part == BLOCK:
            blocks = [first[0], second[0], first[1], second[1]]
        else:
            blocks = [v.reshape(-1, width) for v in (first, second)]
        sides.append(jnp.concatenate(blocks, 0))
    return sides


def project_kernel(
    info_ref, x_ref, msg_ref, rel_ref, bias_ref, *refs
):
    a_refs, b_refs, (q_ref, k_ref, v_ref, h_ref) = refs[:4], refs[4:8], refs[8:]
    frames = x_ref.shape[0]

    @pl.when(pl.program_id(0) == 0)
    def _():
        for f in range(frames):
            rows = with_message(x_ref, msg_ref, info_ref, f)
            normed = norm_rows(rows, rel_ref[0:1], rel_ref[1:2])[0].astype(bf16)
            h_ref[pl.ds(f * ROWS, ROWS)] = normed

    for out_ref, weights, bias in (
        (q_ref, halves(a_refs, 0, 0, 0), bias_ref[10:11]),
        (k_ref, halves(a_refs, 0, 0, 1), 0.0),
        (v_ref, halves(b_refs, 1, 0, 0), bias_ref[11:12]),
    ):
        rows = dot(h_ref[...], jnp.concatenate(weights, 0)) + bias
        for f in range(frames):
            out_ref[f] = rows[f * ROWS : (f + 1) * ROWS].astype(bf16)


def project(info, x, message, vec_rel, vectors, attn):
    frames = x.shape[0]
    n, z, _, part, width = attn[0].shape
    columns = vectors.shape[0]
    bias = pl.BlockSpec((columns, width), lambda j, info_ref: (0, j))
    a_spec = pl.BlockSpec((n, 1, 2, part, width), lambda j, info_ref: (0, j, 0, 0, 0))
    b_spec = pl.BlockSpec((n, 1, 1, part, width), lambda j, info_ref: (0, j, 0, 0, 0))
    out = pl.BlockSpec((frames, ROWS, width), lambda j, info_ref: (0, 0, j))
    return call(
        project_kernel,
        info,
        (x, message, vec_rel, vectors, *attn),
        (z,),
        [once(frames, ROWS, D), once(FRAMES, D), once(columns, D), bias]
        + [a_spec] * 4
        + [b_spec] * 4,
        [out] * 3 + [kept(frames * ROWS, D)],
        [shaped(bf16, frames, ROWS, D)] * 3 + [shaped(bf16, frames * ROWS, D)],
        "project",
        (),
        6 * frames * ROWS * D * D,
    )


def transpose_kernel(info_ref, in_ref, out_ref):
    put_transposed(out_ref, in_ref[...], 0)


def transposed(info, rows):
    frames = rows.shape[0] // ROWS
    return call(
        transpose_kernel,
        info,
        (rows,),
        (frames,),
        [pl.BlockSpec((ROWS, D), lambda f, info_ref: (f, 0))],
        [pl.BlockSpec((D, FRAME_LANES), lambda f, info_ref: (0, f))],
        [shaped(bf16, D, row_count(frames))],
        "transposed",
    )[0]


def combine_kernel(
    info_ref, x_ref, a_ref, bias_ref, gain_ref, shift_ref, *refs
):
    b_refs, (mid_ref, n2_ref, n2t_ref) = refs[:4], refs[4:]
    weight = whole_out(b_refs)
    middle = x_ref[0].astype(f32) + bias_ref[...] + dot(a_ref[0], weight, NT)
    mid_ref[0] = middle
    low = middle.astype(bf16).astype(f32)
    normed = norm_rows(low, gain_ref[...], shift_ref[...])[0].astype(bf16)
    n2_ref[0] = normed
    put_transposed(n2t_ref, normed, 0)


def whole_out(b_refs):
    parts = [jnp.concatenate(halves(b_refs, 1, j, 0), 0) for j in range(b_refs[0].shape[1])]
    return jnp.concatenate(parts, 1)


def combine(info, x, attended, vec_rel, attn):
    frames = x.shape[0]
    n, z, _, part, width = attn[4].shape
    frame = pl.BlockSpec((1, ROWS, D), lambda f, info_ref: (f, 0, 0))
    weight = once(n, z, 1, part, width, at=(0, 0, 1, 0, 0))
    return call(
        combine_kernel,
        info,
        (x, attended, vec_rel[12:13], vec_rel[2:3], vec_rel[3:4], *attn[4:]),
        (frames,),
        [frame] * 2 + [once(1, D)] * 3 + [weight] * 4,
        [frame, frame, pl.BlockSpec((D, FRAME_LANES), lambda f, info_ref: (0, f))],
        [
            shaped(f32, frames, ROWS, D),
            shaped(bf16, frames, ROWS, D),
            shaped(bf16, D, row_count(frames)),
        ],
        "combine",
        (),
        2 * frames * ROWS * D * D,
    )


def between_kernel(
    info_ref, ea_ref, eb_ref, mid_ref, g_ref, a_ref, gain_ref, *refs
):
    b_refs, (dmid_ref, da_ref, keep_ref, send_ref, sums_ref, total_ref, dmt_ref) = refs[:4], refs[4:]
    f = pl.program_id(0)
    n, z, part, width = keep_ref.shape
    grad = ea_ref[0] + eb_ref[0]
    low = mid_ref[0].astype(bf16).astype(f32)
    _, scaled, inverse = norm_rows(low, 1.0, 0.0)
    back = norm_back(grad, scaled, inverse, gain_ref[...])
    dmid = (g_ref[0].astype(f32) + back).astype(bf16)
    dmid_ref[0] = dmid
    sums = jnp.concatenate(
        [
            jnp.sum(grad * scaled, 0, keepdims=True),
            jnp.sum(grad, 0, keepdims=True),
            jnp.sum(dmid.astype(f32), 0, keepdims=True),
        ],
        0,
    )

    @pl.when(f == 0)
    def _():
        sums_ref[...] = jnp.zeros_like(sums_ref)
        total_ref[...] = jnp.zeros_like(total_ref)

    sums_ref[...] += sums
    da_ref[0] = dot(dmid, whole_out(b_refs)).astype(bf16)
    put_transposed(dmt_ref, dmid, 0)
    total_ref[...] += dot(dmt_ref[...], pad_rows(a_ref[0], FRAME_LANES))

    @pl.when(f == pl.num_programs(0) - 1)
    def _():
        for j in range(z):
            lanes = slice(j * width, (j + 1) * width)
            for at, ref in ((0, keep_ref), (D // 2, send_ref)):
                ref[:, j] = total_ref[at : at + D // 2, lanes].astype(bf16).reshape(n, part, width)


def between(info, ea, eb, middle, grads, attended, vec_rel, attn):
    frames = ea.shape[0]
    n, z, _, part, width = attn[4].shape
    frame = pl.BlockSpec((1, ROWS, D), lambda f, info_ref: (f, 0, 0))
    weight = once(n, z, 1, part, width, at=(0, 0, 1, 0, 0))
    return call(
        between_kernel,
        info,
        (ea, eb, middle, grads, attended, vec_rel[2:3], *attn[4:]),
        (frames,),
        [frame] * 5 + [once(1, D)] + [weight] * 4,
        [frame, frame, kept(2 * n, z, part, width), kept(2 * n, z, part, width), kept(3, D)],
        [shaped(bf16, frames, ROWS, D)] * 2
        + [shaped(bf16, 2 * n, z, part, width)] * 2
        + [shaped(f32, 3, D)],
        "between",
        [pltpu.VMEM((D, D), f32), pltpu.VMEM((D, row_count(1)), bf16)],
        4 * frames * ROWS * D * D,
    )


def project_grads_kernel(
    info_ref, ht_ref, dq_ref, dk_ref, dv_ref, ok_ref, os_ref, ak_ref, as_ref, bk_ref, bs_ref, sq_ref, sv_ref
):
    frames = dq_ref.shape[0]
    n, _, _, part, width = bk_ref.shape
    bk_ref[:, 0, 1] = ok_ref[:, 0]
    bs_ref[:, 0, 1] = os_ref[:, 0]
    for w, ref in enumerate((dq_ref, dk_ref, dv_ref)):
        rows = jnp.concatenate([pad_rows(ref[f], FRAME_LANES) for f in range(frames)], 0)
        full = dot(ht_ref[...], rows).astype(bf16)
        for at, a_ref, b_ref in ((0, ak_ref, bk_ref), (D // 2, as_ref, bs_ref)):
            grad = full[at : at + D // 2].reshape(n, part, width)
            if w < 2:
                a_ref[:, 0, w] = grad
            else:
                b_ref[:, 0, 0] = grad
        if w != 1:
            (sq_ref if w == 0 else sv_ref)[...] = jnp.sum(rows.astype(f32), 0, keepdims=True)


def project_grads(info, normed_t, grads, out_grads, attn):
    frames = grads[0].shape[0]
    n, z, _, part, width = attn[0].shape
    n = 2 * n
    block = pl.BlockSpec((frames, ROWS, width), lambda j, info_ref: (0, 0, j))
    spec = pl.BlockSpec((n, 1, 2, part, width), lambda j, info_ref: (0, j, 0, 0, 0))
    o_spec = pl.BlockSpec((n, 1, part, width), lambda j, info_ref: (0, j, 0, 0))
    row = pl.BlockSpec((1, width), lambda j, info_ref: (0, j))
    return call(
        project_grads_kernel,
        info,
        (normed_t, *grads, *out_grads),
        (z,),
        [once(*normed_t.shape)] + [block] * 3 + [o_spec] * 2,
        [spec] * 4 + [row] * 2,
        [shaped(bf16, n, z, 2, part, width)] * 4 + [shaped(f32, 1, D)] * 2,
        "project_grads",
        (),
        6 * frames * ROWS * D * D,
    )


def project_back_kernel(
    info_ref, x_ref, msg_ref, dmid_ref, gain_ref, dq_ref, dk_ref, dv_ref, *refs
):
    a_refs, b_refs, (ing_ref, dmsg_ref, sums_ref, total_ref) = refs[:4], refs[4:8], refs[8:]
    frames = x_ref.shape[0]
    j = pl.program_id(0)

    @pl.when(j == 0)
    def _():
        total_ref[...] = jnp.zeros_like(total_ref)

    parts = [halves(a_refs, 0, 0, 0), halves(a_refs, 0, 0, 1), halves(b_refs, 1, 0, 0)]
    weight = jnp.concatenate([jnp.concatenate(v, 0) for v in parts], 1)
    for f in range(frames):
        rows = jnp.concatenate([dq_ref[f], dk_ref[f], dv_ref[f]], 1)
        total_ref[f] += dot(rows, weight, NT)

    @pl.when(j == pl.num_programs(0) - 1)
    def _():
        gain_sum, shift_sum = jnp.zeros((1, D), f32), jnp.zeros((1, D), f32)
        for f in range(frames):
            rows = with_message(x_ref, msg_ref, info_ref, f)
            _, scaled, inverse = norm_rows(rows, 1.0, 0.0)
            grad = total_ref[f]
            gain_sum += jnp.sum(grad * scaled, 0, keepdims=True)
            shift_sum += jnp.sum(grad, 0, keepdims=True)
            back = norm_back(grad, scaled, inverse, gain_ref[...])
            ing_ref[f] = dmid_ref[f].astype(f32) + back
            dmsg_ref[f] = back[PATCHES : PATCHES + 1]
        sums_ref[...] = jnp.concatenate([gain_sum, shift_sum], 0)


def project_back(info, x, message, dmid, vec_rel, grads, attn):
    frames = x.shape[0]
    n, z, _, part, width = attn[0].shape
    block = pl.BlockSpec((frames, ROWS, width), lambda j, info_ref: (0, 0, j))
    a_spec = pl.BlockSpec((n, 1, 2, part, width), lambda j, info_ref: (0, j, 0, 0, 0))
    b_spec = pl.BlockSpec((n, 1, 1, part, width), lambda j, info_ref: (0, j, 0, 0, 0))
    return call(
        project_back_kernel,
        info,
        (x, message, dmid, vec_rel[0:1], *grads, *attn),
        (z,),
        [once(frames, ROWS, D), once(FRAMES, D), once(frames, ROWS, D), once(1, D)]
        + [block] * 3
        + [a_spec] * 4
        + [b_spec] * 4,
        [once(frames, ROWS, D), kept(frames, 1, D), kept(2, D)],
        [shaped(f32, frames, ROWS, D), shaped(f32, frames, 1, D), shaped(f32, 2, D)],
        "project_back",
        [pltpu.VMEM((frames, ROWS, D), f32)],
        6 * frames * ROWS * D * D,
    )


def message_halves(refs, which, i):
    part = D // (4 * refs[0].shape[0])
    return halves([ref.at[:, i * part : (i + 1) * part] for ref in refs], which)


def message_times(rows, refs, i):
    own, other = rows[:, : D // 2], rows[:, D // 2 :]
    cols = []
    for which in range(2):
        weights = message_halves(refs[4 * which : 4 * which + 4], which, i)
        cols.append(dot(own, weights[0]) + dot(other, weights[1]))
    return jnp.concatenate(cols, 1)


def message_times_t(rows, refs, i):
    left, right = rows[:, : D // 2], rows[:, D // 2 :]
    first, second = message_halves(refs[:4], 0, i), message_halves(refs[4:], 1, i)
    return jnp.concatenate(
        [dot(left, first[s], NT) + dot(right, second[s], NT) for s in range(2)], 1
    )


def by_head(rows):
    full = jnp.concatenate([rows.astype(f32)] * HEADS, 0)
    return jnp.where(head_mask(), full, 0.0).astype(bf16)


def head_mask():
    shape = (HEADS * FRAMES, D)
    head = lax.broadcasted_iota(jnp.int32, shape, 0) // FRAMES
    return head == lax.broadcasted_iota(jnp.int32, shape, 1) // HEAD


def over_heads(rows):
    rows = jnp.where(head_mask(), rows, 0.0)
    return jnp.sum(rows.reshape(HEADS, FRAMES, D), 0)


def message_probability(queries, keys):
    scores = dot(by_head(queries), keys, NT) * HEAD**-0.5
    shifted = jnp.exp(scores - jnp.max(scores, 1, keepdims=True))
    return shifted * (1.0 / jnp.sum(shifted, 1, keepdims=True))


def message_forward_kernel(info_ref, cls_ref, rel_ref, *refs):
    weights, (vec_ref, msg_ref, first_ref, pack_ref, hold_ref) = refs[:8], refs[8:]
    vec_ref[...] = permuted(rel_ref, info_ref, BLOCKS)

    def relative(rows):
        hold_ref[...] = rows
        return permuted(hold_ref, info_ref, 0)

    first = message_times(relative(cls_ref[...]).astype(bf16), weights, 0) + vec_ref[6:7]
    normed = norm_rows(first, vec_ref[4:5], vec_ref[5:6])[0].astype(bf16).astype(f32)
    normed_rel = relative(normed).astype(bf16)
    queries = (message_times(normed_rel, weights, 1) + vec_ref[7:8]).astype(bf16)
    keys = message_times(normed_rel, weights, 2).astype(bf16)
    values = (message_times(normed_rel, weights, 3) + vec_ref[8:9]).astype(bf16)
    probability = message_probability(queries, keys).astype(bf16)
    mixed = over_heads(dot(probability, values)).astype(bf16).astype(f32)
    message = first + message_times(relative(mixed).astype(bf16), weights, 4) + vec_ref[9:10]
    msg_ref[...] = relative(message)
    first_ref[...] = first
    for i, rows in enumerate((normed, mixed, queries, keys, values)):
        pack_ref[i] = rows.astype(f32)


def message_forward(info, class_rows, vec_rel, weights):
    one = kept(FRAMES, D)
    return call(
        message_forward_kernel,
        info,
        (class_rows, vec_rel, *weights),
        (1,),
        [one, kept(*vec_rel.shape)] + [once(*w.shape) for w in weights],
        [kept(*vec_rel.shape), one, one, kept(5, FRAMES, D)],
        [
            shaped(f32, *vec_rel.shape),
            shaped(f32, FRAMES, D),
            shaped(f32, FRAMES, D),
            shaped(f32, 5, FRAMES, D),
        ],
        "message_forward",
        [pltpu.VMEM((FRAMES, D), f32)],
        10 * FRAMES * D * D,
    )


def message_backward_kernel(info_ref, dmsg_ref, table_ref, cls_ref, first_ref, pack_ref, vec_ref, *refs):
    weights, (class_ref, sent_ref, hold_ref, rows_ref) = refs[:8], refs[8:]
    frames = dmsg_ref.shape[1]
    for i in range(dmsg_ref.shape[0]):
        place = lax.bitwise_xor(info_ref[2 * BLOCKS], i)
        for f in range(frames):
            hold_ref[i * frames + f : i * frames + f + 1] = dmsg_ref[place, f : f + 1]
    dmsg = permuted(hold_ref, info_ref, BLOCKS)

    def plain(rows):
        hold_ref[...] = rows
        return permuted(hold_ref, info_ref, BLOCKS)

    queries, keys, values = (pack_ref[i].astype(bf16) for i in (2, 3, 4))
    grad_mixed = plain(message_times_t(dmsg.astype(bf16), weights, 4)).astype(bf16)
    probability = message_probability(queries, keys)
    grads_big = by_head(grad_mixed)
    grad_prob = dot(grads_big, values, NT)
    inner = jnp.sum(grad_prob * probability, 1, keepdims=True)
    grad_scores = (probability * (grad_prob - inner)).astype(bf16)
    dq = (over_heads(dot(grad_scores, keys)) * HEAD**-0.5).astype(bf16)
    dk = (dot(grad_scores, by_head(queries), TN) * HEAD**-0.5).astype(bf16)
    dv = dot(probability.astype(bf16), grads_big, TN).astype(bf16)
    grad = plain(
        message_times_t(dq, weights, 1)
        + message_times_t(dk, weights, 2)
        + message_times_t(dv, weights, 3)
    )
    _, scaled, inverse = norm_rows(first_ref[...], 1.0, 0.0)
    back = norm_back(grad, scaled, inverse, vec_ref[4:5])
    dfirst = (dmsg + back).astype(bf16)
    class_ref[...] = message_times_t(dfirst, weights, 0)
    sent = [rows.astype(f32) for rows in (dfirst, dq, dk, dv, dmsg)]
    hold_ref[...] = jnp.zeros_like(hold_ref)
    hold_ref[0:TABLE_REL] = table_ref[0:TABLE_REL]
    table = permuted(hold_ref, info_ref, BLOCKS)
    rows_ref[...] = jnp.zeros_like(rows_ref)
    for i, rows in enumerate([cls_ref[...], pack_ref[0], pack_ref[1]] + sent):
        rows_ref[i * FRAMES : (i + 1) * FRAMES] = rows
    sums = [grad * scaled, grad, sent[0], sent[1], sent[3], dmsg]
    sums = [jnp.sum(rows, 0, keepdims=True) for rows in sums]
    here = [table[i : i + 1] for i in range(TABLE_REL)]
    given = [table_ref[i : i + 1] for i in range(TABLE_REL, table_ref.shape[0])]
    for i, row in enumerate(here[:4] + sums + given[:2] + here[4:] + given[2:]):
        rows_ref[8 * FRAMES + i : 8 * FRAMES + i + 1] = row
    sent_ref[...] = rows_ref[...].astype(bf16)


TABLE_REL = 6
SENT_ROWS = 96


def message_backward(info, dmsg, table, class_rows, first, pack, vectors, weights):
    one = kept(FRAMES, D)
    return call(
        message_backward_kernel,
        info,
        (dmsg, table, class_rows, first, pack, vectors, *weights),
        (1,),
        [kept(*dmsg.shape), kept(*table.shape), one, one, kept(*pack.shape), kept(*vectors.shape)]
        + [once(*w.shape) for w in weights],
        [one, kept(SENT_ROWS, D)],
        [shaped(f32, FRAMES, D), shaped(bf16, SENT_ROWS, D)],
        "message_backward",
        [pltpu.VMEM((FRAMES, D), f32), pltpu.VMEM((SENT_ROWS, D), f32)],
        10 * FRAMES * D * D,
    )


def relative_order():
    return lax.axis_size("dp") * BLOCK == D


def make_info():
    place = lax.iota(jnp.int32, BLOCKS)
    if relative_order():
        mine = lax.axis_index("dp")
        differs = place ^ mine
        places = mine ^ (2 * (place % 4) + place // 4)
        blocks = (differs % 2) * 4 + differs // 2
    else:
        places = blocks = place
    return jnp.concatenate([places, blocks, lax.axis_index("tensor")[None]]).astype(jnp.int32)


def swap(values, axis, bit):
    pairs = [(i, i ^ bit) for i in range(lax.axis_size(axis))]
    return lax.ppermute(values, axis, pairs)


def bits_of(axis):
    size = lax.axis_size(axis)
    return [1 << i for i in range(size.bit_length() - 1)]


def after(values, *earlier):
    return lax.optimization_barrier((values, earlier))[0]


def join_kernel(*refs):
    count = len(refs) // 3
    for i in range(count):
        out_ref = refs[2 * count + i]
        out_ref[0] = refs[2 * i][...]
        out_ref[1] = refs[2 * i + 1][...]


def join(*pairs):
    flat = [v.reshape(-1, v.shape[-1]) for pair in pairs for v in pair]
    specs = [pl.BlockSpec((v.shape[0] // 2, v.shape[1]), lambda i: (i, 0)) for v in flat]
    out = pl.pallas_call(
        join_kernel,
        grid=(2,),
        in_specs=specs,
        out_specs=[
            pl.BlockSpec((2, v.shape[0] // 2, v.shape[1]), lambda i: (0, i, 0)) for v in flat[::2]
        ],
        out_shape=[shaped(bf16, 2, *v.shape) for v in flat[::2]],
        compiler_params=pltpu.CompilerParams(vmem_limit_bytes=48 << 20),
        cost_estimate=cost(0, sum(2 * v.size for v in flat)),
        name="join",
    )(*flat)
    return [v.reshape((2,) + pair[0].shape) for v, pair in zip(out, pairs)]


class Gather:
    def __init__(self, *values):
        self.own, self.place = list(values), 0
        if relative_order():
            self.arrived = [swap(v, "dp", bit) for v, bit in zip(values, (2, 4))]
            return
        self.pieces = []
        for v in values:
            everything = lax.all_gather(v, "dp", axis=0)
            count = everything.shape[0] // 4
            self.pieces += [everything[i * count : (i + 1) * count] for i in range(4)]
        self.arrived = self.pieces

    def step(self):
        if not relative_order():
            return self.pieces
        self.place += 1
        if self.place == 1:
            self.own = join(*zip(self.own, self.arrived))
            self.arrived = [swap(v, "dp", bit) for v, bit in zip(self.own, (4, 2))]
            return self.own
        self.pieces = [v for pair in zip(self.own, self.arrived) for v in pair]
        self.arrived = [swap(v, "dp", 1) for v in self.pieces]
        return self.pieces

    def result(self):
        if not relative_order():
            return self.pieces
        return [v for i in (0, 2) for v in self.pieces[i : i + 2] + self.arrived[i : i + 2]]


def beside(outputs, *transfers):
    outputs, arrived = lax.optimization_barrier((outputs, [t.arrived for t in transfers]))
    for t, values in zip(transfers, arrived):
        t.arrived = values
    return outputs


def add_low(left_side, right_side):
    return (left_side.astype(f32) + right_side.astype(f32)).astype(bf16)


def add_kernel(axes, *refs):
    ins, outs = refs[: 2 * len(axes)], refs[2 * len(axes) :]
    for i, axis in enumerate(axes):
        for side in range(2):
            at = (side,) if axis == 0 else (slice(None), side)
            outs[2 * i + side][...] = add_low(ins[2 * i][at], ins[2 * i + 1][at])


def add_and_split(pairs, axes):
    lead = pairs[0][0].shape[:-2]
    rows, width = pairs[0][0].shape[-2:]
    steps = 2 if rows % 32 == 0 else 1
    zeros = (0,) * len(lead)
    spec = pl.BlockSpec((*lead, rows // steps, width), lambda i: (*zeros, i, 0))
    out = pl.BlockSpec((*lead[1:], rows // steps, width), lambda i: (*zeros[1:], i, 0))
    return pl.pallas_call(
        functools.partial(add_kernel, axes),
        grid=(steps,),
        in_specs=[spec] * (2 * len(pairs)),
        out_specs=[out] * (2 * len(pairs)),
        out_shape=[shaped(bf16, *lead[1:], rows, width)] * (2 * len(pairs)),
        compiler_params=pltpu.CompilerParams(vmem_limit_bytes=48 << 20),
        cost_estimate=cost(0, sum(4 * a.size for a, _ in pairs)),
        name="add",
    )(*[v for pair in pairs for v in pair])


class Scatter:
    def __init__(self, keep, send):
        self.place, self.shape = 0, keep[0].shape[1:]
        if not relative_order():
            self.held = [
                lax.psum_scatter(jnp.concatenate(v, 0), "dp", scatter_dimension=0, tiled=False)
                for v in zip(keep, send)
            ]
            self.arrived = [jnp.zeros_like(v) for v in self.held]
            return
        width = self.shape[-1]
        self.held = [v.reshape(2, 2, -1, width) for v in keep]
        self.arrived = [swap(v, "dp", 1).reshape(2, 2, -1, width) for v in send]

    def step(self):
        if not relative_order():
            return list(self.held)
        axes, bits = ((0, 1), (4, 2)) if self.place == 0 else ((0, 0), (2, 4))
        self.place += 1
        sums = list(add_and_split(list(zip(self.held, self.arrived)), axes))
        self.held, going = sums[::2], sums[1::2]
        self.arrived = [swap(v, "dp", bit) for v, bit in zip(going, bits)]
        return going


def pair_kernel(info_ref, *refs):
    ins, outs = refs[:-2], refs[-2:]
    rows = ins[0].shape[1]
    for side in range(2):
        for i in range(len(ins) // 4):
            total = add_low(ins[4 * i + side][0], ins[4 * i + 2 + side][0])
            outs[side][0, i * rows : (i + 1) * rows] = total


def add_and_pair(info, held, arrived):
    count = len(held)
    rows, width = held[0][0].size // held[0].shape[-1], held[0].shape[-1]
    own = pl.BlockSpec((1, rows, width), lambda h, ref: (2 * h + ref[2 * BLOCKS] % 2, 0, 0))
    other = pl.BlockSpec((1, rows, width), lambda h, ref: (2 * h + 1 - ref[2 * BLOCKS] % 2, 0, 0))
    flat = [v.reshape(4, rows, width) for pair in zip(held, arrived) for v in pair for _ in range(2)]
    out = pl.BlockSpec((1, count * rows, width), lambda h, ref: (h, 0, 0))
    return call(
        pair_kernel,
        info,
        flat,
        (2,),
        [own, other] * (2 * count),
        [out] * 2,
        [shaped(bf16, 2, count * rows, width)] * 2,
        "add_and_pair",
    )


def single_kernel(info_ref, ho_ref, hp_ref, ao_ref, ap_ref, held_ref, going_ref):
    held_ref[...] = add_low(ho_ref[0], ao_ref[0])
    going_ref[...] = add_low(hp_ref[0], ap_ref[0])


def add_and_single(info, held, arrived):
    _, rows, width = held.shape
    own = pl.BlockSpec((1, rows, width), lambda i, ref: (ref[2 * BLOCKS] // 2, 0, 0))
    other = pl.BlockSpec((1, rows, width), lambda i, ref: (1 - ref[2 * BLOCKS] // 2, 0, 0))
    return call(
        single_kernel,
        info,
        (held, held, arrived, arrived),
        (1,),
        [own, other] * 2,
        [kept(rows, width)] * 2,
        [shaped(bf16, rows, width)] * 2,
        "add_and_single",
    )


class ScatterVideos:
    def __init__(self, info, *scatters):
        self.info, self.shape = info, scatters[0].shape
        self.direct = lax.axis_size("tensor") != 4
        held = [v.reshape(self.shape) for s in scatters for v in s.held]
        arrived = [v.reshape(self.shape) for s in scatters for v in s.arrived]
        if self.direct:
            values = jnp.stack([add_low(h, a) for h, a in zip(held, arrived)], 1)
            self.held = lax.psum_scatter(values, "tensor", scatter_dimension=0, tiled=False)
            self.going, self.arrived = self.held, jnp.zeros_like(self.held)
            return
        self.held, self.going = add_and_pair(info, held, arrived)
        self.arrived = swap(self.going, "tensor", 1)

    def step(self):
        self.add()
        return self.send()

    def add(self):
        if not self.direct:
            self.held, self.going = add_and_single(self.info, self.held, self.arrived)
        return self.held, self.going

    def send(self, *earlier):
        if not self.direct:
            self.going = after(self.going, *earlier) if earlier else self.going
            self.arrived = swap(self.going, "tensor", 2)
        return self.going

    def result(self):
        return add_low(self.held, self.arrived).reshape((-1,) + self.shape[1:])


class GatherSmall:
    def __init__(self, values):
        half = values.shape[0] // 2
        self.bits = [(2, 4), (4, 2), (1, 1)]
        if relative_order():
            self.values = [values[None, :half], values[None, half:]]
            self.send()
        else:
            self.values = self.arrived = [lax.all_gather(values, "dp", axis=0)]

    def send(self):
        self.arrived = [swap(v, "dp", bit) for v, bit in zip(self.values, self.bits[0])]

    def step(self):
        if relative_order():
            pairs = zip(self.values, self.arrived)
            self.values = [jnp.concatenate(pair, 0) for pair in pairs]
            self.bits = self.bits[1:]
            if self.bits:
                self.send()
        return self.values

    def result(self):
        if not relative_order():
            return self.values[0]
        first, second = self.values
        order = (0, 2, 1, 3, 4, 6, 5, 7)
        return jnp.concatenate([first, jnp.stack([second[i] for i in order])], 1)


def sum_everywhere(values):
    rounds = [("dp", bits_of("dp")[:1])]
    for axis, bits in (("dp", bits_of("dp")[1:]), ("tensor", bits_of("tensor"))):
        rounds += [(axis, bits[i : i + 2]) for i in range(0, len(bits), 2)]
    for axis, bits in rounds:
        if len(bits) == 1:
            values = values + swap(values, axis, bits[0])
            continue
        first, second, both = (swap(values, axis, b) for b in (*bits, sum(bits)))
        values = (values + first) + (second + both)
    return values


class VideoRows:
    def __init__(self, values, sums):
        self.values, self.sums, self.bits = values[None], sums, bits_of("tensor")
        self.send()

    def send(self):
        rows = jnp.concatenate([self.sums, self.values.reshape(-1, D)], 0)
        self.arrived = swap(rows, "tensor", self.bits[0])

    def step(self):
        count = self.sums.shape[0]
        self.sums = self.sums + self.arrived[:count]
        others = self.arrived[count:].reshape(self.values.shape)
        self.values = jnp.concatenate([self.values, others], 0)
        self.bits = self.bits[1:]
        if self.bits:
            self.send()


def adam_step(weight, first_moment, second_moment, gradient, factor, step_rate, decay_rate):
    clipped = gradient * factor
    first_new = beta_one * first_moment + (1.0 - beta_one) * clipped
    second_new = beta_two * second_moment + (1.0 - beta_two) * clipped * clipped
    update = (
        first_new
        / (1.0 - beta_one**STEP)
        / (jnp.sqrt(second_new / (1.0 - beta_two**STEP)) + adam_eps)
    )
    weight_new = weight - step_rate * (update + decay_rate * weight)
    return (first_new, second_new, weight_new)


def on_device(
    tokens,
    cotangent,
    attn_master,
    attn_first,
    attn_second,
    attn_ema,
    mlp_master,
    mlp_first,
    mlp_second,
    mlp_ema,
    msg_master,
    msg_first,
    msg_second,
    msg_ema,
    vec_master,
    vec_first,
    vec_second,
    vec_ema,
):
    z_index = lax.axis_index("tensor")
    z_count = lax.axis_size("tensor")
    dp_index = lax.axis_index("dp")
    part = attn_master.shape[0]
    local_width = attn_master.shape[2]
    local_ff = mlp_master.shape[2]
    frames = tokens.shape[0] // PATCHES
    half_ff = local_ff // 2
    info = make_info()

    class_own = jnp.concatenate(
        [tokens[f * PATCHES : f * PATCHES + 1] for f in range(frames)], 0
    ).reshape(-1, local_width)
    attn_low = jnp.swapaxes(attn_master, 0, 1).astype(bf16).reshape(4 * part, local_width)
    attn_rows = pad_rows(jnp.concatenate([attn_low, class_own], 0), 4 * part + 16)
    attn_z = lax.all_gather(attn_rows, "tensor", axis=0)
    class_rows = attn_z[:, 4 * part : 4 * part + class_own.shape[0]].reshape(FRAMES, D)
    attn_z = attn_z[:, : 4 * part].reshape(z_count, 4, part, local_width)

    msg_low = jnp.swapaxes(msg_master, 0, 1).astype(bf16).reshape(5 * part, D)
    vec_count = vec_master.shape[1]
    vec_low = jnp.pad(vec_master.astype(bf16).T, ((0, 32 - vec_count), (0, D // 2 - part)))
    msg_half = [jnp.concatenate([msg_low[:, : D // 2], vec_low], 0), msg_low[:, D // 2 :]]
    msg_go = Gather(*msg_half)
    mlp_low = jnp.swapaxes(after(mlp_master, *msg_half), 0, 1).astype(bf16)
    mlp_z = lax.all_gather(mlp_low, "tensor", axis=0)
    prepared = prepare(info, tokens, cotangent)
    x, grads, grads_t, grad_sum = beside(prepared, msg_go)
    sent_msg = msg_go.step()
    attn_z = after(attn_z, *sent_msg)
    attn_go = Gather(attn_z[:, :2], attn_z[:, 2:])
    sent_attn = attn_go.step()
    beside(sent_attn, msg_go)
    sent_msg = msg_go.step()
    mlp_z = after(mlp_z, *sent_msg)
    mlp_half = [
        [mlp_z[:, i, :, j * half_ff : (j + 1) * half_ff] for i in range(2)] for j in range(2)
    ]
    mlp_go = [Gather(*mlp_half[0])]
    msg_w = msg_go.result()
    vec_rel = jnp.concatenate(msg_w[:4], 0)[:, 5 * part : 5 * part + vec_count, :part]
    vec_rel = jnp.moveaxis(vec_rel, 0, 1).reshape(-1, D).astype(f32)

    sent_mlp = mlp_go[0].own + mlp_half[1]
    vectors, message, first_msg, msg_pack = beside(
        message_forward(info, after(class_rows, *sent_mlp).astype(f32), vec_rel, msg_w), attn_go
    )
    ff_bias = vectors[14:].reshape(z_count, 2, half_ff)
    attn_go.step()
    attn_w = attn_go.result()
    projected = project(info, x, message, vec_rel, vectors, attn_w)
    queries, key_rows, value_rows, normed = beside(projected, mlp_go[0])
    sent_mlp = mlp_go[0].step()
    attended, totals = beside(
        attend_forward(after(queries, *sent_mlp), key_rows, value_rows), mlp_go[0]
    )
    sent_mlp = mlp_go[0].step()
    mlp_go.append(Gather(*after(mlp_half[1], attended)))
    middle, n2, n2_t = beside(
        combine(info, x, after(attended, *sent_mlp), vec_rel, attn_w), *mlp_go
    )
    sent_mlp = mlp_go[1].step()
    n2 = after(n2, *sent_mlp)

    def feed(j, n2):
        return feed_forward(n2, n2_t, grads, grads_t, ff_bias[:, j], mlp_go[j].result())

    out_0, dn2_0, *dw_0, db_0 = beside(feed(0, n2), mlp_go[1])
    sent_mlp = mlp_go[1].step()
    normed_t = beside(transposed(info, after(normed, *sent_mlp)), mlp_go[1])
    dw_0 = after(dw_0, normed_t)
    sums_0 = Scatter(dw_0[::2], dw_0[1::2])
    out_1, dn2_1, *dw_1, db_1 = beside(feed(1, after(n2, normed_t)), sums_0)
    sums_1 = Scatter(dw_1[::2], dw_1[1::2])
    going = sums_0.step()
    dmid, grad_attended, *grad_out_w, sums_two = beside(
        between(info, after(dn2_0, *going), dn2_1, middle, grads, attended, vec_rel, attn_w), sums_1
    )
    going = sums_1.step()
    pairs = HEADS // 2
    back = (queries, key_rows, value_rows, totals)
    grad_qkv = beside(
        attend_backward(*back, after(grad_attended, *going), 0, pairs // 2), sums_0
    )
    going = sums_0.step()
    grad_qkv = beside(
        attend_backward(
            *back, after(grad_attended, *going), pairs // 2, pairs - pairs // 2, grad_qkv
        ),
        sums_0,
        sums_1,
    )
    going = sums_1.step()
    dqk_keep, dqk_send, dvo_keep, dvo_send, sum_q, sum_v = beside(
        project_grads(info, after(normed_t, *going), grad_qkv, grad_out_w, attn_w), sums_1
    )
    sums_attn = Scatter([dqk_keep, dvo_keep], [dqk_send, dvo_send])
    mlp_go = ScatterVideos(info, sums_0, sums_1)
    block_output = beside(
        finish(info, [after(middle, mlp_go.going), out_0, out_1], vec_rel[13:14], "block_output"),
        sums_attn,
    )
    going = sums_attn.step()
    ing, dmsg, sums_one = beside(
        project_back(info, after(x, *going), message, dmid, vec_rel, grad_qkv, attn_w),
        sums_attn,
        mlp_go,
    )
    going = sums_attn.step()

    ff_bias_grad = jnp.stack(
        [db.reshape(z_count, half_ff) for db in (db_0, db_1)], 1
    ).reshape(FF // D, D)
    table = jnp.concatenate([sums_one, sums_two, grad_sum, sum_q, sum_v, ff_bias_grad], 0)
    dmsg = dmsg[:, 0].astype(bf16).astype(f32)
    rows = VideoRows(after(dmsg, *going), table)
    mlp_go.held, mlp_go.going = beside(mlp_go.add(), rows)
    rows.step()
    rows.arrived = after(rows.arrived, mlp_go.going)
    rows.step()
    sent_mlp = mlp_go.send(rows.values)
    dmsg = beside(after(rows.values, sent_mlp), sums_attn)
    attn_go = ScatterVideos(info, sums_attn)
    grad_class, sent = beside(
        message_backward(
            info,
            after(dmsg, attn_go.going),
            rows.sums,
            class_rows.astype(f32),
            first_msg,
            msg_pack,
            vectors,
            msg_w,
        ),
        attn_go,
    )
    going = attn_go.step()

    small = GatherSmall(after(sent, going))
    input_grad = beside(
        finish(info, [after(ing, *small.values)], grad_class, "input_grad"), small, attn_go, mlp_go
    )
    mlp_sum = mlp_go.result()
    small.step()
    attn_grad = attn_go.result()
    mlp_grad = jnp.concatenate([mlp_sum[:2], mlp_sum[2:]], 2)
    mlp_grad = jnp.swapaxes(mlp_grad, 0, 1).astype(f32)
    attn_grad = jnp.swapaxes(attn_grad.reshape(4, part, local_width), 0, 1).astype(f32)
    squares = jnp.sum(attn_grad * attn_grad) + jnp.sum(mlp_grad * mlp_grad)
    squares = beside(squares, small)
    small.step()
    small.step()
    everyone = small.result()
    tables = everyone[:, 8 * FRAMES : 8 * FRAMES + vec_count]
    tables = lax.dynamic_slice_in_dim(tables, dp_index * part, part, 2)
    vec_grad = jnp.sum(tables.astype(f32), 0).T
    everyone = everyone[:, : 8 * FRAMES].reshape(-1, 8, FRAMES, D)
    everyone = jnp.moveaxis(everyone, 0, 1).reshape(8, -1, D)
    mine = lax.dynamic_slice_in_dim(everyone[:3], dp_index * part, part, 2)
    msg_grad = jnp.stack(
        [
            dot(mine[0], everyone[3], TN),
            dot(mine[1], everyone[4], TN),
            dot(mine[1], everyone[5], TN),
            dot(mine[1], everyone[6], TN),
            dot(mine[2], everyone[7], TN),
        ],
        1,
    )

    keep_share = (z_index == 0).astype(f32)
    squares = squares + keep_share * (
        jnp.sum(msg_grad * msg_grad) + jnp.sum(vec_grad * vec_grad)
    )
    squares = sum_everywhere(jnp.broadcast_to(squares, (8, 128)))[0, 0]
    grad_norm = jnp.sqrt(squares)
    factor = clip_limit / jnp.maximum(grad_norm, clip_limit)

    def update(master, first, second, ema, grad, rate, decay):
        first_new, second_new, weight = adam_step(master, first, second, grad, factor, rate, decay)
        return grad, first_new, second_new, weight, ema_keep * ema + (1.0 - ema_keep) * weight

    return (
        block_output,
        input_grad,
        grad_norm,
        *update(attn_master, attn_first, attn_second, attn_ema, attn_grad, rate_mat, decay_mat),
        *update(mlp_master, mlp_first, mlp_second, mlp_ema, mlp_grad, rate_mat, decay_mat),
        *update(msg_master, msg_first, msg_second, msg_ema, msg_grad, rate_mat, decay_mat),
        *update(vec_master, vec_first, vec_second, vec_ema, vec_grad, rate_vec, 0.0),
    )


def solution(mesh):
    rows = P(("dp", "tensor"), None)
    split = P("dp", None, "tensor")
    copied = P("dp", None, None)
    table = P("dp", None)
    in_specs = (rows,) * 2 + (split,) * 8 + (copied,) * 4 + (table,) * 4
    out_specs = (rows,) * 2 + (P(),) + (split,) * 10 + (copied,) * 5 + (table,) * 5
    return jax.shard_map(
        on_device, mesh=mesh, in_specs=in_specs, out_specs=out_specs, check_vma=False
    )
```
